32 devices in a mesh: dp: 8 (over z, y), fsdp: 4 (over x, core).
Axes of the slice: x: 2, y: 2, z: 4, core: 2. Of those that a mesh axis runs over, the one named last changes fastest.
Arguments:
- tokens: bfloat16 [32768, 512], P(('dp', 'fsdp')), may hold values from -6 to 6
- cotangent: bfloat16 [32768, 512], P(('dp', 'fsdp')), may hold values from -6 to 6
- row_length: int32 [8], P('dp'), may hold values from 1024 to 4096, as said below
- first_gain: bfloat16 [512], P(('dp', 'fsdp')), may hold values from 0.099609375 to 1.8984375
- first_shift: bfloat16 [512], P(('dp', 'fsdp')), may hold values from -1.75 to 1.75
- query_weight: bfloat16 [512, 512], P(('dp', 'fsdp')), may hold values from -0.375 to 0.375
- key_weight: bfloat16 [512, 512], P(('dp', 'fsdp')), may hold values from -0.375 to 0.375
- value_weight: bfloat16 [512, 512], P(('dp', 'fsdp')), may hold values from -0.25 to 0.25
- mixer_weight: bfloat16 [512, 512], P(('dp', 'fsdp')), may hold values from -6 to 6
- mixer_bias: bfloat16 [512], P(('dp', 'fsdp')), may hold values from -1.75 to 1.75
- second_gain: bfloat16 [512], P(('dp', 'fsdp')), may hold values from 0.099609375 to 1.8984375
- second_shift: bfloat16 [512], P(('dp', 'fsdp')), may hold values from -1.75 to 1.75
- inner_weight: bfloat16 [512, 2048], P(('dp', 'fsdp')), may hold values from -0.25 to 0.25
- inner_bias: bfloat16 [2048], P(('dp', 'fsdp')), may hold values from -3 to 3
- outer_weight: bfloat16 [2048, 512], P(('dp', 'fsdp')), may hold values from -0.125 to 0.125
- outer_bias: bfloat16 [512], P(('dp', 'fsdp')), may hold values from -1.75 to 1.75
Outputs:
- output: bfloat16 [32768, 512], P(('dp', 'fsdp'))
- grad_tokens: bfloat16 [32768, 512], P(('dp', 'fsdp'))
- grad_first_gain: float32 [512], P(('dp', 'fsdp'))
- grad_first_shift: float32 [512], P(('dp', 'fsdp'))
- grad_query_weight: float32 [512, 512], P(('dp', 'fsdp'))
- grad_key_weight: float32 [512, 512], P(('dp', 'fsdp'))
- grad_value_weight: float32 [512, 512], P(('dp', 'fsdp'))
- grad_mixer_weight: float32 [512, 512], P(('dp', 'fsdp'))
- grad_mixer_bias: float32 [512], P(('dp', 'fsdp'))
- grad_second_gain: float32 [512], P(('dp', 'fsdp'))
- grad_second_shift: float32 [512], P(('dp', 'fsdp'))
- grad_inner_weight: float32 [512, 2048], P(('dp', 'fsdp'))
- grad_inner_bias: float32 [2048], P(('dp', 'fsdp'))
- grad_outer_weight: float32 [2048, 512], P(('dp', 'fsdp'))
- grad_outer_bias: float32 [512], P(('dp', 'fsdp'))
The draws below stay inside these ranges and needn't reach their ends.
Inputs may be any that keep to these rules, and one draw needn't show every extreme that they name: `row_length`: each entry is 1024 or 4096; both values occur.
All inputs are finite; a program needn't handle non-finite values.
Results may differ from the reference program's by a relative error of at most 0.018.
Values may be sent and summed in bfloat16 or wider, within the bound.
A program may use at most 192 MiB of HBM per device.

```python
import jax
import jax.numpy as jnp
from jax import lax

D = 512
HEADS = 8
HEAD = 64
FF = 2048
BLOCK = 16
SHORT = 1024
LONG = 4096
SEQS = 1
TOK_DEV = 1024
TOKENS = 32768
N_DP = 8
N_FSDP = 4


def draw_row_length(key, part):
    key = jax.random.fold_in(key, 7)
    picked = jax.random.randint(key, (N_DP,), 0, 2)
    order = jax.random.permutation(jax.random.fold_in(key, 1), N_DP)
    picked = picked.at[order[0]].set(1).at[order[1]].set(0)
    return jnp.where(picked == 1, LONG, SHORT).astype(jnp.int32)


def with_spikes(array, stream_key, source, target, shards_of, factor):
    def block_of(axis_at):
        return (jnp.arange(array.shape[axis_at]) // (array.shape[axis_at] // shards_of)).reshape((-1,) + (1,) * (array.ndim - 1 - axis_at))

    one_side = jax.random.permutation(stream_key, shards_of)[block_of(target)]
    far = (block_of(target) + shards_of // 2) % shards_of
    return jnp.where((block_of(source) == one_side) | (block_of(source) == far), factor * array, array)


def block_scale(own_key, extent, shards, low, largest):
    level, own = 1.0, jax.random.fold_in(own_key, 6)
    for position, parts in shards:
        steps = jnp.exp(jax.random.uniform(jax.random.fold_in(own, position), (parts,), jnp.float32, low / len(shards), largest / len(shards)))
        level = level * jnp.repeat(steps, extent[position] // parts).reshape([-1 if axis == position else 1 for axis in range(len(extent))])
    return level


def noise(own_key, dims, spread, most, cuts=(), kind=jnp.bfloat16):
    loudness = block_scale(own_key, dims, cuts, -0.22, 0.18) if cuts else 1.0
    values = jax.random.normal(own_key, dims, jnp.float32) * spread * loudness
    return jnp.minimum(jnp.maximum(values, -most), most).astype(kind)


def noise_with(stream_key, extent, width, reach, shards, heavy, dtype=jnp.bfloat16):
    array = width * jax.random.normal(stream_key, extent, jnp.float32)
    if shards:
        array = array * block_scale(stream_key, extent, shards, -0.22, 0.18)
    return jnp.clip(with_spikes(array, jax.random.fold_in(stream_key, 3), *heavy), -reach, reach).astype(dtype)


def setup_inputs(seed: int = 0) -> dict:
    seeds = jax.random.split(jax.random.key(seed), 17)
    tokens = noise_with(seeds[0], (TOKENS, D), 1.0, 6.0, ((0, 32),), (0, 1, 32, 2.75))
    cotangent = noise_with(seeds[1], (TOKENS, D), 1.0, 6.0, ((0, 32),), (0, 1, 32, 2.75))
    row_length = draw_row_length(jax.random.fold_in(seeds[16], 71), 0)
    first_gain = jnp.clip(1.0 + 0.18 * jax.random.normal(seeds[3], (D,), jnp.float32), 0.099609375, 1.8984375).astype(jnp.bfloat16)
    first_shift = noise(seeds[4], (D,), 0.3, 1.75, ((0, 32),))
    query_weight = noise(seeds[5], (D, D), (D // 2) ** -0.5, 0.375, ((0, 32),))
    key_weight = noise(seeds[6], (D, D), (D // 2) ** -0.5, 0.375, ((0, 32),))
    value_weight = noise(seeds[7], (D, D), D ** -0.5, 0.25, ((0, 32),))
    mixer_weight = noise(seeds[8], (D, D), 1 ** -0.5, 6.0, ((0, 32),))
    mixer_bias = noise(seeds[9], (D,), 0.3, 1.75, ((0, 32),))
    second_gain = jnp.clip(1.0 + 0.18 * jax.random.normal(seeds[10], (D,), jnp.float32), 0.099609375, 1.8984375).astype(jnp.bfloat16)
    second_shift = noise(seeds[11], (D,), 0.3, 1.75, ((0, 32),))
    inner_weight = noise(seeds[12], (D, FF), D ** -0.5, 0.25, ((0, 32),))
    inner_bias = noise(seeds[13], (FF,), 0.5, 3.0, ((0, 32),))
    outer_weight = noise(seeds[14], (FF, D), FF ** -0.5, 0.125, ((0, 32),))
    outer_bias = noise(seeds[15], (D,), 0.3, 1.75, ((0, 32),))
    return dict(tokens=tokens, cotangent=cotangent, row_length=row_length, first_gain=first_gain, first_shift=first_shift, query_weight=query_weight, key_weight=key_weight, value_weight=value_weight, mixer_weight=mixer_weight, mixer_bias=mixer_bias, second_gain=second_gain, second_shift=second_shift, inner_weight=inner_weight, inner_bias=inner_bias, outer_weight=outer_weight, outer_bias=outer_bias)


norm_eps = 1e-05
highest = lax.Precision.HIGHEST

@jax.custom_vjp
def low(v):
    return lax.optimization_barrier(v.astype(jnp.bfloat16)).astype(jnp.float32)

@jax.custom_vjp
def low_back(v):
    return v

def low_keep(v):
    return (low(v), None)

def low_pass(kept, grad):
    return (grad,)

def back_keep(v):
    return (v, None)

def back_low(kept, grad):
    return (low(grad),)
low.defvjp(low_keep, low_pass)
low_back.defvjp(back_keep, back_low)

def matmul(left_side, right_side):
    return jnp.dot(left_side, right_side, precision=highest, preferred_element_type=jnp.float32)

def exact_gelu(values):
    return jax.nn.gelu(values, approximate=False)

def layer_norm(values, gain, shift):
    center = values - lax.optimization_barrier(jnp.mean(values, axis=-1, keepdims=True))
    variance = lax.optimization_barrier(jnp.mean(center * center, axis=-1, keepdims=True))
    return center * lax.rsqrt(variance + norm_eps) * gain + shift

def level_terms(query_rows, key_rows, value_rows, degree):
    pieces, length = (query_rows.shape[0], query_rows.shape[1])
    stride = 2 ** degree
    amount = length // stride
    if degree == 0:
        coarse_query, coarse_key, coarse_value = (query_rows, key_rows, value_rows)
    else:
        folded = (pieces, amount, stride, HEADS, HEAD)
        coarse_query = low(lax.optimization_barrier(jnp.mean(query_rows.reshape(folded), axis=2)))
        coarse_key = low(lax.optimization_barrier(jnp.mean(key_rows.reshape(folded), axis=2)))
        coarse_value = low(lax.optimization_barrier(jnp.sum(value_rows.reshape(folded), axis=2)))
    blocks = amount // BLOCK
    blocked = (pieces, blocks, BLOCK, HEADS, HEAD)
    paired = (pieces, blocks // 2, 2, BLOCK, HEADS, HEAD)
    partner_keys = coarse_key.reshape(paired)[:, :, ::-1].reshape(blocked)
    partner_values = coarse_value.reshape(paired)[:, :, ::-1].reshape(blocked)
    if degree == 0:
        read_keys = jnp.concatenate([coarse_key.reshape(blocked), partner_keys], axis=2)
        read_values = jnp.concatenate([coarse_value.reshape(blocked), partner_values], axis=2)
    else:
        read_keys, read_values = (partner_keys, partner_values)
    scores = low_back(jnp.einsum('pbqhe,pbkhe->pbhqk', coarse_query.reshape(blocked), read_keys, precision=highest) * HEAD ** (-0.5))
    maxima = lax.optimization_barrier(jnp.max(scores, axis=-1))
    expscore = jnp.exp(scores - maxima[..., None])
    totals = stride * lax.optimization_barrier(jnp.sum(expscore, axis=-1))
    numerator = low_back(jnp.einsum('pbhqk,pbkhe->pbqhe', low(expscore), read_values, precision=highest))
    maxima = jnp.swapaxes(maxima, 2, 3).reshape(pieces, amount, HEADS)
    totals = jnp.swapaxes(totals, 2, 3).reshape(pieces, amount, HEADS)
    numerator = numerator.reshape(pieces, amount, HEADS, HEAD)
    return (jnp.repeat(maxima, stride, axis=1), jnp.repeat(totals, stride, axis=1), jnp.repeat(numerator, stride, axis=1))

def hier_attention(query_rows, key_rows, value_rows):
    length = query_rows.shape[1]
    levels = (length // BLOCK).bit_length() - 1
    triples = [level_terms(query_rows, key_rows, value_rows, degree) for degree in range(levels)]
    overall = lax.optimization_barrier(jnp.max(jnp.stack([triple[0] for triple in triples]), axis=0))
    factors = [jnp.exp(triple[0] - overall) for triple in triples]
    denominator = sum((factor * triple[1] for factor, triple in zip(factors, triples)))
    num_sum = sum((factor[..., None] * triple[2] for factor, triple in zip(factors, triples)))
    return num_sum / denominator[..., None]

def block_forward(sequences, weights):
    gain_one, shift_one, weight_query, weight_key, weight_value, weight_mix, bias_mix, gain_two, shift_two, weight_in, bias_in, weight_out, bias_out = weights
    pieces, length = (sequences.shape[0], sequences.shape[1])
    flat_rows = sequences.reshape(pieces * length, D)
    normal_one = low(layer_norm(flat_rows, gain_one, shift_one))
    head_split = (pieces, length, HEADS, HEAD)
    query_rows = low(low_back(matmul(normal_one, weight_query))).reshape(head_split)
    key_rows = low(low_back(matmul(normal_one, weight_key))).reshape(head_split)
    value_rows = low(low_back(matmul(normal_one, weight_value))).reshape(head_split)
    mixed = hier_attention(query_rows, key_rows, value_rows).reshape(pieces * length, D)
    resid_mid = flat_rows + low_back(matmul(low(low_back(mixed)), weight_mix) + bias_mix)
    normal_two = low(layer_norm(resid_mid, gain_two, shift_two))
    pre_act = low_back(matmul(normal_two, weight_in) + bias_in)
    hidden = low(exact_gelu(pre_act))
    result = resid_mid + low_back(matmul(hidden, weight_out) + bias_out)
    return result.reshape(sequences.shape)

def group_pass(flat_x, flat_cot, is_long, weights):

    def make(length):

        def shaped_forward(flat_rows, params):
            if length == LONG:
                sequences = flat_rows.reshape(N_FSDP, SEQS, SHORT, D).transpose(1, 0, 2, 3).reshape(SEQS, LONG, D)
                outcome = block_forward(sequences, params).reshape(SEQS, N_FSDP, SHORT, D).transpose(1, 0, 2, 3)
            else:
                outcome = block_forward(flat_rows.reshape(N_FSDP * SEQS, SHORT, D), params)
            return outcome.reshape(flat_rows.shape)

        def branch(operands):
            flat_rows, cot_rows, params = operands
            result, pullback = jax.vjp(shaped_forward, flat_rows, params)
            grad_flat, grad_params = pullback(cot_rows)
            return (result, grad_flat, grad_params)
        return branch
    return lax.cond(is_long, make(LONG), make(SHORT), (flat_x, flat_cot, weights))

def reference(tokens, cotangent, row_length, first_gain, first_shift, query_weight, key_weight, value_weight, mixer_weight, mixer_bias, second_gain, second_shift, inner_weight, inner_bias, outer_weight, outer_bias):
    weights = tuple((parameter.astype(jnp.float32) for parameter in (first_gain, first_shift, query_weight, key_weight, value_weight, mixer_weight, mixer_bias, second_gain, second_shift, inner_weight, inner_bias, outer_weight, outer_bias)))
    group_x = tokens.astype(jnp.float32).reshape(N_DP, N_FSDP * TOK_DEV, D)
    group_cot = cotangent.astype(jnp.float32).reshape(N_DP, N_FSDP * TOK_DEV, D)

    def group_step(carried, inputs):
        flat_x, flat_cot, length = inputs
        result, grad_flat, grad_params = group_pass(flat_x, flat_cot, length > SHORT, weights)
        carried = tuple((summed + fresh for summed, fresh in zip(carried, grad_params)))
        return (carried, (result.astype(jnp.bfloat16), grad_flat.astype(jnp.bfloat16)))
    initial = tuple((jnp.zeros(parameter.shape, jnp.float32) for parameter in weights))
    totals_out, (outputs, grads_in) = lax.scan(group_step, initial, (group_x, group_cot, row_length))
    return (outputs.reshape(TOKENS, D), grads_in.reshape(TOKENS, D), totals_out[0], totals_out[1], totals_out[2], totals_out[3], totals_out[4], totals_out[5], totals_out[6], totals_out[7], totals_out[8], totals_out[9], totals_out[10], totals_out[11], totals_out[12])
```

```python
import functools
import math
import types

import jax
import jax.numpy as jnp
import numpy as np
from jax import lax
from jax.experimental import pallas as pl
from jax.experimental.pallas import tpu as pltpu
from jax.sharding import PartitionSpec as P

D = 512
HEADS = 8
HEAD = 64
BLOCK = 16
SHORT = 1024
LEVELS = 8
TILE = 128
CHUNK = 256
STACK = 2 * SHORT
WIDTH = 3 * D
SMALL = 128
FEED_STEPS = 2
AXES = ("dp", "fsdp")
MESH = pl.DeviceIdType.MESH
SLOTS = (4, 2, 2, 2)

norm_eps = 1e-05
far_off = -1e30
f32 = jnp.float32
bf16 = jnp.bfloat16

FIRST = [STACK - (STACK >> level) for level in range(LEVELS + 1)]
LOW_TOP = 4


def member_matrix():
    token = np.arange(SHORT)
    rows = []
    for level, span in ((1, 256), (2, 512), (3, 1024)):
        rows.append((token[None] % span) >> level == np.arange(TILE)[:, None])
    for level in range(LOW_TOP, LEVELS):
        rows.append(token[None] >> level == np.arange(SHORT >> level)[:, None])
    rows.append(np.zeros((8, SHORT), bool))
    return np.concatenate(rows).astype(np.float32)


def block_bias():
    key = np.arange(32)[:, None]
    query = np.arange(2 * TILE)[None]
    across = (key < BLOCK) != (query % 32 < BLOCK)
    last = np.where(query % TILE >= 96, ~across, across)
    kinds = [np.ones_like(across), across, last]
    return np.stack([np.where(kind, 0.0, far_off) for kind in kinds]).astype(np.float32)


def head_mask():
    lane = np.arange(TILE)[None]
    side = np.arange(2 * TILE)[:, None] // TILE
    return (lane // HEAD == side).astype(np.float32)


def group_mask():
    key = np.arange(TILE)[:, None]
    query = np.arange(2 * TILE)[None]
    return (key // 32 == query % TILE // 32).astype(np.float32)


def top_level_of():
    index = np.arange(TILE)
    return np.minimum(LOW_TOP + (index >= 64) * 1 + (index >= 96) * 1 + (index >= 112) * 1, 7)


def nn(a, b):
    return lax.dot_general(a, b, (((1,), (0,)), ((), ())), preferred_element_type=f32)


def nt(a, b):
    return lax.dot_general(a, b, (((1,), (1,)), ((), ())), preferred_element_type=f32)


def tn(a, b):
    return lax.dot_general(a, b, (((0,), (0,)), ((), ())), preferred_element_type=f32)


def normalize(values):
    center = values - jnp.mean(values, axis=-1, keepdims=True)
    inverse = lax.rsqrt(jnp.mean(center * center, axis=-1, keepdims=True) + norm_eps)
    return center * inverse, inverse


def normalize_back(grad_normed, normed, inverse):
    return inverse * (
        grad_normed
        - jnp.mean(grad_normed, axis=-1, keepdims=True)
        - normed * jnp.mean(grad_normed * normed, axis=-1, keepdims=True)
    )


def gelu_both(v):
    mag = jnp.abs(v) * (0.5**0.5)
    t = 1.0 / (1.0 + 0.3275911 * mag)
    gauss = jnp.exp(-0.5 * v * v)
    poly = t * (
        0.254829592
        + t * (-0.284496736 + t * (1.421413741 + t * (-1.453152027 + t * 1.061405429)))
    )
    tail = 0.5 * poly * gauss
    cdf = jnp.where(v < 0, tail, 1.0 - tail)
    return v * cdf, cdf + v * gauss * ((2 * math.pi) ** -0.5)


def split3(values):
    one = values.astype(bf16)
    rest = values - one.astype(f32)
    two = rest.astype(bf16)
    return one, two, (rest - two.astype(f32)).astype(bf16)


def split2(values):
    one = values.astype(bf16)
    return one, (values - one.astype(f32)).astype(bf16)


class Place:
    def __init__(self):
        self.dp = lax.axis_index("dp")
        self.fs = lax.axis_index("fsdp")
        self.z, self.y = self.dp // 2, self.dp % 2
        self.x, self.c = self.fs // 2, self.fs % 2
        self.oy, self.ox, self.oc = 1 - self.y, 1 - self.x, 1 - self.c
        self.zs = [lax.rem(self.z + step, 4) for step in (1, 2, 3)]
        self.by_core = (self.dp, self.x * 2 + self.oc)
        self.by_x = (self.dp, self.ox * 2 + self.c)
        self.by_y = (self.z * 2 + self.oy, self.fs)
        self.by_z = [(z * 2 + self.y, self.fs) for z in self.zs]


def remote(src, dst, send, recv, device):
    return pltpu.make_async_remote_copy(
        src_ref=src, dst_ref=dst, send_sem=send, recv_sem=recv, device_id=device, device_id_type=MESH
    )


class Gather:
    def __init__(self, ref, p, send, recv, half):
        g = ref
        a, b = pl.ds(0, half), pl.ds(half, g.shape[-1] - half)
        count = iter(range(12))

        def copy(at, device):
            slot = next(count)
            return remote(at, at, send.at[slot], recv.at[slot], device)

        mine = g.at[p.z, p.y, p.x, p.c]
        self.zs = [copy(mine, device) for device in p.by_z]
        self.one = [copy(g.at[:, p.y, p.x, p.c, :, a], p.by_x), copy(g.at[:, p.y, p.x, p.c, :, b], p.by_y)]
        self.core_one = [copy(g.at[:, p.y, p.x, p.c], p.by_core)]
        self.two = [copy(g.at[:, p.y, :, p.c, :, a], p.by_y), copy(g.at[:, :, p.x, p.c, :, b], p.by_x)]
        self.core_two = [
            copy(g.at[:, p.y, p.ox, p.c, :, a], p.by_core),
            copy(g.at[:, p.oy, p.x, p.c, :, b], p.by_core),
        ]
        self.core_three = [
            copy(g.at[:, p.oy, :, p.c, :, a], p.by_core),
            copy(g.at[:, :, p.ox, p.c, :, b], p.by_core),
        ]
        self.every = self.zs + self.one + self.core_one + self.two + self.core_two + self.core_three

    def begin(self):
        for copy in self.zs:
            copy.start()

    def second(self):
        for copy in self.zs:
            copy.wait_recv()
        for copy in self.one + self.core_one:
            copy.start()

    def third(self):
        for copy in self.one:
            copy.wait_recv()
        for copy in self.two + self.core_two:
            copy.start()

    def fourth(self):
        for copy in self.two:
            copy.wait_recv()
        for copy in self.core_three:
            copy.start()

    def finish(self):
        for copy in self.core_one + self.core_two + self.core_three:
            copy.wait_recv()
        for copy in self.every:
            copy.wait_send()


class Scatter:
    def __init__(self, ref, p, send, recv, half, cores, from_core, one_a, one_b, two_a, two_b, far):
        s = ref
        self.s, self.p = ref, p
        self.a, self.b = a, b = pl.ds(0, half), pl.ds(half, s.shape[-1] - half)
        self.from_core, self.one_a, self.one_b = from_core, one_a, one_b
        self.two_a, self.two_b, self.far = two_a, two_b, far
        count = iter(range(7))

        def copy(at, dst, device):
            slot = next(count)
            return remote(at, dst, send.at[slot], recv.at[slot], device)

        self.cores = cores
        self.one = [
            copy(s.at[:, p.oy, :, p.c, :, a], one_a, p.by_y),
            copy(s.at[:, :, p.ox, p.c, :, b], one_b, p.by_x),
        ]
        self.two = [
            copy(s.at[:, p.y, p.ox, p.c, :, a], two_a, p.by_x),
            copy(s.at[:, p.oy, p.x, p.c, :, b], two_b, p.by_y),
        ]
        self.zs = [
            copy(s.at[z, p.y, p.x, p.c], far.at[step], device)
            for step, (z, device) in enumerate(zip(p.zs, p.by_z))
        ]

    def second(self):
        p, s = self.p, self.s
        for copy in self.cores:
            copy.wait_recv()

        def add(z, carry):
            s[z, :, :, p.c] = (s[z, :, :, p.c].astype(f32) + self.from_core[z].astype(f32)).astype(bf16)
            return carry

        lax.fori_loop(0, 4, add, 0)
        for copy in self.one:
            copy.start()

    def third(self):
        p, s, a, b = self.p, self.s, self.a, self.b
        for copy in self.one:
            copy.wait_recv()

        def add(z, carry):
            s[z, p.y, :, p.c, :, a] = (s[z, p.y, :, p.c, :, a].astype(f32) + self.one_a[z].astype(f32)).astype(bf16)
            s[z, :, p.x, p.c, :, b] = (s[z, :, p.x, p.c, :, b].astype(f32) + self.one_b[z].astype(f32)).astype(bf16)
            return carry

        lax.fori_loop(0, 4, add, 0)
        for copy in self.two:
            copy.start()

    def fourth(self):
        p, s, a, b = self.p, self.s, self.a, self.b
        for copy in self.two:
            copy.wait_recv()

        def add(z, carry):
            s[z, p.y, p.x, p.c, :, a] = (s[z, p.y, p.x, p.c, :, a].astype(f32) + self.two_a[z].astype(f32)).astype(bf16)
            s[z, p.y, p.x, p.c, :, b] = (s[z, p.y, p.x, p.c, :, b].astype(f32) + self.two_b[z].astype(f32)).astype(bf16)
            return carry

        lax.fori_loop(0, 4, add, 0)
        for copy in self.zs:
            copy.start()

    def finish(self, out):
        p = self.p
        total = self.s[p.z, p.y, p.x, p.c].astype(f32)
        for step, copy in enumerate(self.zs):
            copy.wait_recv()
            total = total + self.far[step].astype(f32)
        out[...] = total
        for copy in self.cores + self.one + self.two + self.zs:
            copy.wait_send()


def layer_kernel(fast, kinds, *refs):
    shapes = dict(kinds, **scratch_list(fast))
    r, left = types.SimpleNamespace(), list(refs)
    for name, kind in shapes.items():
        amount = len(kind) if isinstance(kind, list) else 1
        taken, left = left[:amount], left[amount:]
        setattr(r, name, taken if isinstance(kind, list) else taken[0])
    assert not left
    p = Place()
    tok, cot = r.tok, r.cot
    member, spread = r.member, r.spread
    stack, probs, out_t, mix_t = r.stack, r.probs, r.out_t, r.mix_t
    lse_s, share, inner_s, total_h = r.lse_s, r.share, r.inner_s, r.total_h
    resid, n_one, n_two = r.resid, r.n_one, r.n_two
    acc_out, acc_two = r.acc_out, r.acc_two
    pair_ff = r.pair_ff
    g_att, g_num = r.g_att, r.g_num
    g_mix, weight = g_num.at[0:SHORT], r.weight
    grad_v = r.grad_v
    vec = r.vec
    wa, wi, wo = r.wa, r.wi, r.wo
    da, di, do = (r.da, r.di, r.do) if fast else (r.o_a, r.o_i, r.o_o)
    grad_k = pair_ff
    grad_qt = out_t

    local = []

    def fetch(src, dst):
        copy = pltpu.make_async_copy(src, dst, r.in_sem.at[len(local)])
        copy.start()
        local.append(copy)

    if fast:
        own = wa.at[p.z, p.y, p.x, p.c]
        for slot, ref in enumerate((r.wq_s, r.wk_s, r.wv_s)):
            fetch(ref, own.at[:, pl.ds(slot * D, D)])
        own = wi.at[p.z, p.y, p.x, p.c]
        fetch(r.wi_s, own.at[:, pl.ds(0, 4 * D)])
        fetch(r.wm_s, own.at[:, pl.ds(4 * D, D)])
        fetch(r.wo_s, wo.at[p.z, p.y, p.x, p.c])
    shards = len(local)
    fetch(r.tok_h, tok)
    fetch(r.member_h, member)
    fetch(r.cot_h, cot)
    fetch(r.spread_h, spread)

    other = p.fs // 2 * 2 + 1 - p.fs % 2
    pair = (1 - p.fs // 2) * 2
    side = p.fs % 2
    barrier = pltpu.get_barrier_semaphore()
    reach = [(p.dp, other), (p.dp, pair), (p.dp, pair + 1)]
    if fast:
        reach += [p.by_y] + p.by_z
    for device in reach:
        pl.semaphore_signal(barrier, inc=1, device_id=device, device_id_type=MESH)
    if fast:
        whose = p.dp * 4 + p.fs
        at = lax.broadcasted_iota(jnp.int32, (HEAD, SMALL), 0)
        lane = lax.broadcasted_iota(jnp.int32, (HEAD, SMALL), 1)
        rows = [ref[...].astype(f32).reshape(1, 16) for ref in r.vectors[:6]]
        rows = jnp.concatenate(rows + [jnp.zeros((10, 16), f32)], axis=0).astype(bf16)
        spot = (lane[0:16] == at[0:16] + 16 * (whose % 8)).astype(f32).astype(bf16)
        own = nn(rows, spot)
        bias = jnp.concatenate([r.vectors[6][...].astype(f32).reshape(1, HEAD), jnp.zeros((15, HEAD), f32)], axis=0)
        spot = (lane == at + HEAD * (whose % 2)).astype(f32).astype(bf16)
        own_bias = nn(bias.astype(bf16), spot)
        own = jnp.concatenate([own[0:6], own_bias[0:1], jnp.zeros((9, SMALL), f32)], axis=0)
        wa[p.z, p.y, p.x, p.c, :, WIDTH : WIDTH + SMALL] = own.astype(bf16)
    for copy in local[:shards]:
        copy.wait()
    pl.semaphore_wait(barrier, len(reach))


    def first_norm(step, carry):
        at = pl.ds(pl.multiple_of(step * CHUNK, CHUNK), CHUNK)
        acc_two[at, :] = normalize(tok[at, :].astype(f32))[0]
        return carry

    if fast:
        gat_a = Gather(wa, p, *r.ga, 768)
        gat_i = Gather(wi, p, *r.gi, 1280)
        gat_o = Gather(wo, p, *r.go, 256)
        gat_a.begin()
    for copy in local[shards:]:
        copy.wait()
    lax.fori_loop(0, SHORT // CHUNK, first_norm, 0)
    if fast:
        gat_a.second()
        gat_i.begin()
        gat_a.third()
        gat_a.fourth()
        gat_i.second()
        gat_o.begin()
        gat_a.finish()

    def rows_of(ref, lo, width):
        return ref[:, :, :, :, :, lo : lo + width].reshape(512, width)

    small = wa[:, :, :, :, :, WIDTH : WIDTH + SMALL].astype(f32)
    by_z = jnp.sum(small, axis=(1, 2, 3))
    param = jnp.concatenate([by_z[z] for z in range(4)], axis=1)
    r.param[...] = param
    by_pair = jnp.sum(small, axis=3)
    r.bias_in[...] = jnp.concatenate(
        [by_pair[z, y, x, 6:7, :] for z in range(4) for y in range(2) for x in range(2)], axis=1
    )
    vec[...] = jnp.zeros_like(vec)
    r.lanes_in[...] = jnp.zeros_like(r.lanes_in)

    gain_one, shift_one = r.param[0:1, :], r.param[1:2, :]

    def scale_shift(step, carry):
        at = pl.ds(pl.multiple_of(step * CHUNK, CHUNK), CHUNK)
        n_one[at, :] = (acc_two[at, :] * gain_one + shift_one).astype(bf16)
        return carry

    lax.fori_loop(0, SHORT // CHUNK, scale_shift, 0)

    def project(third, carry):
        lanes = pl.ds(pl.multiple_of(third * D, D), D)
        made = nn(n_one[...], wa[:, :, :, :, :, lanes].reshape(D, D))
        stack[0:SHORT, lanes] = (made * jnp.where(third == 0, 0.125, 1.0)).astype(bf16)
        return carry

    lax.fori_loop(0, 3, project, 0)
    if fast:
        gat_i.third()

    index = lax.broadcasted_iota(jnp.int32, (TILE, 1), 0)
    steps_down = jnp.where(
        index < 64, 1 / 16, jnp.where(index < 96, 1 / 32, jnp.where(index < 112, 1 / 64, 1 / 128))
    ).astype(f32)

    def chunk_rows(step):
        one = pl.ds(pl.multiple_of(FIRST[1] + step * 128, 128), 128)
        two = pl.ds(pl.multiple_of(FIRST[2] + step * 64, 64), 64)
        return one, two, pl.ds(pl.multiple_of(FIRST[3] + step * 32, 32), 32)

    def chunk_members(chunk):
        near = [member[lo:hi, 0:CHUNK] for lo, hi in ((0, 128), (128, 192), (256, 288))]
        return near + [member[lo:hi, chunk] for lo, hi in ((384, 448), (448, 480), (480, 496), (496, 512))]

    tops_acc = acc_out
    tops_acc[0:384, :] = jnp.zeros((384, D), f32)

    def pool(step, carry):
        chunk = pl.ds(pl.multiple_of(step * CHUNK, CHUNK), CHUNK)
        rows = jnp.concatenate(chunk_members(chunk), axis=0)
        to = chunk_rows(step)
        for third in range(3):
            lanes = pl.ds(third * D, D)
            made = nn(rows, stack[chunk, lanes])
            for level, (lo, hi) in enumerate(((0, 128), (128, 192), (192, 224))):
                scale = 1.0 if third == 2 else 0.5 ** (level + 1)
                stack[to[level], lanes] = (made[lo:hi] * scale).astype(bf16)
            tops_acc[third * TILE : (third + 1) * TILE, :] += made[224:352]
        return carry

    lax.fori_loop(0, SHORT // CHUNK, pool, 0)
    for third in range(3):
        made = tops_acc[third * TILE : (third + 1) * TILE, :]
        stack[FIRST[4] : STACK, third * D : (third + 1) * D] = (
            made if third == 2 else made * steps_down
        ).astype(bf16)

    far_s, far_r = r.far_s, r.far_r
    far_s[0] = stack[2016:2032, D:]
    far_s[1] = stack[2032:2048, D:]
    send, recv = r.far_send, r.far_recv
    far_out = [
        remote(far_s.at[0], far_r.at[0], send.at[0], recv.at[0], (p.dp, other)),
        remote(far_s.at[1], far_r.at[1 + side], send.at[1], recv.at[1 + side], (p.dp, pair)),
        remote(far_s.at[1], far_r.at[1 + side], send.at[2], recv.at[1 + side], (p.dp, pair + 1)),
    ]
    for copy in far_out:
        copy.start()

    lane_group = lax.broadcasted_iota(jnp.int32, (32, 2 * TILE), 1) % TILE // 32

    def squeeze(tall):
        parts = [tall[32 * part : 32 * part + 32, :] for part in range(4)]
        return jnp.where(
            lane_group < 2,
            jnp.where(lane_group == 0, parts[0], parts[1]),
            jnp.where(lane_group == 2, parts[2], parts[3]),
        )

    def widen(low):
        return jnp.concatenate([low, low, low, low], axis=0) * r.group_m[...]

    def two_heads(low):
        return jnp.concatenate([low, low], axis=0) * r.head_m[...]

    def tile_forward(tile, kind, scale_t):
        rows = pl.ds(pl.multiple_of(tile * TILE, TILE), TILE)
        bias = r.bias[kind]
        tops = []
        for pair_at in range(HEADS // 2):
            lo = pair_at * TILE
            query = two_heads(stack[rows, lo : lo + TILE])
            score = squeeze(nt(stack[rows, D + lo : D + lo + TILE], query)) + bias
            peak = jnp.max(score, axis=0, keepdims=True)
            prob = jnp.exp(score - peak)
            total = jnp.sum(prob, axis=0, keepdims=True)
            low = (prob * (1.0 / total)).astype(bf16)
            probs[tile, :, pair_at * 2 * TILE : (pair_at + 1) * 2 * TILE] = low
            log_total = peak + jnp.log(total)
            tops += [log_total[:, :TILE], log_total[:, TILE:]]
            wide = widen(low)
            made = nn(stack[rows, 2 * D + lo : 2 * D + lo + TILE].T, wide)
            out_t[lo : lo + HEAD, rows] = (made[:HEAD, :TILE] * scale_t).astype(bf16)
            out_t[lo + HEAD : lo + TILE, rows] = (made[HEAD:, TILE:] * scale_t).astype(bf16)
        lse_s[:, rows] = jnp.concatenate(tops, axis=0)

    top_lane = lax.broadcasted_iota(jnp.int32, (HEADS, TILE), 1)
    top_scale_t = jnp.where(
        top_lane < 64, 1 / 16, jnp.where(top_lane < 96, 1 / 32, jnp.where(top_lane < 112, 1 / 64, 1 / 128))
    ).astype(f32)

    def tile_scale(tile):
        return jnp.where(
            tile < 8, 1.0, jnp.where(tile < 12, 0.5, jnp.where(tile < 14, 0.25, 0.125))
        ).astype(f32)

    def near_tiles(tile, carry):
        if fast:
            pl.when(tile == 3)(gat_i.fourth)
            pl.when(tile == 4)(gat_o.second)
            pl.when(tile == 8)(gat_o.third)
            pl.when(tile == 13)(gat_o.fourth)
        tile_forward(tile, jnp.where(tile < 8, 0, 1), tile_scale(tile))
        return carry

    lax.fori_loop(0, 15, near_tiles, 0)
    for slot in range(3):
        remote(far_s.at[0], far_r.at[slot], send.at[slot], recv.at[slot], (p.dp, other)).wait_recv()
    for copy in far_out:
        copy.wait_send()
    stack[2016:2032, D:] = far_r[0]
    stack[2032:2048, D:] = jnp.concatenate(
        [far_r[1].astype(f32)[:8], far_r[2].astype(f32)[:8]], axis=0
    ).astype(bf16)
    tile_forward(15, 2, top_scale_t[0:1, :])
    idle = jnp.where(r.row_length[0] > SHORT, 0.0, far_off)
    lse_s[:, 1920:2048] = lse_s[:, 1920:2048] + jnp.where(top_lane >= 96, idle, 0.0)

    edges = (0, 64, 96, 112, 128)

    def windows(step):
        one = pl.ds(pl.multiple_of(FIRST[1] + step * TILE, TILE), TILE)
        two = pl.ds(pl.multiple_of(FIRST[2] + step // 2 * TILE, TILE), TILE)
        return one, two, pl.ds(FIRST[3], TILE), pl.ds(FIRST[4], TILE)

    def per_level(step, chunk):
        one = member[0:512, chunk]

        def for_head(head):
            rows = []
            spans = [(0, 128), (128, 256), (256, 384), (384, 448), (448, 480), (480, 496), (496, 512)]
            for level, (lo, hi) in enumerate(spans, 1):
                rows.append(one[lo:hi] * share[level, head : head + 1, chunk].astype(bf16))
            return jnp.concatenate(rows, axis=0)

        return for_head

    def combine(step, carry):
        chunk = pl.ds(pl.multiple_of(step * CHUNK, CHUNK), CHUNK)
        wins = windows(step)
        logs = [lse_s[:, chunk]]
        for slot in range(3):
            parts = jnp.concatenate(split3(lse_s[:, wins[slot]]), axis=0)
            made = nn(parts, member[slot * TILE : (slot + 1) * TILE, chunk])
            logs.append(made[0:8] + made[8:16] + made[16:24] + (slot + 1) * math.log(2.0))
        top = lse_s[:, wins[3]]
        parts = []
        for slot in range(4):
            inside = (top_lane >= edges[slot]) & (top_lane < edges[slot + 1])
            parts += list(split3(jnp.where(inside, top, 0.0)))
        made = nn(jnp.concatenate(parts, axis=0), member[384:512, chunk])
        for slot in range(4):
            b = slot * 24
            logs.append(made[b : b + 8] + made[b + 8 : b + 16] + made[b + 16 : b + 24] + (slot + 4) * math.log(2.0))
        peak = functools.reduce(jnp.maximum, logs)
        den = functools.reduce(jnp.add, [jnp.exp(one - peak) for one in logs])
        lse = peak + jnp.log(den)
        for level in range(LEVELS):
            share[level, :, chunk] = jnp.exp(logs[level] - lse)
        for_head = per_level(step, chunk)
        for head in range(HEADS):
            at = slice(head * HEAD, (head + 1) * HEAD)
            coarse = jnp.concatenate([out_t[at, win] for win in wins], axis=1)
            made = nn(coarse, for_head(head))
            made = made + share[0, head : head + 1, chunk] * out_t[at, chunk].astype(f32)
            mix_t[at, chunk] = made.astype(bf16)
        return carry

    lax.fori_loop(0, SHORT // CHUNK, combine, 0)

    if fast:
        gat_i.finish()
    bias_mix, gain_two = r.param[2:3, :], r.param[3:4, :]
    shift_two, bias_out = r.param[4:5, :], r.param[5:6, :]
    w_mix = rows_of(wi, 4 * D, D)
    resid[...] = tn(mix_t[...], w_mix)

    def second_norm(step, carry):
        at = pl.ds(pl.multiple_of(step * CHUNK, CHUNK), CHUNK)
        mid = tok[at, :].astype(f32) + resid[at, :] + bias_mix
        resid[at, :] = mid
        normed, _ = normalize(mid)
        n_two[at, :] = (normed * gain_two + shift_two).astype(bf16)
        return carry

    lax.fori_loop(0, SHORT // CHUNK, second_norm, 0)
    if fast:
        gat_o.finish()

    hid, g_pre = pair_ff.at[0:SHORT], pair_ff.at[SHORT:STACK]
    acc_out[...] = jnp.zeros_like(acc_out)
    acc_two[...] = jnp.zeros_like(acc_two)

    if fast:
        ways = (r.si[2], r.so[2], r.core_send, r.core_recv)

        def core_i(part):
            lanes = pl.ds(pl.multiple_of(part * 512, 512), 512)
            return remote(
                di.at[:, :, :, p.oc, :, lanes], ways[0].at[:, :, :, :, lanes], ways[2].at[part], ways[3].at[part], p.by_core
            )

        def core_o(part):
            return remote(do.at[part, :, :, p.oc], ways[1].at[part], ways[2].at[part + 5], ways[3].at[part + 5], p.by_core)

    def feed(part, carry):
        lanes = pl.ds(pl.multiple_of(part * 512, 512), 512)
        w_in = wi[:, :, :, :, :, lanes].reshape(512, 512)
        w_out = wo[part].reshape(512, 512)
        b_in = r.bias_in[:, lanes]
        sums = jnp.zeros((1, 512), f32)
        for step in range(FEED_STEPS):
            at = pl.ds(step * (SHORT // FEED_STEPS), SHORT // FEED_STEPS)
            act, slope = gelu_both(nn(n_two[at, :], w_in) + b_in)
            act = act.astype(bf16)
            hid[at, :] = act
            back = (nt(cot[at, :], w_out) * slope).astype(bf16)
            g_pre[at, :] = back
            acc_out[at, :] += nn(act, w_out)
            acc_two[at, :] += nt(back, w_in)
            sums = sums + jnp.sum(back.astype(f32), axis=0, keepdims=True)
        r.lanes_in[0:1, lanes] = sums
        di[:, :, :, :, :, lanes] = tn(n_two[...], g_pre[...]).astype(bf16).reshape(4, 2, 2, 2, 16, 512)
        do[part] = tn(hid[...], cot[...]).astype(bf16).reshape(2, 2, 2, 64, 512)
        if fast:
            core_i(part).start()
            core_o(part).start()
        return carry

    lax.fori_loop(0, 4, feed, 0)

    if fast:
        sc_i = Scatter(
            di, p, *r.si[:2], 1280, [core_i(k) for k in range(5)], *r.si[2:]
        )
        sc_o = Scatter(
            do, p, *r.so[:2], 256, [core_o(k) for k in range(4)], *r.so[2:]
        )
        sc_o.second()

    def middle(step, carry):
        at = pl.ds(pl.multiple_of(step * CHUNK, CHUNK), CHUNK)
        mid = resid[at, :]
        r.out[at, :] = (mid + acc_out[at, :] + bias_out).astype(bf16)
        normed, inverse = normalize(mid)
        g_two = acc_two[at, :]
        c = cot[at, :].astype(f32)
        g_mid = c + normalize_back(g_two * gain_two, normed, inverse)
        resid[at, :] = g_mid
        low = g_mid.astype(bf16)
        g_att[at, :] = low
        vec[2:3, :] += jnp.sum(low.astype(f32), axis=0, keepdims=True)
        vec[3:4, :] += jnp.sum(g_two * normed, axis=0, keepdims=True)
        vec[4:5, :] += jnp.sum(g_two, axis=0, keepdims=True)
        vec[5:6, :] += jnp.sum(c, axis=0, keepdims=True)
        return carry

    lax.fori_loop(0, SHORT // CHUNK, middle, 0)
    g_mix[...] = nt(g_att[...], w_mix).astype(bf16)

    def inner_sums(step, carry):
        at = pl.ds(pl.multiple_of(step * 512, 512), 512)
        turned = nt(w_mix, g_att[at, :]).astype(bf16).astype(f32) * mix_t[:, at].astype(f32)
        inner_s[:, at] = jnp.concatenate(
            [jnp.sum(turned[h * HEAD : (h + 1) * HEAD], axis=0, keepdims=True) for h in range(HEADS)], axis=0
        )
        return carry

    lax.fori_loop(0, SHORT // 512, inner_sums, 0)

    made = nn(mix_t[...], g_att[...])
    di[:, :, :, :, :, 4 * D :] = made.astype(bf16).reshape(4, 2, 2, 2, 16, D)
    if fast:
        core_i(4).start()
        sc_o.third()


    def sums_of(level, source, members):
        both = jnp.concatenate(split2(share[level, :, source] * inner_s[:, source]), axis=0)
        made = nt(both, members)
        return made[0:8] + made[8:16]

    tops_acc[0:TILE, :] = jnp.zeros((TILE, D), f32)

    def lift(step, carry):
        chunk = pl.ds(pl.multiple_of(step * CHUNK, CHUNK), CHUNK)
        to = chunk_rows(step)
        members = chunk_members(chunk)
        for pair_at in range(HEADS // 2):
            lo = pair_at * TILE
            left = [
                jnp.concatenate(
                    [one * share[1 + k, head : head + 1, chunk].astype(bf16) for k, one in enumerate(members)], axis=0
                )
                for head in (2 * pair_at, 2 * pair_at + 1)
            ]
            tokens = g_num[chunk, lo : lo + TILE]
            right = [tokens * r.head_m[0:1, :], tokens * r.head_m[TILE : TILE + 1, :]]
            made = nn(jnp.concatenate(left, axis=1), jnp.concatenate(right, axis=0))
            for level, (low, high) in enumerate(((0, 128), (128, 192), (192, 224))):
                g_num[to[level], lo : lo + TILE] = (made[low:high] * 0.5 ** (level + 1)).astype(bf16)
            tops_acc[0:TILE, lo : lo + TILE] += made[224:352]
        total_h[:, chunk] = share[0, :, chunk] * inner_s[:, chunk]
        total_h[:, to[0]] = sums_of(1, chunk, member[0:128, chunk])
        return carry

    lax.fori_loop(0, SHORT // CHUNK, lift, 0)
    g_num[FIRST[4] : STACK, :] = (tops_acc[0:TILE, :] * steps_down).astype(bf16)

    def lift_two(step, carry):
        source = pl.ds(pl.multiple_of(step * 512, 512), 512)
        rows = pl.ds(pl.multiple_of(FIRST[2] + step * TILE, TILE), TILE)
        total_h[:, rows] = sums_of(2, source, member[128:256, source])
        return carry

    lax.fori_loop(0, 2, lift_two, 0)
    every = pl.ds(0, SHORT)
    total_h[:, FIRST[3] : FIRST[4]] = sums_of(3, every, member[256:384, :])
    tops = [sums_of(4 + slot, every, member[384:512, :]) for slot in range(4)]
    total_h[:, FIRST[4] : STACK] = jnp.where(
        top_lane < 64, tops[0], jnp.where(top_lane < 96, tops[1], jnp.where(top_lane < 112, tops[2], tops[3]))
    )
    if fast:
        sc_i.second()
        sc_o.fourth()
    weight[:, 0:SHORT] = share[0]
    weight[:, SHORT:STACK] = jnp.ones((HEADS, SHORT), f32)

    def tile_backward(tile, scale, scale_t):
        rows = pl.ds(pl.multiple_of(tile * TILE, TILE), TILE)
        for pair_at in range(HEADS // 2):
            lo = pair_at * TILE
            both = lambda ref: jnp.concatenate(
                [ref[2 * pair_at : 2 * pair_at + 1, rows], ref[2 * pair_at + 1 : 2 * pair_at + 2, rows]], axis=1
            )
            low = probs[tile, :, pair_at * 2 * TILE : (pair_at + 1) * 2 * TILE].astype(f32)
            times = both(weight)
            num = two_heads(g_num[rows, lo : lo + TILE])
            got = squeeze(nt(stack[rows, 2 * D + lo : 2 * D + lo + TILE], num))
            wide_s = widen((low * (got * times - both(total_h))).astype(bf16))
            wide_p = widen((low * times).astype(bf16))
            query = two_heads(stack[rows, lo : lo + TILE])
            grad_k[rows, lo : lo + TILE] = (nn(wide_s, query) * scale).astype(bf16)
            grad_v[rows, lo : lo + TILE] = nn(wide_p, num).astype(bf16)
            made = nn(stack[rows, D + lo : D + lo + TILE].T, wide_s)
            grad_qt[lo : lo + HEAD, rows] = (made[:HEAD, :TILE] * scale_t).astype(bf16)
            grad_qt[lo + HEAD : lo + TILE, rows] = (made[HEAD:, TILE:] * scale_t).astype(bf16)

    tile_backward(15, steps_down, top_scale_t[0:1, :] * 0.125)
    back_s, back_r = r.back_s, r.back_r
    top_k, top_v = grad_k[2016:2048, :].astype(f32), grad_v[2016:2048, :].astype(f32)
    tall = jnp.concatenate([top_k, top_v], axis=1)
    nothing = jnp.zeros((8, 2 * D), f32)
    back_s[0] = tall[0:16].astype(bf16)
    back_s[1] = jnp.concatenate([tall[16:24], nothing], axis=0).astype(bf16)
    back_s[2] = jnp.concatenate([tall[24:32], nothing], axis=0).astype(bf16)
    send, recv = r.back_send, r.back_recv
    back_out = [
        remote(back_s.at[0], back_r.at[0], send.at[0], recv.at[0], (p.dp, other)),
        remote(back_s.at[1], back_r.at[1 + side], send.at[1], recv.at[1 + side], (p.dp, pair)),
        remote(back_s.at[2], back_r.at[1 + side], send.at[2], recv.at[1 + side], (p.dp, pair + 1)),
    ]
    for copy in back_out:
        copy.start()

    def near_back(tile, carry):
        if fast:
            pl.when(tile == 2)(sc_i.third)
            pl.when(tile == 8)(sc_i.fourth)
        scale = tile_scale(tile)
        tile_backward(tile, scale, scale * 0.125)
        return carry

    lax.fori_loop(0, 15, near_back, 0)
    for slot in range(3):
        remote(back_s.at[slot], back_r.at[slot], send.at[slot], recv.at[slot], (p.dp, other)).wait_recv()
    for copy in back_out:
        copy.wait_send()
    two = back_r[1].astype(f32) + back_r[2].astype(f32)
    grad_k[2016:2032, :] = back_r[0, :, 0:D]
    grad_v[2016:2032, :] = back_r[0, :, D:]
    grad_k[2032:2048, :] = two[:, 0:D].astype(bf16)
    grad_v[2032:2048, :] = two[:, D:].astype(bf16)

    def level_sums(step, carry):
        chunk = pl.ds(pl.multiple_of(step * CHUNK, CHUNK), CHUNK)
        wins = windows(step)
        turned = nn(jnp.concatenate([grad_qt[:, win] for win in wins], axis=1), member[:, chunk])
        turned = (turned + grad_qt[:, chunk].astype(f32)).astype(bf16)
        stack[chunk, 0:D] = turned.T
        for slot, ref in ((1, grad_k), (2, grad_v)):
            made = nn(spread[chunk, :], jnp.concatenate([ref[win, :] for win in wins], axis=0))
            stack[chunk, slot * D : (slot + 1) * D] = (made + ref[chunk, :].astype(f32)).astype(bf16)
        return carry

    lax.fori_loop(0, SHORT // CHUNK, level_sums, 0)

    def project_grad(part, carry):
        lanes = pl.ds(pl.multiple_of(part * D, D), D)
        made = tn(n_one[...], stack[0:SHORT, lanes])
        da[:, :, :, :, :, lanes] = made.astype(bf16).reshape(4, 2, 2, 2, 16, D)
        return carry

    lax.fori_loop(0, 3, project_grad, 0)
    if fast:
        core_a = remote(da.at[:, :, :, p.oc], r.sa[2], r.core_send.at[9], r.core_recv.at[9], p.by_core)
        core_a.start()
        sc_a = Scatter(da, p, *r.sa[:2], 768, [core_a], *r.sa[2:])
        sc_o.finish(r.o_o)
        sc_i.finish(r.o_i)

    acc_two[...] = nt(stack[0:SHORT, :], wa[:, :, :, :, :, 0:WIDTH].reshape(D, WIDTH))
    if fast:
        sc_a.second()

    def first_back(step, carry):
        if fast:
            pl.when(step == 3)(sc_a.third)
        chunk = pl.ds(pl.multiple_of(step * CHUNK, CHUNK), CHUNK)
        g_one = acc_two[chunk, :]
        normed, inverse = normalize(tok[chunk, :].astype(f32))
        vec[0:1, :] += jnp.sum(g_one * normed, axis=0, keepdims=True)
        vec[1:2, :] += jnp.sum(g_one, axis=0, keepdims=True)
        r.g_tok[chunk, :] = (resid[chunk, :] + normalize_back(g_one * gain_one, normed, inverse)).astype(bf16)
        return carry

    lax.fori_loop(0, SHORT // CHUNK, first_back, 0)
    for part in range(4):
        vec[8 + part : 9 + part, :] = r.lanes_in[0:1, part * 512 : (part + 1) * 512]
    if fast:
        vec_r, vec_n = r.vec_r, r.vec_n
        send, recv = r.v_send, r.v_recv
        hops = [
            remote(src, vec_r.at[k], send.at[k], recv.at[k], device)
            for k, (src, device) in enumerate(((vec, p.by_core), (vec_n.at[0], p.by_y), (vec_n.at[1], p.by_x)))
        ]
        hops += [
            remote(vec_n.at[2], vec_r.at[3 + k], send.at[3 + k], recv.at[3 + k], p.by_z[k]) for k in range(3)
        ]
        hops[0].start()
        hops[0].wait_recv()
        vec_n[0] = vec[...] + vec_r[0]
        hops[1].start()
        sc_a.fourth()
        hops[1].wait_recv()
        vec_n[1] = vec_n[0] + vec_r[1]
        hops[2].start()
        hops[2].wait_recv()
        vec_n[2] = vec_n[1] + vec_r[2]
        for hop in hops[3:]:
            hop.start()
        sc_a.finish(r.o_a)
        for hop in hops[3:]:
            hop.wait_recv()
        for hop in hops:
            hop.wait_send()
        total = vec_n[2] + vec_r[3] + vec_r[4] + vec_r[5]
        short = pltpu.roll(total[0:8], 512 - 16 * whose, axis=1)[:, 0:SMALL]
        long = jnp.concatenate([total[8 + k : 9 + k] for k in range(4)], axis=1)
        long = pltpu.roll(jnp.concatenate([long] * 8, axis=0), 2048 - HEAD * whose, axis=1)[:, 0:SMALL]
        r.o_v[0:8] = short
        r.o_v[8:16] = long
    else:
        r.o_v[...] = vec[...]


def final_kernel(out, g_tok, o_a, o_i, o_o, o_v, *rest):
    outs, (kept, sem) = rest[:-2], rest[-2:]
    halves = [pl.ds(k * 512, 512) for k in range(2)]
    into = [
        pltpu.make_async_copy(ref.at[half], kept.at[slot, half], sem.at[0, slot, k])
        for slot, ref in enumerate((out, g_tok)) for k, half in enumerate(halves)
    ]
    onto = [
        pltpu.make_async_copy(kept.at[slot, half], outs[slot].at[half], sem.at[1, slot, k])
        for slot in range(2) for k, half in enumerate(halves)
    ]
    for copy in into:
        copy.start()
    for slot, at in ((2, 0), (3, 1), (8, 2), (9, 3), (10, 4), (14, 5)):
        outs[slot][...] = o_v[at : at + 1, 0:16].reshape(16)
    outs[12][...] = o_v[8:9, 0:HEAD].reshape(HEAD)
    for k in range(3):
        outs[4 + k][...] = o_a[:, k * D : (k + 1) * D]
    outs[7][...] = o_i[:, 4 * D :]
    outs[11][...] = o_i[:, : 4 * D]
    outs[13][...] = o_o[...]
    for copy, then in zip(into, onto):
        copy.wait()
        then.start()
    for copy in onto:
        copy.wait()


def scratch_list(fast):
    V, S = pltpu.VMEM, pltpu.SemaphoreType.DMA
    made = dict(
        tok=V((SHORT, D), bf16),
        cot=V((SHORT, D), bf16),
        member=V((D, SHORT), bf16),
        spread=V((SHORT, D), bf16),
        in_sem=S((10,)),
        stack=V((STACK, WIDTH), bf16),
        probs=V((16, 32, HEADS * TILE), bf16),
        out_t=V((D, STACK), bf16),
        mix_t=V((D, SHORT), bf16),
        lse_s=V((HEADS, STACK), f32),
        share=V((LEVELS, HEADS, SHORT), f32),
        inner_s=V((HEADS, SHORT), f32),
        total_h=V((HEADS, STACK), f32),
        resid=V((SHORT, D), f32),
        n_one=V((SHORT, D), bf16),
        n_two=V((SHORT, D), bf16),
        acc_out=V((SHORT, D), f32),
        acc_two=V((SHORT, D), f32),
        pair_ff=V((STACK, D), bf16),
        g_att=V((SHORT, D), bf16),
        weight=V((HEADS, STACK), f32),
        g_num=V((STACK, D), bf16),
        grad_v=V((STACK, D), bf16),
        vec=V((16, D), f32),
        param=V((16, D), f32),
        bias_in=V((1, 4 * D), f32),
        lanes_in=V((8, 4 * D), f32),
        far_s=V((2, 16, 2 * D), bf16),
        far_r=V((3, 16, 2 * D), bf16),
        far_send=S((3,)),
        far_recv=S((3,)),
        back_s=V((3, 16, 2 * D), bf16),
        back_r=V((3, 16, 2 * D), bf16),
        back_send=S((3,)),
        back_recv=S((3,)),
    )
    if fast:
        pairs = lambda count: [S((count,)), S((count,))]

        def sums(rows, wide):
            half = wide // 2
            return pairs(7) + [
                V((4, 2, 2, rows, wide), bf16),
                V((4, 2, rows, half), bf16),
                V((4, 2, rows, half), bf16),
                V((4, rows, half), bf16),
                V((4, rows, half), bf16),
                V((3, rows, wide), bf16),
            ]

        made.update(
            wa=V(SLOTS + (16, WIDTH + SMALL), bf16),
            wi=V(SLOTS + (16, 5 * D), bf16),
            wo=V(SLOTS + (64, D), bf16),
            da=V(SLOTS + (16, WIDTH), bf16),
            di=V(SLOTS + (16, 5 * D), bf16),
            do=V(SLOTS + (64, D), bf16),
            ga=pairs(12),
            gi=pairs(12),
            go=pairs(12),
            si=sums(16, 5 * D),
            so=sums(64, D),
            sa=sums(16, WIDTH),
            core_send=S((10,)),
            core_recv=S((10,)),
            vec_r=V((6, 16, D), f32),
            vec_n=V((3, 16, D), f32),
            v_send=S((6,)),
            v_recv=S((6,)),
        )
    return made


def constants():
    member = member_matrix()
    as_low = lambda values: jnp.asarray(values.astype(np.float32), bf16)
    return dict(
        member_h=as_low(member),
        spread_h=as_low(np.ascontiguousarray(member.T)),
        head_m=as_low(head_mask()),
        group_m=as_low(group_mask()),
        bias=jnp.asarray(block_bias()),
    )


def run_layer(fast, hbm, vmem):
    sd = jax.ShapeDtypeStruct
    const = constants()
    hbm = dict(hbm, member_h=const.pop("member_h"), spread_h=const.pop("spread_h"))
    vmem = dict(vmem, **const)
    here, there = pl.BlockSpec(memory_space=pltpu.VMEM), pl.BlockSpec(memory_space=pl.ANY)
    slots = () if fast else SLOTS
    kind = f32 if fast else bf16
    outs = dict(
        out=sd((SHORT, D), bf16),
        g_tok=sd((SHORT, D), bf16),
        o_a=sd(slots + (16, WIDTH), kind),
        o_i=sd(slots + (16, 5 * D), kind),
        o_o=sd(slots + (64, D), kind),
        o_v=sd((16, SMALL if fast else D), f32),
    )
    row_length = hbm.pop("row_length")
    operands = dict(hbm, row_length=row_length, **vmem)
    specs = [there] * len(hbm) + [pl.BlockSpec(memory_space=pltpu.SMEM)]
    for operand in vmem.values():
        specs += [here] * (len(operand) if isinstance(operand, list) else 1)
    flat = lambda parts: [one for part in parts.values() for one in (part if isinstance(part, list) else [part])]
    return pl.pallas_call(
        functools.partial(layer_kernel, fast, dict(operands, **outs)),
        out_shape=list(outs.values()),
        in_specs=specs,
        out_specs=[here] * len(outs),
        scratch_shapes=flat(scratch_list(fast)),
        compiler_params=pltpu.CompilerParams(
            collective_id=0, has_side_effects=True, vmem_limit_bytes=63 * 2**20
        ),
    )(*flat(operands))


def finish_outputs(*parts):
    sd = jax.ShapeDtypeStruct
    vmem, hbm = pl.BlockSpec(memory_space=pltpu.VMEM), pl.BlockSpec(memory_space=pl.ANY)
    own, square = sd((16,), f32), sd((16, D), f32)
    tokens = sd((SHORT, D), bf16)
    outs = [tokens, tokens, own, own, square, square, square, square, own, own, own]
    outs += [sd((16, 4 * D), f32), sd((HEAD,), f32), sd((HEAD, D), f32), own]
    return pl.pallas_call(
        final_kernel,
        out_shape=outs,
        in_specs=[hbm] * 2 + [vmem] * 4,
        out_specs=[hbm] * 2 + [vmem] * 13,
        scratch_shapes=[pltpu.VMEM((2, SHORT, D), bf16), pltpu.SemaphoreType.DMA((2, 2, 2))],
    )(*parts)


def on_device(
    tokens, cotangent, row_length, first_gain, first_shift, query_weight, key_weight, value_weight,
    mixer_weight, mixer_bias, second_gain, second_shift, inner_weight, inner_bias, outer_weight, outer_bias,
):
    n_dp, n_fsdp = lax.axis_size("dp"), lax.axis_size("fsdp")
    fast = (n_dp, n_fsdp) == (8, 4) and query_weight.shape[0] == 16
    vectors = (first_gain, first_shift, mixer_bias, second_gain, second_shift, outer_bias)
    first = dict(tok_h=tokens, cot_h=cotangent, row_length=row_length)
    if fast:
        first.update(
            wq_s=query_weight, wk_s=key_weight, wv_s=value_weight, wm_s=mixer_weight, wi_s=inner_weight, wo_s=outer_weight
        )
        return finish_outputs(*run_layer(True, first, dict(vectors=list(vectors) + [inner_bias])))
    whole = lambda part: lax.all_gather(part, AXES, axis=0, tiled=True)
    wide = whole(jnp.concatenate((query_weight, key_weight, value_weight), axis=1))
    eights = [whole(vector).reshape(4, 8, 16) for vector in vectors]
    small = jnp.zeros((4, 8, 16, SMALL), bf16)
    for row, vector in enumerate(eights):
        for at in range(8):
            small = small.at[:, at, row, 16 * at : 16 * at + 16].set(vector[:, at])
    pairs = whole(inner_bias).reshape(4, 4, 2, 64)
    pairs_at = small.reshape(4, 4, 2, 16, SMALL)
    for at in range(2):
        pairs_at = pairs_at.at[:, :, at, 6, 64 * at : 64 * at + 64].set(pairs[:, :, at])
    wide = jnp.concatenate((wide.reshape(4, 8, 16, WIDTH), pairs_at.reshape(4, 8, 16, SMALL)), axis=-1)
    weights = dict(
        wa=wide.reshape(SLOTS + (16, WIDTH + SMALL)),
        wi=whole(jnp.concatenate((inner_weight, mixer_weight), axis=1)).reshape(SLOTS + (16, 5 * D)),
        wo=whole(outer_weight).reshape(SLOTS + (64, D)),
    )
    out, g_tok, d_a, d_i, d_o, o_v = run_layer(False, first, weights)
    owned = lambda part: lax.psum_scatter(part, AXES, scatter_dimension=0, tiled=True)
    g_a = owned(d_a.astype(f32).reshape(D, WIDTH))
    g_q, g_k, g_v = (g_a[:, k * D : (k + 1) * D] for k in range(3))
    g_i = owned(d_i.astype(f32).reshape(D, 5 * D))
    g_i, g_m = g_i[:, : 4 * D], g_i[:, 4 * D :]
    g_o = owned(d_o.astype(f32).reshape(4 * D, D))
    six = [owned(o_v[k]) for k in range(6)]
    g_bias_in = owned(o_v[8:12].reshape(-1))
    return (
        out, g_tok, six[0], six[1], g_q, g_k, g_v, g_m, six[2], six[3], six[4], g_i, g_bias_in, g_o, six[5],
    )


def solution(mesh):
    rows, flat, both = P(AXES, None), P(AXES), P("dp")
    in_specs = (rows, rows, both, flat, flat, rows, rows, rows, rows, flat, flat, flat, rows, flat, rows, flat)
    out_specs = (rows, rows, flat, flat, rows, rows, rows, rows, flat, flat, flat, rows, flat, rows, flat)
    return jax.shard_map(on_device, mesh=mesh, in_specs=in_specs, out_specs=out_specs, check_vma=False)
```

```python
import functools
import math
import types

import jax
import jax.numpy as jnp
import numpy as np
from jax import lax
from jax.experimental import pallas as pl
from jax.experimental.pallas import tpu as pltpu
from jax.sharding import PartitionSpec as P

D = 512
HEADS = 8
HEAD = 64
BLOCK = 16
SHORT = 1024
LEVELS = 8
TILE = 128
TOGETHER = 5
CHUNK = 256
STACK = 2 * SHORT
WIDTH = 3 * D
SMALL = 128
GROUP = 3 * TILE
PAIRS = HEADS // 2
FEED_STEPS = 2
AXES = ("dp", "fsdp")
MESH = pl.DeviceIdType.MESH
SLOTS = (4, 2, 2, 2)

norm_eps = 1e-05
far_off = -1e30
f32 = jnp.float32
bf16 = jnp.bfloat16

FIRST = [STACK - (STACK >> level) for level in range(LEVELS + 1)]
LOW_TOP = 4


def member_matrix():
    token = np.arange(SHORT)
    rows = []
    for level, span in ((1, 256), (2, 512), (3, 1024)):
        rows.append((token[None] % span) >> level == np.arange(TILE)[:, None])
    for level in range(LOW_TOP, LEVELS):
        rows.append(token[None] >> level == np.arange(SHORT >> level)[:, None])
    rows.append(np.zeros((8, SHORT), bool))
    return np.concatenate(rows).astype(np.float32)


def block_bias():
    key = np.arange(32)[:, None]
    query = np.arange(2 * TILE)[None]
    across = (key < BLOCK) != (query % 32 < BLOCK)
    last = np.where(query % TILE >= 96, ~across, across)
    kinds = [np.ones_like(across), across, last]
    return np.stack([np.where(kind, 0.0, far_off) for kind in kinds]).astype(np.float32)


def head_mask():
    lane = np.arange(TILE)[None]
    side = np.arange(2 * TILE)[:, None] // TILE
    return (lane // HEAD == side).astype(np.float32)


def group_mask():
    key = np.arange(TILE)[:, None]
    query = np.arange(2 * TILE)[None]
    return (key // 32 == query % TILE // 32).astype(np.float32)


def top_level_of():
    index = np.arange(TILE)
    return np.minimum(LOW_TOP + (index >= 64) * 1 + (index >= 96) * 1 + (index >= 112) * 1, 7)


def nn(a, b):
    return lax.dot_general(a, b, (((1,), (0,)), ((), ())), preferred_element_type=f32)


def nt(a, b):
    return lax.dot_general(a, b, (((1,), (1,)), ((), ())), preferred_element_type=f32)


def tn(a, b):
    return lax.dot_general(a, b, (((0,), (0,)), ((), ())), preferred_element_type=f32)


def normalize(values):
    center = values - jnp.mean(values, axis=-1, keepdims=True)
    inverse = lax.rsqrt(jnp.mean(center * center, axis=-1, keepdims=True) + norm_eps)
    return center * inverse, inverse


def normalize_back(grad_normed, normed, inverse):
    return inverse * (
        grad_normed
        - jnp.mean(grad_normed, axis=-1, keepdims=True)
        - normed * jnp.mean(grad_normed * normed, axis=-1, keepdims=True)
    )


def gelu_both(v):
    mag = jnp.abs(v) * (0.5**0.5)
    t = 1.0 / (1.0 + 0.3275911 * mag)
    gauss = jnp.exp(-0.5 * v * v)
    poly = t * (
        0.254829592
        + t * (-0.284496736 + t * (1.421413741 + t * (-1.453152027 + t * 1.061405429)))
    )
    tail = 0.5 * poly * gauss
    cdf = jnp.where(v < 0, tail, 1.0 - tail)
    return v * cdf, cdf + v * gauss * ((2 * math.pi) ** -0.5)


def split3(values):
    one = values.astype(bf16)
    rest = values - one.astype(f32)
    two = rest.astype(bf16)
    return one, two, (rest - two.astype(f32)).astype(bf16)


def split2(values):
    one = values.astype(bf16)
    return one, (values - one.astype(f32)).astype(bf16)


class Place:
    def __init__(self):
        self.dp = lax.axis_index("dp")
        self.fs = lax.axis_index("fsdp")
        self.z, self.y = self.dp // 2, self.dp % 2
        self.x, self.c = self.fs // 2, self.fs % 2
        self.oy, self.ox, self.oc = 1 - self.y, 1 - self.x, 1 - self.c
        self.zs = [lax.rem(self.z + step, 4) for step in (1, 2, 3)]
        self.by_core = (self.dp, self.x * 2 + self.oc)
        self.by_x = (self.dp, self.ox * 2 + self.c)
        self.by_y = (self.z * 2 + self.oy, self.fs)
        self.by_z = [(z * 2 + self.y, self.fs) for z in self.zs]
        ys, xs, cs = (self.y, self.oy), (self.x, self.ox), (self.c, self.oc)
        self.plane = [(self.z * 2 + ys[k // 4], xs[k // 2 % 2] * 2 + cs[k % 2]) for k in range(1, 8)]


def remote(src, dst, send, recv, device):
    return pltpu.make_async_remote_copy(
        src_ref=src, dst_ref=dst, send_sem=send, recv_sem=recv, device_id=device, device_id_type=MESH
    )


def arrived(ref, sem, device):
    remote(ref, ref, sem, sem, device).wait_recv()


def gone(ref, sem, device):
    remote(ref, ref, sem, sem, device).wait_send()


class Gather:
    def __init__(self, ref, lanes, p, sems):
        self.at = lambda z, y, x: ref.at[z, y, x, p.c, :, lanes]
        self.p, self.sems = p, sems

    def advance(self, step):
        p, at, sems = self.p, self.at, self.sems
        low, high, both, full = pl.ds(0, 2), pl.ds(2, 2), pl.ds(0, 2), pl.ds(0, 4)
        if step:
            ref = (at(pl.ds(0, 3), p.y, p.x), at(full, p.y, p.x), at(full, both, p.x), at(full, both, both))[step - 1]
            arrived(ref, sems.at[step - 1], p.by_core)
        if step == 4:
            gone(at(pl.ds(0, 3), p.y, p.x), sems.at[4], p.by_core)
            gone(at(pl.ds(0, 3), both, both), sems.at[5], p.by_core)
            gone(at(full, both, both), sems.at[6], p.by_core)
            return
        if step == 0:
            parts = [(at(p.z, p.y, p.x), device) for device in p.by_z]
        elif step == 1:
            parts = [(at(low, p.y, p.x), p.by_x), (at(high, p.y, p.x), p.by_y)]
        elif step == 2:
            parts = [(at(low, p.y, both), p.by_y), (at(high, both, p.x), p.by_x)]
        else:
            parts = [(at(full, both, both), p.by_core)]
        for part, device in parts:
            remote(part, part, sems.at[(4, 5, 5, 6)[step]], sems.at[step], device).start()


class Total:
    def __init__(self, ref, lanes, part, p, sems, bufs):
        self.ref, self.lanes, self.part, self.p, self.sems, self.bufs = ref, lanes, part, p, sems.at[part], bufs

    def add(self, index, buf):
        at = index + (self.p.c, slice(None), self.lanes)
        self.ref[at] = self.ref[at] + buf

    def advance(self, step):
        p, part, sems = self.p, self.part, self.sems
        from_core, one_a, one_b, two_a, two_b, far = self.bufs
        at = lambda z, y, x, c: self.ref.at[z, y, x, c, :, self.lanes]
        low, high, both, full, every = pl.ds(0, 2), pl.ds(2, 2), pl.ds(0, 2), pl.ds(0, 4), slice(None)
        if step:
            ref = (from_core.at[part], from_core.at[part, both], from_core.at[part, 0])[step - 1]
            arrived(ref, sems.at[step - 1], p.by_core)
        if step == 0:
            sends = [(at(full, both, both, p.oc), from_core, p.by_core)]
        elif step == 1:
            for z in range(4):
                self.add((z, every, every), from_core[part, z])
            sends = [(at(low, p.oy, both, p.c), one_a, p.by_y), (at(high, both, p.ox, p.c), one_b, p.by_x)]
        elif step == 2:
            for z in range(2):
                self.add((z, p.y, every), one_a[part, z])
                self.add((2 + z, every, p.x), one_b[part, z])
            sends = [(at(low, p.y, p.ox, p.c), two_a, p.by_x), (at(high, p.oy, p.x, p.c), two_b, p.by_y)]
        else:
            for z in range(2):
                self.add((z, p.y, p.x), two_a[part, z])
                self.add((2 + z, p.y, p.x), two_b[part, z])
            for k, z in enumerate(p.zs):
                remote(at(z, p.y, p.x, p.c), far.at[part, k], sems.at[6], sems.at[3], p.by_z[k]).start()
            return
        for src, buf, device in sends:
            remote(src, buf.at[part], sems.at[(4, 5, 5)[step]], sems.at[step], device).start()

    def finish(self, out):
        p, sems, far, part = self.p, self.sems, self.bufs[5], self.part
        arrived(far.at[part], sems.at[3], p.by_core)
        total = self.ref[p.z, p.y, p.x, p.c, :, self.lanes].astype(f32)
        out[:, self.lanes] = functools.reduce(jnp.add, [far[part, k].astype(f32) for k in range(3)], total)
        gone(self.bufs[0].at[part], sems.at[4], p.by_core)
        gone(self.bufs[0].at[part, pl.ds(0, 3)], sems.at[5], p.by_core)
        gone(far.at[part], sems.at[6], p.by_core)


class TotalRows:
    def __init__(self, ref, part, p, sems, bufs):
        self.ref, self.part, self.p, self.sems, self.bufs = ref, part, p, sems.at[part], bufs

    def add(self, index, buf):
        at = (self.part,) + index
        self.ref[at] = self.ref[at] + buf

    def advance(self, step):
        p, part, sems = self.p, self.part, self.sems
        from_core, one_a, one_b, two_a, two_b, _ = self.bufs
        both, every, low, high = pl.ds(0, 2), slice(None), pl.ds(0, 32), pl.ds(32, 32)
        at = lambda y, x, c, *rows: self.ref.at[(part, y, x, c) + rows]
        if step:
            ref = (from_core.at[part], from_core.at[part, 0], from_core.at[part, 0, 0])[step - 1]
            arrived(ref, sems.at[step - 1], p.by_core)
        if step == 0:
            sends = [(at(both, both, p.oc), from_core, p.by_core)]
        elif step == 1:
            self.add((every, every, p.c), from_core[part])
            sends = [(at(p.oy, both, p.c, low), one_a, p.by_y), (at(both, p.ox, p.c, high), one_b, p.by_x)]
        elif step == 2:
            self.add((p.y, every, p.c, low), one_a[part])
            self.add((every, p.x, p.c, high), one_b[part])
            sends = [(at(p.y, p.ox, p.c, low), two_a, p.by_x), (at(p.oy, p.x, p.c, high), two_b, p.by_y)]
        else:
            self.add((p.y, p.x, p.c, low), two_a[part])
            self.add((p.y, p.x, p.c, high), two_b[part])
            return
        for src, buf, device in sends:
            remote(src, buf.at[part], sems.at[(3, 4, 4)[step]], sems.at[step], device).start()

    def settle(self):
        gone(self.bufs[0].at[self.part], self.sems.at[3], self.p.by_core)
        gone(self.bufs[5], self.sems.at[4], self.p.by_core)


class TotalVectors:
    def __init__(self, ref, p, sems, got, mid, far):
        self.ref, self.p, self.sems, self.got, self.mid, self.far = ref, p, sems, got, mid, far

    def begin(self):
        for k, device in enumerate(self.p.plane):
            remote(self.ref, self.got.at[k], self.sems.at[1], self.sems.at[0], device).start()

    def second(self):
        arrived(self.got, self.sems.at[0], self.p.by_core)
        self.mid[...] = functools.reduce(jnp.add, [self.got[k] for k in range(7)], self.ref[...])
        for k, device in enumerate(self.p.by_z):
            remote(self.mid, self.far.at[k], self.sems.at[3], self.sems.at[2], device).start()

    def finish(self):
        arrived(self.far, self.sems.at[2], self.p.by_core)
        gone(self.got, self.sems.at[1], self.p.by_core)
        gone(self.far, self.sems.at[3], self.p.by_core)
        return functools.reduce(jnp.add, [self.far[k] for k in range(3)], self.mid[...])


def layer_kernel(fast, kinds, *refs):
    shapes = dict(kinds, **scratch_list(fast))
    r, left = types.SimpleNamespace(), list(refs)
    for name, kind in shapes.items():
        amount = len(kind) if isinstance(kind, list) else 1
        taken, left = left[:amount], left[amount:]
        setattr(r, name, taken if isinstance(kind, list) else taken[0])
    assert not left
    p = Place()
    tok, cot = r.tok, r.cot
    member, spread = r.member, r.spread
    stack, probs, out_t, mix_t = r.stack, r.probs, r.out_t, r.mix_t
    lse_s, share, inner_s, total_h = r.lse_s, r.share, r.inner_s, r.total_h
    resid, n_one, n_two = r.resid, r.n_one, r.n_two
    acc_out, acc_two = r.acc_out, r.acc_two
    g_att, g_num = r.g_att, r.g_num
    g_mix, weight = g_num.at[0:SHORT], r.weight
    grad_kv = r.grad_kv
    vec_a, vec_b = r.vec_a, r.vec_b
    wa, wi, wo = r.wa, r.wi, r.wo
    da, di, do = (r.da, r.di, r.do) if fast else (r.o_a, r.o_i, r.o_o)
    grad_qt = out_t

    def fetch(src, dst, slot):
        copy = pltpu.make_async_copy(src, dst, r.in_sem.at[slot])
        copy.start()
        return copy

    def taken(ref, slot):
        pltpu.make_async_copy(ref, ref, r.in_sem.at[slot]).wait()

    if fast:
        small_in = [fetch(ref, kept, k) for k, (ref, kept) in enumerate(zip(r.vectors, r.vec_in))]
        own_a, own_i, own_o = (ref.at[p.z, p.y, p.x, p.c] for ref in (wa, wi, wo))
        for pair in range(PAIRS):
            for slot, ref in enumerate((r.wq_s, r.wk_s, r.wv_s)):
                there = pl.ds(SMALL + pair * GROUP + slot * TILE, TILE)
                fetch(ref.at[:, pl.ds(pair * TILE, TILE)], own_a.at[:, there], 7)
        fetch(r.wi_s, own_i.at[:, pl.ds(0, 4 * D)], 8)
        fetch(r.wm_s, own_i.at[:, pl.ds(4 * D, D)], 8)
        fetch(r.wo_s, own_o, 9)
    tok_in = fetch(r.tok_h, tok, 10)
    rest_in = [
        fetch(src, dst, 11 + k)
        for k, (src, dst) in enumerate(
            ((r.member_h, member), (r.head_h, r.head_m), (r.group_h, r.group_m), (r.bias_h, r.bias), (r.cot_h, cot), (r.spread_h, spread))
        )
    ]

    other = p.fs // 2 * 2 + 1 - p.fs % 2
    pairs_at = (1 - p.fs // 2) * 2
    side = p.fs % 2
    barrier = pltpu.get_barrier_semaphore()
    reach = [(p.dp, other), (p.dp, pairs_at), (p.dp, pairs_at + 1)]
    if fast:
        reach += p.plane[3:] + p.by_z
    for device in reach:
        pl.semaphore_signal(barrier, inc=1, device_id=device, device_id_type=MESH)
    if fast:
        whose = p.dp * 4 + p.fs
        for copy in small_in:
            copy.wait()
        at = lax.broadcasted_iota(jnp.int32, (HEAD, SMALL), 0)
        lane = lax.broadcasted_iota(jnp.int32, (HEAD, SMALL), 1)
        rows = [ref[...].astype(f32).reshape(1, 16) for ref in r.vec_in[:6]]
        rows = jnp.concatenate(rows + [jnp.zeros((10, 16), f32)], axis=0).astype(bf16)
        spot = (lane[0:16] == at[0:16] + 16 * (whose % 8)).astype(f32).astype(bf16)
        own = nn(rows, spot)
        bias = jnp.concatenate([r.vec_in[6][...].astype(f32).reshape(1, HEAD), jnp.zeros((15, HEAD), f32)], axis=0)
        spot = (lane == at + HEAD * (whose % 2)).astype(f32).astype(bf16)
        own_bias = nn(bias.astype(bf16), spot)
        own = jnp.concatenate([own[0:6], own_bias[0:1], jnp.zeros((9, SMALL), f32)], axis=0)
        own_a[:, 0:SMALL] = own.astype(bf16)
    if fast:
        taken(own_a.at[:, pl.ds(SMALL, WIDTH)], 7)
    pl.semaphore_wait(barrier, len(reach))


    def first_norm(step, carry):
        at = pl.ds(pl.multiple_of(step * CHUNK, CHUNK), CHUNK)
        acc_two[at, :] = normalize(tok[at, :].astype(f32))[0]
        return carry

    if fast:
        spans = [(wa, 0, SMALL + GROUP)] + [(wa, SMALL + k * GROUP, GROUP) for k in range(1, PAIRS)]
        spans += [(wi, 0, 1280), (wi, 1280, 1280), (wo, 0, 256), (wo, 256, 256)]
        gathers = [
            Gather(ref, pl.ds(lo, wide), p, r.g_sem.at[k]) for k, (ref, lo, wide) in enumerate(spans)
        ]

    def pump(*events):
        if fast:
            for k, step in events:
                gathers[k].advance(step)

    pump((0, 0), (1, 0), (2, 0), (3, 0))
    tok_in.wait()
    lax.fori_loop(0, SHORT // CHUNK, first_norm, 0)
    if fast:
        taken(own_i, 8)
        taken(own_o, 9)
    pump((0, 1), (1, 1), (0, 2), (2, 1), (1, 2), (0, 3), (3, 1), (4, 0), (2, 2), (0, 4))
    for copy in rest_in:
        copy.wait()

    def rows_of(ref, lo, width):
        return ref[:, :, :, :, :, lo : lo + width].reshape(512, width)

    small = wa[:, :, :, :, :, 0:SMALL].astype(f32)
    by_z = jnp.sum(small, axis=(1, 2, 3))
    param = jnp.concatenate([by_z[z] for z in range(4)], axis=1)
    r.param[...] = param
    by_pair = jnp.sum(small, axis=3)
    r.bias_in[...] = jnp.concatenate(
        [by_pair[z, y, x, 6:7, :] for z in range(4) for y in range(2) for x in range(2)], axis=1
    )
    vec_a[...] = jnp.zeros_like(vec_a)
    vec_b[...] = jnp.zeros_like(vec_b)
    r.lanes_in[...] = jnp.zeros_like(r.lanes_in)

    gain_one, shift_one = r.param[0:1, :], r.param[1:2, :]

    def scale_shift(step, carry):
        at = pl.ds(pl.multiple_of(step * CHUNK, CHUNK), CHUNK)
        n_one[at, :] = (acc_two[at, :] * gain_one + shift_one).astype(bf16)
        return carry

    lax.fori_loop(0, SHORT // CHUNK, scale_shift, 0)

    index = lax.broadcasted_iota(jnp.int32, (TILE, 1), 0)
    steps_down = jnp.where(
        index < 64, 1 / 16, jnp.where(index < 96, 1 / 32, jnp.where(index < 112, 1 / 64, 1 / 128))
    ).astype(f32)

    def chunk_rows(step):
        one = pl.ds(pl.multiple_of(FIRST[1] + step * 128, 128), 128)
        two = pl.ds(pl.multiple_of(FIRST[2] + step * 64, 64), 64)
        return one, two, pl.ds(pl.multiple_of(FIRST[3] + step * 32, 32), 32)

    def chunk_members(chunk):
        near = [member[lo:hi, 0:CHUNK] for lo, hi in ((0, 128), (128, 192), (256, 288))]
        return near + [member[lo:hi, chunk] for lo, hi in ((384, 448), (448, 480), (480, 496), (496, 512))]

    lane_group = lax.broadcasted_iota(jnp.int32, (32, 2 * TILE), 1) % TILE // 32

    def squeeze(tall):
        parts = [tall[32 * part : 32 * part + 32, :] for part in range(4)]
        return jnp.where(
            lane_group < 2,
            jnp.where(lane_group == 0, parts[0], parts[1]),
            jnp.where(lane_group == 2, parts[2], parts[3]),
        )

    def widen(low):
        return jnp.concatenate([low, low, low, low], axis=0) * r.group_m[...]

    def two_heads(low):
        return jnp.concatenate([low, low], axis=0) * r.head_m[...]

    top_lane = lax.broadcasted_iota(jnp.int32, (HEADS, TILE), 1)
    top_scale_t = jnp.where(
        top_lane < 64, 1 / 16, jnp.where(top_lane < 96, 1 / 32, jnp.where(top_lane < 112, 1 / 64, 1 / 128))
    ).astype(f32)

    def tile_scale(tile):
        return jnp.where(
            tile < 8, 1.0, jnp.where(tile < 12, 0.5, jnp.where(tile < 14, 0.25, 0.125))
        ).astype(f32)

    def lanes_at(start, wide):
        return pl.ds(pl.multiple_of(start, TILE), wide)

    def tile_forward(tile, pair, kind, scale_t):
        rows = lanes_at(tile * TILE, TILE)
        at = lambda slot: (rows, lanes_at(pair * GROUP + slot * TILE, TILE))
        score = squeeze(nt(stack[at(1)], two_heads(stack[at(0)]))) + r.bias[kind]
        peak = jnp.max(score, axis=0, keepdims=True)
        prob = jnp.exp(score - peak)
        total = jnp.sum(prob, axis=0, keepdims=True)
        low = (prob * (1.0 / total)).astype(bf16)
        probs[tile, :, lanes_at(pair * 2 * TILE, 2 * TILE)] = low
        log_total = peak + jnp.log(total)
        lse_s[pair, 0:1, rows] = log_total[:, :TILE]
        lse_s[pair, 1:2, rows] = log_total[:, TILE:]
        made = nn(stack[at(2)].T, widen(low))
        head = pl.multiple_of(pair * TILE, TILE)
        out_t[pl.ds(head, HEAD), rows] = (made[:HEAD, :TILE] * scale_t).astype(bf16)
        out_t[pl.ds(head + HEAD, HEAD), rows] = (made[HEAD:, TILE:] * scale_t).astype(bf16)

    far_s, far_r = r.far_s, r.far_r
    far_out = [
        remote(far_s.at[0], far_r.at[0], r.far_sem.at[1], r.far_sem.at[0], (p.dp, other)),
        remote(far_s.at[1], far_r.at[1 + side], r.far_sem.at[1], r.far_sem.at[0], (p.dp, pairs_at)),
        remote(far_s.at[1], far_r.at[1 + side], r.far_sem.at[1], r.far_sem.at[0], (p.dp, pairs_at + 1)),
    ]
    tops_acc = acc_out

    def pair_forward(pair, carry):
        def pump_here(*plan):
            for number, events in enumerate(plan):
                if events:
                    pl.when(pair == number)(functools.partial(pump, *events))

        pump_here([], [(1, 4), (5, 1)], [(2, 4)], [(3, 4)])
        lanes = lanes_at(pair * GROUP, GROUP)
        made = nn(n_one[...], wa[:, :, :, :, :, lanes_at(SMALL + pair * GROUP, GROUP)].reshape(D, GROUP))
        first = lax.broadcasted_iota(jnp.int32, (1, GROUP), 1)
        stack[0:SHORT, lanes] = (made * jnp.where(first < TILE, 0.125, 1.0)).astype(bf16)
        key_like = first < 2 * TILE
        pump_here([(1, 3), (3, 2), (5, 0)])
        tops_acc[0:TILE, 0:GROUP] = jnp.zeros((TILE, GROUP), f32)

        def pool(step, carry):
            chunk = pl.ds(pl.multiple_of(step * CHUNK, CHUNK), CHUNK)
            made = nn(jnp.concatenate(chunk_members(chunk), axis=0), stack[chunk, lanes])
            to = chunk_rows(step)
            for level, (lo, hi) in enumerate(((0, 128), (128, 192), (192, 224))):
                scale = jnp.where(key_like, 0.5 ** (level + 1), 1.0)
                stack[to[level], lanes] = (made[lo:hi] * scale).astype(bf16)
            tops_acc[0:TILE, 0:GROUP] += made[224:352]
            return carry

        lax.fori_loop(0, SHORT // CHUNK, pool, 0)
        stack[FIRST[4] : STACK, lanes] = (
            tops_acc[0:TILE, 0:GROUP] * jnp.where(key_like, steps_down, 1.0)
        ).astype(bf16)
        theirs = lanes_at(pair * GROUP + TILE, 2 * TILE)
        mine = lanes_at(pair * 2 * TILE, 2 * TILE)
        far_s[0, :, mine] = stack[2016:2032, theirs]
        far_s[1, :, mine] = stack[2032:2048, theirs]

        @pl.when(pair == PAIRS - 1)
        def _():
            for copy in far_out:
                copy.start()

        def near_tiles(group, carry):
            for one in range(TOGETHER):
                tile = group * TOGETHER + one
                tile_forward(tile, pair, jnp.where(tile < 8, 0, 1), tile_scale(tile))
            return carry

        pump_here([(2, 3), (4, 1)], [(4, 3), (6, 1)], [(5, 3), (7, 1)], [(6, 3)])
        lax.fori_loop(0, 15 // TOGETHER, near_tiles, 0)
        pump_here([(3, 3), (4, 2), (6, 0)], [(5, 2), (7, 0)], [(4, 4), (6, 2)], [(7, 2)])
        return carry

    lax.fori_loop(0, PAIRS, pair_forward, 0)
    arrived(far_r, r.far_sem.at[0], p.by_core)
    gone(far_r, r.far_sem.at[1], p.by_core)
    last_rows = jnp.concatenate([far_r[1].astype(f32)[:8], far_r[2].astype(f32)[:8]], axis=0).astype(bf16)
    for pair in range(PAIRS):
        theirs = slice(pair * GROUP + TILE, (pair + 1) * GROUP)
        mine = slice(pair * 2 * TILE, (pair + 1) * 2 * TILE)
        stack[2016:2032, theirs] = far_r[0, :, mine]
        stack[2032:2048, theirs] = last_rows[:, mine]
    for pair in range(PAIRS):
        tile_forward(15, pair, 2, top_scale_t[0:1, :])
    idle = jnp.where(r.row_length[0] > SHORT, 0.0, far_off)
    lse_s[:, :, 1920:2048] = lse_s[:, :, 1920:2048] + jnp.where(top_lane[0:2] >= 96, idle, 0.0)

    edges = (0, 64, 96, 112, 128)

    def windows(step):
        one = pl.ds(pl.multiple_of(FIRST[1] + step * TILE, TILE), TILE)
        two = pl.ds(pl.multiple_of(FIRST[2] + step // 2 * TILE, TILE), TILE)
        return one, two, pl.ds(FIRST[3], TILE), pl.ds(FIRST[4], TILE)

    def per_level(step, chunk):
        one = member[0:512, chunk]

        def for_head(head):
            rows = []
            spans = [(0, 128), (128, 256), (256, 384), (384, 448), (448, 480), (480, 496), (496, 512)]
            for level, (lo, hi) in enumerate(spans, 1):
                rows.append(one[lo:hi] * share[level, head : head + 1, chunk].astype(bf16))
            return jnp.concatenate(rows, axis=0)

        return for_head

    def lse_of(lanes):
        return jnp.concatenate([lse_s[pair, :, lanes] for pair in range(PAIRS)], axis=0)

    def combine(step, carry):
        chunk = pl.ds(pl.multiple_of(step * CHUNK, CHUNK), CHUNK)
        wins = windows(step)
        logs = [lse_of(chunk)]
        for slot in range(3):
            parts = jnp.concatenate(split3(lse_of(wins[slot])), axis=0)
            made = nn(parts, member[slot * TILE : (slot + 1) * TILE, chunk])
            logs.append(made[0:8] + made[8:16] + made[16:24] + (slot + 1) * math.log(2.0))
        top = lse_of(wins[3])
        parts = []
        for slot in range(4):
            inside = (top_lane >= edges[slot]) & (top_lane < edges[slot + 1])
            parts += list(split3(jnp.where(inside, top, 0.0)))
        made = nn(jnp.concatenate(parts, axis=0), member[384:512, chunk])
        for slot in range(4):
            b = slot * 24
            logs.append(made[b : b + 8] + made[b + 8 : b + 16] + made[b + 16 : b + 24] + (slot + 4) * math.log(2.0))
        peak = functools.reduce(jnp.maximum, logs)
        den = functools.reduce(jnp.add, [jnp.exp(one - peak) for one in logs])
        lse = peak + jnp.log(den)
        for level in range(LEVELS):
            share[level, :, chunk] = jnp.exp(logs[level] - lse)
        for_head = per_level(step, chunk)
        for head in range(HEADS):
            at = slice(head * HEAD, (head + 1) * HEAD)
            coarse = jnp.concatenate([out_t[at, win] for win in wins], axis=1)
            made = nn(coarse, for_head(head))
            made = made + share[0, head : head + 1, chunk] * out_t[at, chunk].astype(f32)
            mix_t[at, chunk] = made.astype(bf16)
        return carry

    lax.fori_loop(0, SHORT // CHUNK, combine, 0)
    pump((7, 3), (5, 4), (6, 4))

    bias_mix, gain_two = r.param[2:3, :], r.param[3:4, :]
    shift_two, bias_out = r.param[4:5, :], r.param[5:6, :]
    w_mix = rows_of(wi, 4 * D, D)
    resid[...] = tn(mix_t[...], w_mix)

    def second_norm(step, carry):
        at = pl.ds(pl.multiple_of(step * CHUNK, CHUNK), CHUNK)
        mid = tok[at, :].astype(f32) + resid[at, :] + bias_mix
        resid[at, :] = mid
        normed, _ = normalize(mid)
        n_two[at, :] = (normed * gain_two + shift_two).astype(bf16)
        return carry

    lax.fori_loop(0, SHORT // CHUNK, second_norm, 0)
    pump((7, 4))

    hid, g_pre = grad_kv.at[0:SHORT, 0:D], grad_kv.at[0:SHORT, D : 2 * D]
    acc_out[...] = jnp.zeros_like(acc_out)
    acc_two[...] = jnp.zeros_like(acc_two)

    def total_i(part):
        return Total(di, lanes_at(part * 512, 512), part, p, r.si[0], r.si[1:])

    def total_o(part):
        return TotalRows(do, part, p, r.so[0], r.so[1:7])

    def onward(total, *steps):
        if fast:
            for part, step in steps:
                if isinstance(part, int):
                    total(part).advance(step)
                else:
                    pl.when(part >= 0)(lambda: total(part).advance(step))

    def feed(part, carry):
        lanes = pl.ds(pl.multiple_of(part * 512, 512), 512)
        w_in = wi[:, :, :, :, :, lanes].reshape(512, 512)
        w_out = wo[part].reshape(512, 512)
        b_in = r.bias_in[:, lanes]
        sums = jnp.zeros((1, 512), f32)
        for step in range(FEED_STEPS):
            at = pl.ds(step * (SHORT // FEED_STEPS), SHORT // FEED_STEPS)
            act, slope = gelu_both(nn(n_two[at, :], w_in) + b_in)
            act = act.astype(bf16)
            hid[at, :] = act
            back = (nt(cot[at, :], w_out) * slope).astype(bf16)
            g_pre[at, :] = back
            acc_out[at, :] += nn(act, w_out)
            acc_two[at, :] += nt(back, w_in)
            sums = sums + jnp.sum(back.astype(f32), axis=0, keepdims=True)
            if step == 0:
                onward(total_i, (part - 2, 2), (part - 1, 1))
                onward(total_o, (part - 2, 2), (part - 1, 1))
        r.lanes_in[0:1, lanes] = sums
        di[:, :, :, :, :, lanes] = tn(n_two[...], g_pre[...]).astype(bf16).reshape(4, 2, 2, 2, 16, 512)
        do[part] = tn(hid[...], cot[...]).astype(bf16).reshape(2, 2, 2, 64, 512)
        if fast:
            onward(total_i, (part - 2, 3), (part, 0))
            onward(total_o, (part - 2, 3), (part, 0))
        return carry

    lax.fori_loop(0, 4, feed, 0)

    def middle(step, carry):
        at = pl.ds(pl.multiple_of(step * CHUNK, CHUNK), CHUNK)
        mid = resid[at, :]
        n_two[at, :] = (mid + acc_out[at, :] + bias_out).astype(bf16)
        normed, inverse = normalize(mid)
        g_two = acc_two[at, :]
        c = cot[at, :].astype(f32)
        g_mid = c + normalize_back(g_two * gain_two, normed, inverse)
        resid[at, :] = g_mid
        low = g_mid.astype(bf16)
        g_att[at, :] = low
        vec_b[0:1, :] += jnp.sum(low.astype(f32), axis=0, keepdims=True)
        vec_b[1:2, :] += jnp.sum(g_two * normed, axis=0, keepdims=True)
        vec_b[2:3, :] += jnp.sum(g_two, axis=0, keepdims=True)
        vec_b[3:4, :] += jnp.sum(c, axis=0, keepdims=True)
        return carry

    lax.fori_loop(0, SHORT // CHUNK, middle, 0)
    out_copy = pltpu.make_async_copy(n_two, r.out, r.out_sem.at[0])
    out_copy.start()
    onward(total_i, (2, 2), (3, 1))
    onward(total_o, (2, 2), (3, 1))
    g_mix[...] = nt(g_att[...], w_mix).astype(bf16)

    def inner_sums(step, carry):
        at = pl.ds(pl.multiple_of(step * 512, 512), 512)
        turned = nt(w_mix, g_att[at, :]).astype(bf16).astype(f32) * mix_t[:, at].astype(f32)
        inner_s[:, at] = jnp.concatenate(
            [jnp.sum(turned[h * HEAD : (h + 1) * HEAD], axis=0, keepdims=True) for h in range(HEADS)], axis=0
        )
        return carry

    lax.fori_loop(0, SHORT // 512, inner_sums, 0)

    made = nn(mix_t[...], g_att[...])
    di[:, :, :, :, :, 4 * D :] = made.astype(bf16).reshape(4, 2, 2, 2, 16, D)
    onward(total_i, (4, 0), (2, 3), (3, 2))
    onward(total_o, (2, 3), (3, 2))


    def keep_h(lanes, values):
        for pair in range(PAIRS):
            total_h[pair, :, lanes] = values[2 * pair : 2 * pair + 2]

    def sums_of(level, source, members):
        both = jnp.concatenate(split2(share[level, :, source] * inner_s[:, source]), axis=0)
        made = nt(both, members)
        return made[0:8] + made[8:16]

    tops_acc[0:TILE, :] = jnp.zeros((TILE, D), f32)

    def lift(step, carry):
        pl.when(step == 2)(lambda: onward(total_i, (4, 1)))
        chunk = pl.ds(pl.multiple_of(step * CHUNK, CHUNK), CHUNK)
        to = chunk_rows(step)
        members = chunk_members(chunk)
        for pair_at in range(HEADS // 2):
            lo = pair_at * TILE
            left = [
                jnp.concatenate(
                    [one * share[1 + k, head : head + 1, chunk].astype(bf16) for k, one in enumerate(members)], axis=0
                )
                for head in (2 * pair_at, 2 * pair_at + 1)
            ]
            tokens = g_num[chunk, lo : lo + TILE]
            right = [tokens * r.head_m[0:1, :], tokens * r.head_m[TILE : TILE + 1, :]]
            made = nn(jnp.concatenate(left, axis=1), jnp.concatenate(right, axis=0))
            for level, (low, high) in enumerate(((0, 128), (128, 192), (192, 224))):
                g_num[to[level], lo : lo + TILE] = (made[low:high] * 0.5 ** (level + 1)).astype(bf16)
            tops_acc[0:TILE, lo : lo + TILE] += made[224:352]
        keep_h(chunk, share[0, :, chunk] * inner_s[:, chunk])
        keep_h(to[0], sums_of(1, chunk, member[0:128, chunk]))
        return carry

    lax.fori_loop(0, SHORT // CHUNK, lift, 0)
    g_num[FIRST[4] : STACK, :] = (tops_acc[0:TILE, :] * steps_down).astype(bf16)

    def lift_two(step, carry):
        source = pl.ds(pl.multiple_of(step * 512, 512), 512)
        rows = pl.ds(pl.multiple_of(FIRST[2] + step * TILE, TILE), TILE)
        keep_h(rows, sums_of(2, source, member[128:256, source]))
        return carry

    lax.fori_loop(0, 2, lift_two, 0)
    every = pl.ds(0, SHORT)
    keep_h(pl.ds(FIRST[3], TILE), sums_of(3, every, member[256:384, :]))
    tops = [sums_of(4 + slot, every, member[384:512, :]) for slot in range(4)]
    keep_h(
        pl.ds(FIRST[4], TILE),
        jnp.where(top_lane < 64, tops[0], jnp.where(top_lane < 96, tops[1], jnp.where(top_lane < 112, tops[2], tops[3]))),
    )
    onward(total_i, (3, 3))
    onward(total_o, (3, 3))
    if fast:
        for k, z in enumerate(p.zs):
            remote(do.at[z, p.y, p.x, p.c], r.so[6].at[k], r.so[7].at[1], r.so[7].at[0], p.by_z[k]).start()
    for pair in range(PAIRS):
        weight[pair, :, 0:SHORT] = share[0, 2 * pair : 2 * pair + 2]
    weight[:, :, SHORT:STACK] = jnp.ones((PAIRS, 2, SHORT), f32)

    def tile_backward(tile, pair, scale, scale_t):
        rows = lanes_at(tile * TILE, TILE)
        at = lambda slot: (rows, lanes_at(pair * GROUP + slot * TILE, TILE))
        both = lambda ref: jnp.concatenate([ref[pair, 0:1, rows], ref[pair, 1:2, rows]], axis=1)
        low = probs[tile, :, lanes_at(pair * 2 * TILE, 2 * TILE)].astype(f32)
        times = both(weight)
        num = two_heads(g_num[rows, lanes_at(pair * TILE, TILE)])
        got = squeeze(nt(stack[at(2)], num))
        wide_s = widen((low * (got * times - both(total_h))).astype(bf16))
        wide_p = widen((low * times).astype(bf16))
        query = two_heads(stack[at(0)])
        grad_kv[rows, lanes_at(pair * 2 * TILE, TILE)] = (nn(wide_s, query) * scale).astype(bf16)
        grad_kv[rows, lanes_at(pair * 2 * TILE + TILE, TILE)] = nn(wide_p, num).astype(bf16)
        made = nn(stack[at(1)].T, wide_s)
        head = pl.multiple_of(pair * TILE, TILE)
        grad_qt[pl.ds(head, HEAD), rows] = (made[:HEAD, :TILE] * scale_t).astype(bf16)
        grad_qt[pl.ds(head + HEAD, HEAD), rows] = (made[HEAD:, TILE:] * scale_t).astype(bf16)

    for pair in range(PAIRS):
        tile_backward(15, pair, steps_down, top_scale_t[0:1, :] * 0.125)
    back_s, back_r = r.back_s, r.back_r
    tall = grad_kv[2016:2048, :].astype(f32)
    nothing = jnp.zeros((8, 2 * D), f32)
    back_s[0] = tall[0:16].astype(bf16)
    back_s[1] = jnp.concatenate([tall[16:24], nothing], axis=0).astype(bf16)
    back_s[2] = jnp.concatenate([tall[24:32], nothing], axis=0).astype(bf16)
    back_out = [
        remote(back_s.at[0], back_r.at[0], r.far_sem.at[3], r.far_sem.at[2], (p.dp, other)),
        remote(back_s.at[1], back_r.at[1 + side], r.far_sem.at[3], r.far_sem.at[2], (p.dp, pairs_at)),
        remote(back_s.at[2], back_r.at[1 + side], r.far_sem.at[3], r.far_sem.at[2], (p.dp, pairs_at + 1)),
    ]
    for copy in back_out:
        copy.start()

    def total_a(part):
        return Total(da, lanes_at(part * GROUP, GROUP), part, p, r.sa[0], r.sa[1:])

    def far_grads():
        arrived(back_r, r.far_sem.at[2], p.by_core)
        gone(back_r, r.far_sem.at[3], p.by_core)
        grad_kv[2016:2032, :] = back_r[0]
        grad_kv[2032:2048, :] = (back_r[1].astype(f32) + back_r[2].astype(f32)).astype(bf16)

    def finish_feed():
        for part in range(5):
            total_i(part).finish(r.keep_i)
        arrived(r.so[6], r.so[7].at[0], p.by_core)
        total = do[p.z, p.y, p.x, p.c].astype(f32)
        r.keep_o[...] = functools.reduce(jnp.add, [r.so[6][k].astype(f32) for k in range(3)], total)
        gone(r.so[6], r.so[7].at[1], p.by_core)
        for part in range(4):
            total_o(part).settle()
        for copy in kept[:2]:
            copy.start()

    if fast:
        kept = [
            pltpu.make_async_copy(src, dst, r.keep_sem.at[k])
            for k, (src, dst) in enumerate(
                ((r.keep_i, r.o_i), (r.keep_o, r.o_o), (r.keep_a, r.o_a), (r.keep_v, r.o_v))
            )
        ]

        early = TotalVectors(r.vec_b, p, r.v_sem.at[0], r.got_b, r.mid_b, r.far_b)
        late = TotalVectors(r.vec_a, p, r.v_sem.at[1], r.got_a, r.mid_a, r.far_a)
    vec_b[4:8, :] = jnp.concatenate([r.lanes_in[0:1, k * 512 : (k + 1) * 512] for k in range(4)], axis=0)

    def early_done():
        r.done_b[...] = early.finish()

    def pair_backward(pair, carry):
        def near_back(group, carry):
            for one in range(TOGETHER):
                tile = group * TOGETHER + one
                scale = tile_scale(tile)
                tile_backward(tile, pair, scale, scale * 0.125)
            return carry

        lax.fori_loop(0, 15 // TOGETHER, near_back, 0)
        pl.when(pair == 0)(far_grads)
        if fast:
            pl.when(pair == 0)(lambda: onward(total_i, (4, 2)))
            pl.when(pair == 1)(lambda: onward(total_i, (4, 3)))
            pl.when(pair == 0)(early.begin)
            pl.when(pair == 1)(early.second)
            pl.when(pair == 2)(finish_feed)
            pl.when(pair == 3)(early_done)
        onward(total_a, (pair - 3, 3), (pair - 2, 2), (pair - 1, 1))

        @pl.when(pair == PAIRS - 1)
        def _():
            done = (PAIRS - 1) * GROUP
            acc_two[...] = nt(stack[0:SHORT, 0:done], wa[:, :, :, :, :, SMALL : SMALL + done].reshape(D, done))

        turned_rows = pl.ds(pl.multiple_of(pair * TILE, TILE), TILE)
        kv = lanes_at(pair * 2 * TILE, 2 * TILE)

        def level_sums(step, carry):
            chunk = pl.ds(pl.multiple_of(step * CHUNK, CHUNK), CHUNK)
            wins = windows(step)
            turned = nn(jnp.concatenate([grad_qt[turned_rows, win] for win in wins], axis=1), member[:, chunk])
            turned = (turned + grad_qt[turned_rows, chunk].astype(f32)).astype(bf16)
            stack[chunk, lanes_at(pair * GROUP, TILE)] = turned.T
            made = nn(spread[chunk, :], jnp.concatenate([grad_kv[win, kv] for win in wins], axis=0))
            stack[chunk, lanes_at(pair * GROUP + TILE, 2 * TILE)] = (
                made + grad_kv[chunk, kv].astype(f32)
            ).astype(bf16)
            return carry

        lax.fori_loop(0, SHORT // CHUNK, level_sums, 0)
        lanes = lanes_at(pair * GROUP, GROUP)
        da[:, :, :, :, :, lanes] = tn(n_one[...], stack[0:SHORT, lanes]).astype(bf16).reshape(4, 2, 2, 2, 16, GROUP)
        onward(total_a, (pair, 0))
        return carry

    lax.fori_loop(0, PAIRS, pair_backward, 0)

    done = (PAIRS - 1) * GROUP
    acc_two[...] += nt(stack[0:SHORT, done:], wa[:, :, :, :, :, SMALL + done :].reshape(D, GROUP))
    onward(total_a, (1, 3), (2, 2))

    def first_back(step, carry):
        chunk = pl.ds(pl.multiple_of(step * CHUNK, CHUNK), CHUNK)
        g_one = acc_two[chunk, :]
        normed, inverse = normalize(tok[chunk, :].astype(f32))
        vec_a[0:1, :] += jnp.sum(g_one * normed, axis=0, keepdims=True)
        vec_a[1:2, :] += jnp.sum(g_one, axis=0, keepdims=True)
        g_att[chunk, :] = (resid[chunk, :] + normalize_back(g_one * gain_one, normed, inverse)).astype(bf16)
        return carry

    lax.fori_loop(0, SHORT // CHUNK, first_back, 0)
    tok_copy = pltpu.make_async_copy(g_att, r.g_tok, r.out_sem.at[1])
    tok_copy.start()
    if fast:
        late.begin()
        onward(total_a, (3, 1), (2, 3))
        total_a(0).finish(r.keep_a)
        total_a(1).finish(r.keep_a)
        onward(total_a, (3, 2))
        late.second()
        total_a(2).finish(r.keep_a)
        onward(total_a, (3, 3))
        short = jnp.concatenate([late.finish()[0:2], r.done_b[0:4], jnp.zeros((2, D), f32)], axis=0)
        short = pltpu.roll(short, 512 - 16 * whose, axis=1)[:, 0:SMALL]
        long = jnp.concatenate([r.done_b[4 + k : 5 + k] for k in range(4)], axis=1)
        long = pltpu.roll(jnp.concatenate([long] * 8, axis=0), 2048 - HEAD * whose, axis=1)[:, 0:SMALL]
        r.keep_v[0:8] = short
        r.keep_v[8:16] = long
        kept[3].start()
        total_a(3).finish(r.keep_a)
        kept[2].start()
        for copy in kept:
            copy.wait()
    else:
        r.o_v[0:8] = vec_a[...]
        r.o_v[8:16] = vec_b[...]
    out_copy.wait()
    tok_copy.wait()


def final_kernel(*refs):
    big, small, outs, (kept, vmem_a, vmem_i, vmem_o, vmem_v, sem) = refs[:2], refs[2:6], refs[6:21], refs[21:]
    parts = [pl.ds(k * CHUNK, CHUNK) for k in range(SHORT // CHUNK)]
    count = iter(range(24))
    copy = lambda src, dst: pltpu.make_async_copy(src, dst, sem.at[next(count)])
    into = [copy(ref.at[at], kept.at[slot, at]) for slot, ref in enumerate(big) for at in parts]
    onto = [copy(kept.at[slot, at], outs[slot].at[at]) for slot in range(2) for at in parts]
    rest = [copy(src, dst) for src, dst in zip(small, (vmem_a, vmem_i, vmem_o, vmem_v))]
    for one in into + rest:
        one.start()
    for one, then in zip(into, onto):
        one.wait()
        then.start()
    for one in rest:
        one.wait()
    for slot, at in ((2, 0), (3, 1), (8, 2), (9, 3), (10, 4), (14, 5)):
        outs[slot][...] = vmem_v[at : at + 1, 0:16].reshape(16)
    outs[12][...] = vmem_v[8:9, 0:HEAD].reshape(HEAD)
    for k in range(3):
        for pair in range(PAIRS):
            at = pair * GROUP + k * TILE
            outs[4 + k][:, pair * TILE : (pair + 1) * TILE] = vmem_a[:, at : at + TILE]
    outs[7][...] = vmem_i[:, 4 * D :]
    outs[11][...] = vmem_i[:, : 4 * D]
    outs[13][...] = vmem_o[...]
    for one in onto:
        one.wait()


def scratch_list(fast):
    V, S = pltpu.VMEM, pltpu.SemaphoreType.DMA
    made = dict(
        tok=V((SHORT, D), bf16),
        cot=V((SHORT, D), bf16),
        member=V((D, SHORT), bf16),
        spread=V((SHORT, D), bf16),
        head_m=V((2 * TILE, TILE), bf16),
        group_m=V((TILE, 2 * TILE), bf16),
        bias=V((3, 32, 2 * TILE), f32),
        in_sem=S((17,)),
        out_sem=S((2,)),
        stack=V((STACK, WIDTH), bf16),
        probs=V((16, 32, HEADS * TILE), bf16),
        out_t=V((D, STACK), bf16),
        mix_t=V((D, SHORT), bf16),
        lse_s=V((PAIRS, 2, STACK), f32),
        share=V((LEVELS, HEADS, SHORT), f32),
        inner_s=V((HEADS, SHORT), f32),
        total_h=V((PAIRS, 2, STACK), f32),
        resid=V((SHORT, D), f32),
        n_one=V((SHORT, D), bf16),
        n_two=V((SHORT, D), bf16),
        acc_out=V((SHORT, D), f32),
        acc_two=V((SHORT, D), f32),
        grad_kv=V((STACK, 2 * D), bf16),
        g_att=V((SHORT, D), bf16),
        weight=V((PAIRS, 2, STACK), f32),
        g_num=V((STACK, D), bf16),
        vec_a=V((8, D), f32),
        vec_b=V((8, D), f32),
        param=V((16, D), f32),
        bias_in=V((1, 4 * D), f32),
        lanes_in=V((8, 4 * D), f32),
        far_s=V((2, 16, 2 * D), bf16),
        far_r=V((3, 16, 2 * D), bf16),
        far_sem=S((4,)),
        back_s=V((3, 16, 2 * D), bf16),
        back_r=V((3, 16, 2 * D), bf16),
    )
    if fast:

        def sums(parts, wide):
            shape = lambda *dims: V((parts,) + dims + (16, wide), bf16)
            return [S((parts, 7)), shape(4, 2, 2), shape(2, 2), shape(2, 2), shape(2), shape(2), shape(3)]

        rows = lambda *dims: V((4,) + dims + (D,), bf16)
        made.update(
            wa=V(SLOTS + (16, WIDTH + SMALL), bf16),
            wi=V(SLOTS + (16, 5 * D), bf16),
            wo=V(SLOTS + (64, D), bf16),
            da=V(SLOTS + (16, WIDTH), bf16),
            di=V(SLOTS + (16, 5 * D), bf16),
            do=V(SLOTS + (64, D), bf16),
            g_sem=S((8, 7)),
            si=sums(5, D),
            so=[S((4, 5)), rows(2, 2, 64), rows(2, 32), rows(2, 32), rows(32), rows(32), V((3, 64, D), bf16), S((2,))],
            sa=sums(4, GROUP),
            v_sem=S((2, 4)),
            got_a=V((7, 8, D), f32),
            mid_a=V((8, D), f32),
            far_a=V((3, 8, D), f32),
            got_b=V((7, 8, D), f32),
            mid_b=V((8, D), f32),
            far_b=V((3, 8, D), f32),
            done_b=V((8, D), f32),
            vec_in=[V((16,), bf16)] * 6 + [V((HEAD,), bf16)],
            keep_a=V((16, WIDTH), f32),
            keep_i=V((16, 5 * D), f32),
            keep_o=V((HEAD, D), f32),
            keep_v=V((16, SMALL), f32),
            keep_sem=S((4,)),
        )
    return made


def constants():
    member = member_matrix()
    as_low = lambda values: jnp.asarray(values.astype(np.float32), bf16)
    return dict(
        member_h=as_low(member),
        spread_h=as_low(np.ascontiguousarray(member.T)),
        head_h=as_low(head_mask()),
        group_h=as_low(group_mask()),
        bias_h=jnp.asarray(block_bias()),
    )


def run_layer(fast, hbm, vmem):
    sd = jax.ShapeDtypeStruct
    const = constants()
    hbm = dict(hbm, **const)
    here, there = pl.BlockSpec(memory_space=pltpu.VMEM), pl.BlockSpec(memory_space=pl.ANY)
    slots = () if fast else SLOTS
    kind = f32 if fast else bf16
    outs = dict(
        out=sd((SHORT, D), bf16),
        g_tok=sd((SHORT, D), bf16),
        o_a=sd(slots + (16, WIDTH), kind),
        o_i=sd(slots + (16, 5 * D), kind),
        o_o=sd(slots + (64, D), kind),
        o_v=sd((16, SMALL if fast else D), f32),
    )
    row_length = hbm.pop("row_length")
    operands = dict(hbm, row_length=row_length, **vmem)
    flat = lambda parts: [one for part in parts.values() for one in (part if isinstance(part, list) else [part])]
    specs = [there] * len(flat(hbm)) + [pl.BlockSpec(memory_space=pltpu.SMEM)] + [here] * len(vmem)
    hbm_outs = len(outs) if fast else 2
    return pl.pallas_call(
        functools.partial(layer_kernel, fast, dict(operands, **outs)),
        out_shape=list(outs.values()),
        in_specs=specs,
        out_specs=[there] * hbm_outs + [here] * (len(outs) - hbm_outs),
        scratch_shapes=flat(scratch_list(fast)),
        compiler_params=pltpu.CompilerParams(
            collective_id=0, has_side_effects=True, vmem_limit_bytes=63 * 2**20
        ),
    )(*flat(operands))


def finish_outputs(*parts):
    sd = jax.ShapeDtypeStruct
    vmem, hbm = pl.BlockSpec(memory_space=pltpu.VMEM), pl.BlockSpec(memory_space=pl.ANY)
    own, square = sd((16,), f32), sd((16, D), f32)
    tokens = sd((SHORT, D), bf16)
    outs = [tokens, tokens, own, own, square, square, square, square, own, own, own]
    outs += [sd((16, 4 * D), f32), sd((HEAD,), f32), sd((HEAD, D), f32), own]
    return pl.pallas_call(
        final_kernel,
        out_shape=outs,
        in_specs=[hbm] * 6,
        out_specs=[hbm] * 2 + [vmem] * 13,
        scratch_shapes=[
            pltpu.VMEM((2, SHORT, D), bf16),
            pltpu.VMEM((16, WIDTH), f32),
            pltpu.VMEM((16, 5 * D), f32),
            pltpu.VMEM((HEAD, D), f32),
            pltpu.VMEM((16, SMALL), f32),
            pltpu.SemaphoreType.DMA((20,)),
        ],
    )(*parts)


def on_device(
    tokens, cotangent, row_length, first_gain, first_shift, query_weight, key_weight, value_weight,
    mixer_weight, mixer_bias, second_gain, second_shift, inner_weight, inner_bias, outer_weight, outer_bias,
):
    n_dp, n_fsdp = lax.axis_size("dp"), lax.axis_size("fsdp")
    fast = (n_dp, n_fsdp) == (8, 4) and query_weight.shape[0] == 16
    vectors = (first_gain, first_shift, mixer_bias, second_gain, second_shift, outer_bias)
    first = dict(tok_h=tokens, cot_h=cotangent, row_length=row_length)
    if fast:
        first.update(
            wq_s=query_weight, wk_s=key_weight, wv_s=value_weight, wm_s=mixer_weight, wi_s=inner_weight, wo_s=outer_weight,
            vectors=list(vectors) + [inner_bias],
        )
        return finish_outputs(*run_layer(True, first, dict()))
    whole = lambda part: lax.all_gather(part, AXES, axis=0, tiled=True)
    three = jnp.stack([part.reshape(-1, PAIRS, TILE) for part in (query_weight, key_weight, value_weight)], axis=2)
    wide = whole(three.reshape(-1, WIDTH))
    eights = [whole(vector).reshape(4, 8, 16) for vector in vectors]
    small = jnp.zeros((4, 8, 16, SMALL), bf16)
    for row, vector in enumerate(eights):
        for at in range(8):
            small = small.at[:, at, row, 16 * at : 16 * at + 16].set(vector[:, at])
    pairs = whole(inner_bias).reshape(4, 4, 2, 64)
    pairs_at = small.reshape(4, 4, 2, 16, SMALL)
    for at in range(2):
        pairs_at = pairs_at.at[:, :, at, 6, 64 * at : 64 * at + 64].set(pairs[:, :, at])
    wide = jnp.concatenate((pairs_at.reshape(4, 8, 16, SMALL), wide.reshape(4, 8, 16, WIDTH)), axis=-1)
    weights = dict(
        wa=wide.reshape(SLOTS + (16, WIDTH + SMALL)),
        wi=whole(jnp.concatenate((inner_weight, mixer_weight), axis=1)).reshape(SLOTS + (16, 5 * D)),
        wo=whole(outer_weight).reshape(SLOTS + (64, D)),
    )
    out, g_tok, d_a, d_i, d_o, o_v = run_layer(False, first, weights)
    owned = lambda part: lax.psum_scatter(part, AXES, scatter_dimension=0, tiled=True)
    g_a = owned(d_a.astype(f32).reshape(D, WIDTH))
    g_q, g_k, g_v = (g_a.reshape(-1, PAIRS, 3, TILE)[:, :, k].reshape(-1, D) for k in range(3))
    g_i = owned(d_i.astype(f32).reshape(D, 5 * D))
    g_i, g_m = g_i[:, : 4 * D], g_i[:, 4 * D :]
    g_o = owned(d_o.astype(f32).reshape(4 * D, D))
    six = [owned(o_v[k]) for k in (0, 1, 8, 9, 10, 11)]
    g_bias_in = owned(o_v[12:16].reshape(-1))
    return (
        out, g_tok, six[0], six[1], g_q, g_k, g_v, g_m, six[2], six[3], six[4], g_i, g_bias_in, g_o, six[5],
    )


def solution(mesh):
    rows, flat, both = P(AXES, None), P(AXES), P("dp")
    in_specs = (rows, rows, both, flat, flat, rows, rows, rows, rows, flat, flat, flat, rows, flat, rows, flat)
    out_specs = (rows, rows, flat, flat, rows, rows, rows, rows, flat, flat, flat, rows, flat, rows, flat)
    return jax.shard_map(on_device, mesh=mesh, in_specs=in_specs, out_specs=out_specs, check_vma=False)
```

```python
import functools
import math
import types

import jax
import jax.numpy as jnp
import numpy as np
from jax import lax
from jax.experimental import pallas as pl
from jax.experimental.pallas import tpu as pltpu
from jax.sharding import PartitionSpec as P

D = 512
HEADS = 8
HEAD = 64
BLOCK = 16
SHORT = 1024
LEVELS = 8
TILE = 128
TOGETHER = 5
CHUNK = 256
STACK = 2 * SHORT
WIDTH = 3 * D
SMALL = 128
GROUP = 3 * TILE
PAIRS = HEADS // 2
FEED_STEPS = 2
AXES = ("dp", "fsdp")
MESH = pl.DeviceIdType.MESH
SLOTS = (4, 2, 2, 2)

norm_eps = 1e-05
far_off = -1e30
f32 = jnp.float32
bf16 = jnp.bfloat16

FIRST = [STACK - (STACK >> level) for level in range(LEVELS + 1)]
LOW_TOP = 4


def member_matrix():
    token = np.arange(SHORT)
    rows = []
    for level, span in ((1, 256), (2, 512), (3, 1024)):
        rows.append((token[None] % span) >> level == np.arange(TILE)[:, None])
    for level in range(LOW_TOP, LEVELS):
        rows.append(token[None] >> level == np.arange(SHORT >> level)[:, None])
    rows.append(np.zeros((8, SHORT), bool))
    return np.concatenate(rows).astype(np.float32)


def spread_matrix():
    member = member_matrix()
    near = np.concatenate([member[0:128, :CHUNK], member[128:192, :CHUNK], member[256:288, :CHUNK], np.zeros((32, CHUNK))])
    return np.concatenate([np.tile(near, (1, SHORT // CHUNK)), member[384:]]).T.astype(np.float32)


def block_bias():
    key = np.arange(32)[:, None]
    query = np.arange(2 * TILE)[None]
    across = (key < BLOCK) != (query % 32 < BLOCK)
    last = np.where(query % TILE >= 96, ~across, across)
    kinds = [np.ones_like(across), across, last]
    return np.stack([np.where(kind, 0.0, far_off) for kind in kinds]).astype(np.float32)


def head_mask():
    lane = np.arange(TILE)[None]
    side = np.arange(2 * TILE)[:, None] // TILE
    return (lane // HEAD == side).astype(np.float32)


def group_mask():
    key = np.arange(TILE)[:, None]
    query = np.arange(2 * TILE)[None]
    return (key // 32 == query % TILE // 32).astype(np.float32)


def top_level_of():
    index = np.arange(TILE)
    return np.minimum(LOW_TOP + (index >= 64) * 1 + (index >= 96) * 1 + (index >= 112) * 1, 7)


def nn(a, b):
    return lax.dot_general(a, b, (((1,), (0,)), ((), ())), preferred_element_type=f32)


def nt(a, b):
    return lax.dot_general(a, b, (((1,), (1,)), ((), ())), preferred_element_type=f32)


def tn(a, b):
    return lax.dot_general(a, b, (((0,), (0,)), ((), ())), preferred_element_type=f32)


def normalize(values):
    center = values - jnp.mean(values, axis=-1, keepdims=True)
    inverse = lax.rsqrt(jnp.mean(center * center, axis=-1, keepdims=True) + norm_eps)
    return center * inverse, inverse


def normalize_back(grad_normed, normed, inverse):
    return inverse * (
        grad_normed
        - jnp.mean(grad_normed, axis=-1, keepdims=True)
        - normed * jnp.mean(grad_normed * normed, axis=-1, keepdims=True)
    )


def gelu_both(v):
    mag = jnp.abs(v) * (0.5**0.5)
    t = 1.0 / (1.0 + 0.3275911 * mag)
    gauss = jnp.exp(-0.5 * v * v)
    poly = t * (
        0.254829592
        + t * (-0.284496736 + t * (1.421413741 + t * (-1.453152027 + t * 1.061405429)))
    )
    tail = 0.5 * poly * gauss
    cdf = jnp.where(v < 0, tail, 1.0 - tail)
    return v * cdf, cdf + v * gauss * ((2 * math.pi) ** -0.5)


def split3(values):
    one = values.astype(bf16)
    rest = values - one.astype(f32)
    two = rest.astype(bf16)
    return one, two, (rest - two.astype(f32)).astype(bf16)


def split2(values):
    one = values.astype(bf16)
    return one, (values - one.astype(f32)).astype(bf16)


class Place:
    def __init__(self):
        self.dp = lax.axis_index("dp")
        self.fs = lax.axis_index("fsdp")
        self.z, self.y = self.dp // 2, self.dp % 2
        self.x, self.c = self.fs // 2, self.fs % 2
        self.oy, self.ox, self.oc = 1 - self.y, 1 - self.x, 1 - self.c
        self.zs = [lax.rem(self.z + step, 4) for step in (1, 2, 3)]
        self.by_core = (self.dp, self.x * 2 + self.oc)
        self.by_x = (self.dp, self.ox * 2 + self.c)
        self.by_y = (self.z * 2 + self.oy, self.fs)
        self.by_z = [(z * 2 + self.y, self.fs) for z in self.zs]
        ys, xs, cs = (self.y, self.oy), (self.x, self.ox), (self.c, self.oc)
        self.plane = [(self.z * 2 + ys[k // 4], xs[k // 2 % 2] * 2 + cs[k % 2]) for k in range(1, 8)]


def remote(src, dst, send, recv, device):
    return pltpu.make_async_remote_copy(
        src_ref=src, dst_ref=dst, send_sem=send, recv_sem=recv, device_id=device, device_id_type=MESH
    )


def arrived(ref, sem, device):
    remote(ref, ref, sem, sem, device).wait_recv()


def gone(ref, sem, device):
    remote(ref, ref, sem, sem, device).wait_send()


class Gather:
    def __init__(self, ref, lanes, p, sems):
        self.at = lambda z, y, x: ref.at[z, y, x, p.c, :, lanes]
        self.p, self.sems = p, sems

    def advance(self, step):
        p, at, sems = self.p, self.at, self.sems
        low, high, both, full = pl.ds(0, 2), pl.ds(2, 2), pl.ds(0, 2), pl.ds(0, 4)
        if step:
            ref = (at(pl.ds(0, 3), p.y, p.x), at(full, p.y, p.x), at(full, both, p.x), at(full, both, both))[step - 1]
            arrived(ref, sems.at[step - 1], p.by_core)
        if step == 4:
            gone(at(pl.ds(0, 3), p.y, p.x), sems.at[4], p.by_core)
            gone(at(pl.ds(0, 3), both, both), sems.at[5], p.by_core)
            gone(at(full, both, both), sems.at[6], p.by_core)
            return
        if step == 0:
            parts = [(at(p.z, p.y, p.x), device) for device in p.by_z]
        elif step == 1:
            parts = [(at(low, p.y, p.x), p.by_x), (at(high, p.y, p.x), p.by_y)]
        elif step == 2:
            parts = [(at(low, p.y, both), p.by_y), (at(high, both, p.x), p.by_x)]
        else:
            parts = [(at(full, both, both), p.by_core)]
        for part, device in parts:
            remote(part, part, sems.at[(4, 5, 5, 6)[step]], sems.at[step], device).start()


class Total:
    def __init__(self, ref, lanes, part, p, sems, bufs):
        self.ref, self.lanes, self.part, self.p, self.sems, self.bufs = ref, lanes, part, p, sems.at[part], bufs

    def add(self, index, buf):
        at = index + (self.p.c, slice(None), self.lanes)
        self.ref[at] = self.ref[at] + buf

    def advance(self, step):
        p, part, sems = self.p, self.part, self.sems
        from_core, one_a, one_b, two_a, two_b, far = self.bufs
        at = lambda z, y, x, c: self.ref.at[z, y, x, c, :, self.lanes]
        low, high, both, full, every = pl.ds(0, 2), pl.ds(2, 2), pl.ds(0, 2), pl.ds(0, 4), slice(None)
        if step:
            ref = (from_core.at[part], from_core.at[part, both], from_core.at[part, 0])[step - 1]
            arrived(ref, sems.at[step - 1], p.by_core)
        if step == 0:
            sends = [(at(full, both, both, p.oc), from_core, p.by_core)]
        elif step == 1:
            for z in range(4):
                self.add((z, every, every), from_core[part, z])
            sends = [(at(low, p.oy, both, p.c), one_a, p.by_y), (at(high, both, p.ox, p.c), one_b, p.by_x)]
        elif step == 2:
            for z in range(2):
                self.add((z, p.y, every), one_a[part, z])
                self.add((2 + z, every, p.x), one_b[part, z])
            sends = [(at(low, p.y, p.ox, p.c), two_a, p.by_x), (at(high, p.oy, p.x, p.c), two_b, p.by_y)]
        else:
            for z in range(2):
                self.add((z, p.y, p.x), two_a[part, z])
                self.add((2 + z, p.y, p.x), two_b[part, z])
            for k, z in enumerate(p.zs):
                remote(at(z, p.y, p.x, p.c), far.at[part, k], sems.at[6], sems.at[3], p.by_z[k]).start()
            return
        for src, buf, device in sends:
            remote(src, buf.at[part], sems.at[(4, 5, 5)[step]], sems.at[step], device).start()

    def finish(self, out):
        p, sems, far, part = self.p, self.sems, self.bufs[5], self.part
        arrived(far.at[part], sems.at[3], p.by_core)
        total = self.ref[p.z, p.y, p.x, p.c, :, self.lanes].astype(f32)
        out[:, self.lanes] = functools.reduce(jnp.add, [far[part, k].astype(f32) for k in range(3)], total)
        gone(self.bufs[0].at[part], sems.at[4], p.by_core)
        gone(self.bufs[0].at[part, pl.ds(0, 3)], sems.at[5], p.by_core)
        gone(far.at[part], sems.at[6], p.by_core)


class TotalRows:
    def __init__(self, ref, part, p, sems, bufs):
        self.ref, self.part, self.p, self.sems, self.bufs = ref, part, p, sems.at[part], bufs

    def add(self, index, buf):
        at = (self.part,) + index
        self.ref[at] = self.ref[at] + buf

    def advance(self, step):
        p, part, sems = self.p, self.part, self.sems
        from_core, one_a, one_b, two_a, two_b, _ = self.bufs
        both, every, low, high = pl.ds(0, 2), slice(None), pl.ds(0, 32), pl.ds(32, 32)
        at = lambda y, x, c, *rows: self.ref.at[(part, y, x, c) + rows]
        if step:
            ref = (from_core.at[part], from_core.at[part, 0], from_core.at[part, 0, 0])[step - 1]
            arrived(ref, sems.at[step - 1], p.by_core)
        if step == 0:
            sends = [(at(both, both, p.oc), from_core, p.by_core)]
        elif step == 1:
            self.add((every, every, p.c), from_core[part])
            sends = [(at(p.oy, both, p.c, low), one_a, p.by_y), (at(both, p.ox, p.c, high), one_b, p.by_x)]
        elif step == 2:
            self.add((p.y, every, p.c, low), one_a[part])
            self.add((every, p.x, p.c, high), one_b[part])
            sends = [(at(p.y, p.ox, p.c, low), two_a, p.by_x), (at(p.oy, p.x, p.c, high), two_b, p.by_y)]
        else:
            self.add((p.y, p.x, p.c, low), two_a[part])
            self.add((p.y, p.x, p.c, high), two_b[part])
            return
        for src, buf, device in sends:
            remote(src, buf.at[part], sems.at[(3, 4, 4)[step]], sems.at[step], device).start()

    def settle(self):
        gone(self.bufs[0].at[self.part], self.sems.at[3], self.p.by_core)
        gone(self.bufs[5], self.sems.at[4], self.p.by_core)


class TotalVectors:
    def __init__(self, ref, p, sems, got, mid, far):
        self.ref, self.p, self.sems, self.got, self.mid, self.far = ref, p, sems, got, mid, far

    def begin(self):
        for k, device in enumerate(self.p.plane):
            remote(self.ref, self.got.at[k], self.sems.at[1], self.sems.at[0], device).start()

    def second(self):
        arrived(self.got, self.sems.at[0], self.p.by_core)
        self.mid[...] = functools.reduce(jnp.add, [self.got[k] for k in range(7)], self.ref[...])
        for k, device in enumerate(self.p.by_z):
            remote(self.mid, self.far.at[k], self.sems.at[3], self.sems.at[2], device).start()

    def finish(self):
        arrived(self.far, self.sems.at[2], self.p.by_core)
        gone(self.got, self.sems.at[1], self.p.by_core)
        gone(self.far, self.sems.at[3], self.p.by_core)
        return functools.reduce(jnp.add, [self.far[k] for k in range(3)], self.mid[...])


def layer_kernel(fast, kinds, *refs):
    shapes = dict(kinds, **scratch_list(fast))
    r, left = types.SimpleNamespace(), list(refs)
    for name, kind in shapes.items():
        amount = len(kind) if isinstance(kind, list) else 1
        taken, left = left[:amount], left[amount:]
        setattr(r, name, taken if isinstance(kind, list) else taken[0])
    assert not left
    p = Place()
    tok, cot = r.tok, r.cot
    member, spread = r.member, r.spread
    stack, probs, out_t, mix_t = r.stack, r.probs, r.out_t, r.mix_t
    lse_s, share, inner_s, total_h = r.lse_s, r.share, r.inner_s, r.total_h
    resid, n_one, n_two = r.resid, r.n_one, r.n_two
    acc_out, acc_two = r.acc_out, r.acc_two
    g_att, g_num = r.g_att, r.g_num
    g_mix, weight = g_num.at[0:SHORT], r.weight
    grads = r.grads
    vec_a, vec_b = r.vec_a, r.vec_b
    wa, wi, wo = r.wa, r.wi, r.wo
    da, di, do = (r.da, r.di, r.do) if fast else (r.o_a, r.o_i, r.o_o)

    def fetch(src, dst, slot):
        copy = pltpu.make_async_copy(src, dst, r.in_sem.at[slot])
        copy.start()
        return copy

    def taken(ref, slot):
        pltpu.make_async_copy(ref, ref, r.in_sem.at[slot]).wait()

    if fast:
        small_in = [fetch(ref, kept, k) for k, (ref, kept) in enumerate(zip(r.vectors, r.vec_in))]
        own_a, own_i, own_o = (ref.at[p.z, p.y, p.x, p.c] for ref in (wa, wi, wo))
        for pair in range(PAIRS):
            for slot, ref in enumerate((r.wq_s, r.wk_s, r.wv_s)):
                there = pl.ds(SMALL + pair * GROUP + slot * TILE, TILE)
                fetch(ref.at[:, pl.ds(pair * TILE, TILE)], own_a.at[:, there], 7)
        fetch(r.wi_s, own_i.at[:, pl.ds(0, 4 * D)], 8)
        fetch(r.wm_s, own_i.at[:, pl.ds(4 * D, D)], 8)
        fetch(r.wo_s, own_o, 9)
    tok_in = fetch(r.tok_h, tok, 10)
    rest_in = [
        fetch(src, dst, 11 + k)
        for k, (src, dst) in enumerate(
            ((r.member_h, member), (r.head_h, r.head_m), (r.group_h, r.group_m), (r.bias_h, r.bias), (r.cot_h, cot), (r.spread_h, spread))
        )
    ]

    other = p.fs // 2 * 2 + 1 - p.fs % 2
    pairs_at = (1 - p.fs // 2) * 2
    side = p.fs % 2
    barrier = pltpu.get_barrier_semaphore()
    reach = [(p.dp, other), (p.dp, pairs_at), (p.dp, pairs_at + 1)]
    if fast:
        reach += p.plane[3:] + p.by_z
    for device in reach:
        pl.semaphore_signal(barrier, inc=1, device_id=device, device_id_type=MESH)
    if fast:
        whose = p.dp * 4 + p.fs
        for copy in small_in:
            copy.wait()
        at = lax.broadcasted_iota(jnp.int32, (HEAD, SMALL), 0)
        lane = lax.broadcasted_iota(jnp.int32, (HEAD, SMALL), 1)
        rows = [ref[...].astype(f32).reshape(1, 16) for ref in r.vec_in[:6]]
        rows = jnp.concatenate(rows + [jnp.zeros((10, 16), f32)], axis=0).astype(bf16)
        spot = (lane[0:16] == at[0:16] + 16 * (whose % 8)).astype(f32).astype(bf16)
        own = nn(rows, spot)
        bias = jnp.concatenate([r.vec_in[6][...].astype(f32).reshape(1, HEAD), jnp.zeros((15, HEAD), f32)], axis=0)
        spot = (lane == at + HEAD * (whose % 2)).astype(f32).astype(bf16)
        own_bias = nn(bias.astype(bf16), spot)
        own = jnp.concatenate([own[0:6], own_bias[0:1], jnp.zeros((9, SMALL), f32)], axis=0)
        own_a[:, 0:SMALL] = own.astype(bf16)
    if fast:
        taken(own_a.at[:, pl.ds(SMALL, WIDTH)], 7)
    pl.semaphore_wait(barrier, len(reach))


    def first_norm(step, carry):
        at = pl.ds(pl.multiple_of(step * CHUNK, CHUNK), CHUNK)
        acc_two[at, :] = normalize(tok[at, :].astype(f32))[0]
        return carry

    if fast:
        spans = [(wa, 0, SMALL + GROUP), (wa, SMALL + GROUP, 3 * GROUP), (wi, 0, 1280), (wi, 1280, 1280), (wo, 0, D)]
        gathers = [
            Gather(ref, pl.ds(lo, wide), p, r.g_sem.at[k]) for k, (ref, lo, wide) in enumerate(spans)
        ]

    def pump(*events):
        if fast:
            for k, step in events:
                gathers[k].advance(step)

    pump((0, 0), (1, 0))
    if fast:
        taken(own_i, 8)
        taken(own_o, 9)
    pump((2, 0))
    tok_in.wait()
    lax.fori_loop(0, SHORT // CHUNK, first_norm, 0)
    pump((0, 1), (3, 0), (0, 2), (1, 1), (0, 3), (1, 2), (0, 4))
    for copy in rest_in:
        copy.wait()

    def rows_of(ref, lo, width):
        return ref[:, :, :, :, :, lo : lo + width].reshape(512, width)

    small = wa[:, :, :, :, :, 0:SMALL].astype(f32)
    by_z = jnp.sum(small, axis=(1, 2, 3))
    param = jnp.concatenate([by_z[z] for z in range(4)], axis=1)
    r.param[...] = param
    by_pair = jnp.sum(small, axis=3)
    r.bias_in[...] = jnp.concatenate(
        [by_pair[z, y, x, 6:7, :] for z in range(4) for y in range(2) for x in range(2)], axis=1
    )
    vec_a[...] = jnp.zeros_like(vec_a)
    vec_b[...] = jnp.zeros_like(vec_b)
    r.lanes_in[...] = jnp.zeros_like(r.lanes_in)

    gain_one, shift_one = r.param[0:1, :], r.param[1:2, :]

    def scale_shift(step, carry):
        at = pl.ds(pl.multiple_of(step * CHUNK, CHUNK), CHUNK)
        n_one[at, :] = (acc_two[at, :] * gain_one + shift_one).astype(bf16)
        return carry

    lax.fori_loop(0, SHORT // CHUNK, scale_shift, 0)

    index = lax.broadcasted_iota(jnp.int32, (TILE, 1), 0)
    steps_down = jnp.where(
        index < 64, 1 / 16, jnp.where(index < 96, 1 / 32, jnp.where(index < 112, 1 / 64, 1 / 128))
    ).astype(f32)

    def chunk_rows(step):
        one = pl.ds(pl.multiple_of(FIRST[1] + step * 128, 128), 128)
        two = pl.ds(pl.multiple_of(FIRST[2] + step * 64, 64), 64)
        return one, two, pl.ds(pl.multiple_of(FIRST[3] + step * 32, 32), 32)

    def chunk_members(chunk):
        near = [member[lo:hi, 0:CHUNK] for lo, hi in ((0, 128), (128, 192), (256, 288))]
        return near + [member[lo:hi, chunk] for lo, hi in ((384, 448), (448, 480), (480, 496), (496, 512))]

    lane_group = lax.broadcasted_iota(jnp.int32, (32, TILE), 1) // 32

    def squeeze(tall):
        parts = [tall[32 * part : 32 * part + 32, :] for part in range(4)]
        return jnp.where(
            lane_group < 2,
            jnp.where(lane_group == 0, parts[0], parts[1]),
            jnp.where(lane_group == 2, parts[2], parts[3]),
        )

    def widen(low):
        return jnp.concatenate([low, low, low, low], axis=0) * r.group_m[:, 0 : low.shape[1]]

    def by_head(both):
        half = both.shape[0] // 2
        lane = lax.broadcasted_iota(jnp.int32, (half, TILE), 1)
        return jnp.where(lane < HEAD, both[:half], both[half:])

    def two_heads(low):
        return jnp.concatenate([low, low], axis=0) * r.head_m[...]

    top_lane = lax.broadcasted_iota(jnp.int32, (HEADS, TILE), 1)
    top_scale_t = jnp.where(
        top_lane < 64, 1 / 16, jnp.where(top_lane < 96, 1 / 32, jnp.where(top_lane < 112, 1 / 64, 1 / 128))
    ).astype(f32)

    def tile_scale(tile):
        return jnp.where(
            tile < 8, 1.0, jnp.where(tile < 12, 0.5, jnp.where(tile < 14, 0.25, 0.125))
        ).astype(f32)

    def lanes_at(start, wide):
        return pl.ds(pl.multiple_of(start, TILE), wide)

    def tile_forward(tile, pair, kind, scale_t):
        rows = lanes_at(tile * TILE, TILE)
        at = lambda slot: (rows, lanes_at(pair * GROUP + slot * TILE, TILE))
        score = nt(two_heads(stack[at(1)]), stack[at(0)])
        score = jnp.concatenate([squeeze(score[:TILE]), squeeze(score[TILE:])], axis=1) + r.bias[kind]
        peak = jnp.max(score, axis=0, keepdims=True)
        prob = jnp.exp(score - peak)
        total = jnp.sum(prob, axis=0, keepdims=True)
        low = (prob * (1.0 / total)).astype(bf16)
        probs[tile, :, lanes_at(pair * 2 * TILE, 2 * TILE)] = low
        log_total = peak + jnp.log(total)
        lse_s[pair, 0:1, rows] = log_total[:, :TILE]
        lse_s[pair, 1:2, rows] = log_total[:, TILE:]
        made = nn(stack[at(2)].T, widen(low))
        head = pl.multiple_of(pair * TILE, TILE)
        out_t[pl.ds(head, HEAD), rows] = (made[:HEAD, :TILE] * scale_t).astype(bf16)
        out_t[pl.ds(head + HEAD, HEAD), rows] = (made[HEAD:, TILE:] * scale_t).astype(bf16)

    far_s, far_r = r.far_s, r.far_r
    far_out = [
        remote(far_s.at[0], far_r.at[0], r.far_sem.at[1], r.far_sem.at[0], (p.dp, other)),
        remote(far_s.at[1], far_r.at[1 + side], r.far_sem.at[1], r.far_sem.at[0], (p.dp, pairs_at)),
        remote(far_s.at[1], far_r.at[1 + side], r.far_sem.at[1], r.far_sem.at[0], (p.dp, pairs_at + 1)),
    ]
    tops_acc = acc_out

    def pair_forward(pair, carry):
        def pump_here(*plan):
            for number, events in enumerate(plan):
                if events:
                    pl.when(pair == number)(functools.partial(pump, *events))

        pump_here([], [(1, 4)])
        lanes = lanes_at(pair * GROUP, GROUP)
        made = nn(n_one[...], wa[:, :, :, :, :, lanes_at(SMALL + pair * GROUP, GROUP)].reshape(D, GROUP))
        first = lax.broadcasted_iota(jnp.int32, (1, GROUP), 1)
        stack[0:SHORT, lanes] = (made * jnp.where(first < TILE, 0.125, 1.0)).astype(bf16)
        key_like = first < 2 * TILE
        pump_here([(2, 1), (4, 0)])
        tops_acc[0:TILE, 0:GROUP] = jnp.zeros((TILE, GROUP), f32)

        def pool(step, carry):
            chunk = pl.ds(pl.multiple_of(step * CHUNK, CHUNK), CHUNK)
            made = nn(jnp.concatenate(chunk_members(chunk), axis=0), stack[chunk, lanes])
            to = chunk_rows(step)
            for level, (lo, hi) in enumerate(((0, 128), (128, 192), (192, 224))):
                scale = jnp.where(key_like, 0.5 ** (level + 1), 1.0)
                stack[to[level], lanes] = (made[lo:hi] * scale).astype(bf16)
            tops_acc[0:TILE, 0:GROUP] += made[224:352]
            return carry

        lax.fori_loop(0, SHORT // CHUNK, pool, 0)
        stack[FIRST[4] : STACK, lanes] = (
            tops_acc[0:TILE, 0:GROUP] * jnp.where(key_like, steps_down, 1.0)
        ).astype(bf16)
        theirs = lanes_at(pair * GROUP + TILE, 2 * TILE)
        mine = lanes_at(pair * 2 * TILE, 2 * TILE)
        far_s[0, :, mine] = stack[2016:2032, theirs]
        far_s[1, :, mine] = stack[2032:2048, theirs]

        @pl.when(pair == PAIRS - 1)
        def _():
            for copy in far_out:
                copy.start()

        def near_tiles(group, carry):
            for one in range(TOGETHER):
                tile = group * TOGETHER + one
                tile_forward(tile, pair, jnp.where(tile < 8, 0, 1), tile_scale(tile))
            for when, what, events in (
                (0, 1, [(1, 3)]),
                (0, 2, [(2, 2), (3, 1)]),
                (1, 2, [(2, 3), (3, 2), (4, 1)]),
                (2, 2, [(2, 4)]),
                (3, 1, [(3, 3), (4, 2)]),
            ):
                pl.when((pair == when) & (group == what))(functools.partial(pump, *events))
            return carry

        lax.fori_loop(0, 15 // TOGETHER, near_tiles, 0)
        return carry

    lax.fori_loop(0, PAIRS, pair_forward, 0)
    arrived(far_r, r.far_sem.at[0], p.by_core)
    gone(far_r, r.far_sem.at[1], p.by_core)
    last_rows = jnp.concatenate([far_r[1].astype(f32)[:8], far_r[2].astype(f32)[:8]], axis=0).astype(bf16)
    for pair in range(PAIRS):
        theirs = slice(pair * GROUP + TILE, (pair + 1) * GROUP)
        mine = slice(pair * 2 * TILE, (pair + 1) * 2 * TILE)
        stack[2016:2032, theirs] = far_r[0, :, mine]
        stack[2032:2048, theirs] = last_rows[:, mine]
    for pair in range(PAIRS):
        tile_forward(15, pair, 2, top_scale_t[0:1, :])
    idle = jnp.where(r.row_length[0] > SHORT, 0.0, far_off)
    lse_s[:, :, 1920:2048] = lse_s[:, :, 1920:2048] + jnp.where(top_lane[0:2] >= 96, idle, 0.0)

    edges = (0, 64, 96, 112, 128)

    def windows(step):
        one = pl.ds(pl.multiple_of(FIRST[1] + step * TILE, TILE), TILE)
        two = pl.ds(pl.multiple_of(FIRST[2] + step // 2 * TILE, TILE), TILE)
        return one, two, pl.ds(FIRST[3], TILE), pl.ds(FIRST[4], TILE)

    def per_level(step, chunk):
        one = member[0:512, chunk]

        def for_head(head):
            rows = []
            spans = [(0, 128), (128, 256), (256, 384), (384, 448), (448, 480), (480, 496), (496, 512)]
            for level, (lo, hi) in enumerate(spans, 1):
                rows.append(one[lo:hi] * share[level, head : head + 1, chunk].astype(bf16))
            return jnp.concatenate(rows, axis=0)

        return for_head

    def lse_of(lanes):
        return jnp.concatenate([lse_s[pair, :, lanes] for pair in range(PAIRS)], axis=0)

    def combine(step, carry):
        chunk = pl.ds(pl.multiple_of(step * CHUNK, CHUNK), CHUNK)
        wins = windows(step)
        logs = [lse_of(chunk)]
        for slot in range(3):
            parts = jnp.concatenate(split3(lse_of(wins[slot])), axis=0)
            made = nn(parts, member[slot * TILE : (slot + 1) * TILE, chunk])
            logs.append(made[0:8] + made[8:16] + made[16:24] + (slot + 1) * math.log(2.0))
        top = lse_of(wins[3])
        parts = []
        for slot in range(4):
            inside = (top_lane >= edges[slot]) & (top_lane < edges[slot + 1])
            parts += list(split3(jnp.where(inside, top, 0.0)))
        made = nn(jnp.concatenate(parts, axis=0), member[384:512, chunk])
        for slot in range(4):
            b = slot * 24
            logs.append(made[b : b + 8] + made[b + 8 : b + 16] + made[b + 16 : b + 24] + (slot + 4) * math.log(2.0))
        peak = functools.reduce(jnp.maximum, logs)
        den = functools.reduce(jnp.add, [jnp.exp(one - peak) for one in logs])
        lse = peak + jnp.log(den)
        for level in range(LEVELS):
            share[level, :, chunk] = jnp.exp(logs[level] - lse)
        for_head = per_level(step, chunk)
        for head in range(HEADS):
            at = slice(head * HEAD, (head + 1) * HEAD)
            coarse = jnp.concatenate([out_t[at, win] for win in wins], axis=1)
            made = nn(coarse, for_head(head))
            made = made + share[0, head : head + 1, chunk] * out_t[at, chunk].astype(f32)
            mix_t[at, chunk] = made.astype(bf16)
        return carry

    lax.fori_loop(0, SHORT // CHUNK, combine, 0)
    pump((3, 4), (4, 3))

    bias_mix, gain_two = r.param[2:3, :], r.param[3:4, :]
    shift_two, bias_out = r.param[4:5, :], r.param[5:6, :]
    w_mix = rows_of(wi, 4 * D, D)
    resid[...] = tn(mix_t[...], w_mix)

    def second_norm(step, carry):
        at = pl.ds(pl.multiple_of(step * CHUNK, CHUNK), CHUNK)
        mid = tok[at, :].astype(f32) + resid[at, :] + bias_mix
        resid[at, :] = mid
        normed, _ = normalize(mid)
        n_two[at, :] = (normed * gain_two + shift_two).astype(bf16)
        return carry

    lax.fori_loop(0, SHORT // CHUNK, second_norm, 0)
    pump((4, 4))

    hid, g_pre = grads.at[0:SHORT, 0:D], grads.at[0:SHORT, D : 2 * D]
    acc_out[...] = jnp.zeros_like(acc_out)
    acc_two[...] = jnp.zeros_like(acc_two)

    def total_i(part):
        return Total(di, lanes_at(part * 512, 512), part, p, r.si[0], r.si[1:])

    def total_o(part):
        return TotalRows(do, part, p, r.so[0], r.so[1:7])

    def onward(total, *steps):
        if fast:
            for part, step in steps:
                if isinstance(part, int):
                    total(part).advance(step)
                else:
                    pl.when(part >= 0)(lambda: total(part).advance(step))

    def feed(part, carry):
        lanes = pl.ds(pl.multiple_of(part * 512, 512), 512)
        w_in = wi[:, :, :, :, :, lanes].reshape(512, 512)
        w_out = wo[part].reshape(512, 512)
        b_in = r.bias_in[:, lanes]
        sums = jnp.zeros((1, 512), f32)
        for step in range(FEED_STEPS):
            at = pl.ds(step * (SHORT // FEED_STEPS), SHORT // FEED_STEPS)
            act, slope = gelu_both(nn(n_two[at, :], w_in) + b_in)
            act = act.astype(bf16)
            hid[at, :] = act
            back = (nt(cot[at, :], w_out) * slope).astype(bf16)
            g_pre[at, :] = back
            acc_out[at, :] += nn(act, w_out)
            acc_two[at, :] += nt(back, w_in)
            sums = sums + jnp.sum(back.astype(f32), axis=0, keepdims=True)
            if step == 0:
                onward(total_i, (part - 3, 3), (part - 2, 2), (part - 1, 1))
                onward(total_o, (part - 3, 3), (part - 2, 2), (part - 1, 1))
        r.lanes_in[0:1, lanes] = sums
        di[:, :, :, :, :, lanes] = tn(n_two[...], g_pre[...]).astype(bf16).reshape(4, 2, 2, 2, 16, 512)
        do[part] = tn(hid[...], cot[...]).astype(bf16).reshape(2, 2, 2, 64, 512)
        if fast:
            onward(total_i, (part, 0))
            onward(total_o, (part, 0))
        return carry

    lax.fori_loop(0, 4, feed, 0)

    def middle(step, carry):
        at = pl.ds(pl.multiple_of(step * CHUNK, CHUNK), CHUNK)
        mid = resid[at, :]
        n_two[at, :] = (mid + acc_out[at, :] + bias_out).astype(bf16)
        normed, inverse = normalize(mid)
        g_two = acc_two[at, :]
        c = cot[at, :].astype(f32)
        g_mid = c + normalize_back(g_two * gain_two, normed, inverse)
        resid[at, :] = g_mid
        low = g_mid.astype(bf16)
        g_att[at, :] = low
        vec_b[0:1, :] += jnp.sum(low.astype(f32), axis=0, keepdims=True)
        vec_b[1:2, :] += jnp.sum(g_two * normed, axis=0, keepdims=True)
        vec_b[2:3, :] += jnp.sum(g_two, axis=0, keepdims=True)
        vec_b[3:4, :] += jnp.sum(c, axis=0, keepdims=True)
        return carry

    lax.fori_loop(0, SHORT // CHUNK, middle, 0)
    out_copy = pltpu.make_async_copy(n_two, r.out, r.out_sem.at[0])
    out_copy.start()
    onward(total_i, (1, 3), (2, 2), (3, 1))
    onward(total_o, (1, 3), (2, 2), (3, 1))
    g_mix[...] = nt(g_att[...], w_mix).astype(bf16)

    def inner_sums(step, carry):
        at = pl.ds(pl.multiple_of(step * 512, 512), 512)
        turned = nt(w_mix, g_att[at, :]).astype(bf16).astype(f32) * mix_t[:, at].astype(f32)
        inner_s[:, at] = jnp.concatenate(
            [jnp.sum(turned[h * HEAD : (h + 1) * HEAD], axis=0, keepdims=True) for h in range(HEADS)], axis=0
        )
        return carry

    lax.fori_loop(0, SHORT // 512, inner_sums, 0)

    made = nn(mix_t[...], g_att[...])
    di[:, :, :, :, :, 4 * D :] = made.astype(bf16).reshape(4, 2, 2, 2, 16, D)
    onward(total_i, (4, 0))


    def keep_h(lanes, values):
        for pair in range(PAIRS):
            total_h[pair, :, lanes] = values[2 * pair : 2 * pair + 2]

    def sums_of(level, source, members):
        both = jnp.concatenate(split2(share[level, :, source] * inner_s[:, source]), axis=0)
        made = nt(both, members)
        return made[0:8] + made[8:16]

    tops_acc[0:TILE, :] = jnp.zeros((TILE, D), f32)

    def lift(step, carry):
        pl.when(step == 2)(lambda: onward(total_i, (2, 3)))
        pl.when(step == 3)(lambda: onward(total_o, (2, 3)))
        chunk = pl.ds(pl.multiple_of(step * CHUNK, CHUNK), CHUNK)
        to = chunk_rows(step)
        members = chunk_members(chunk)
        made = []
        for pair in range(PAIRS):
            weighted = [
                one * share[1 + k, head : head + 1, chunk].astype(bf16)
                for head in (2 * pair, 2 * pair + 1)
                for k, one in enumerate(members)
            ]
            tokens = g_num[chunk, pair * TILE : (pair + 1) * TILE]
            made.append(by_head(nn(jnp.concatenate(weighted, axis=0), tokens)))
        made = jnp.concatenate(made, axis=1)
        for level, (low, high) in enumerate(((0, 128), (128, 192), (192, 224))):
            g_num[to[level], :] = (made[low:high] * 0.5 ** (level + 1)).astype(bf16)
        tops_acc[0:TILE, :] += made[224:352]
        keep_h(chunk, share[0, :, chunk] * inner_s[:, chunk])
        keep_h(to[0], sums_of(1, chunk, member[0:128, chunk]))
        return carry

    lax.fori_loop(0, SHORT // CHUNK, lift, 0)
    g_num[FIRST[4] : STACK, :] = (tops_acc[0:TILE, :] * steps_down).astype(bf16)

    def lift_two(step, carry):
        source = pl.ds(pl.multiple_of(step * 512, 512), 512)
        rows = pl.ds(pl.multiple_of(FIRST[2] + step * TILE, TILE), TILE)
        keep_h(rows, sums_of(2, source, member[128:256, source]))
        return carry

    lax.fori_loop(0, 2, lift_two, 0)
    every = pl.ds(0, SHORT)
    keep_h(pl.ds(FIRST[3], TILE), sums_of(3, every, member[256:384, :]))
    tops = [sums_of(4 + slot, every, member[384:512, :]) for slot in range(4)]
    keep_h(
        pl.ds(FIRST[4], TILE),
        jnp.where(top_lane < 64, tops[0], jnp.where(top_lane < 96, tops[1], jnp.where(top_lane < 112, tops[2], tops[3]))),
    )
    onward(total_i, (3, 2))
    onward(total_o, (3, 2))
    for pair in range(PAIRS):
        weight[pair, :, 0:SHORT] = share[0, 2 * pair : 2 * pair + 2]
    weight[:, :, SHORT:STACK] = jnp.ones((PAIRS, 2, SHORT), f32)

    def tile_backward(tile, pair, scale):
        rows = lanes_at(tile * TILE, TILE)
        at = lambda slot: (rows, lanes_at(pair * GROUP + slot * TILE, TILE))
        num = g_num[rows, lanes_at(pair * TILE, TILE)]
        got = nt(two_heads(stack[at(2)]), num)
        got = jnp.concatenate([squeeze(got[:TILE]), squeeze(got[TILE:])], axis=1)
        both = lambda ref: jnp.concatenate([ref[pair, 0:1, rows], ref[pair, 1:2, rows]], axis=1)
        low = probs[tile, :, lanes_at(pair * 2 * TILE, 2 * TILE)].astype(f32)
        times = both(weight)
        wide_s = widen((low * (got * times - both(total_h))).astype(bf16))
        wide_p = widen((low * times).astype(bf16))
        tall = lambda wide: jnp.concatenate([wide[:, :TILE], wide[:, TILE:]], axis=0)
        grads[at(1)] = (by_head(nn(tall(wide_s), stack[at(0)])) * scale).astype(bf16)
        grads[at(2)] = by_head(nn(tall(wide_p), num)).astype(bf16)
        made = nn(stack[at(1)].T, wide_s)
        made = jnp.concatenate([made[:HEAD, :TILE], made[HEAD:, TILE:]], axis=0).astype(bf16).T
        grads[at(0)] = (made.astype(f32) * (scale * 0.125)).astype(bf16)

    for pair in range(PAIRS):
        tile_backward(15, pair, steps_down)
    onward(total_i, (4, 1))
    back_s, back_r = r.back_s, r.back_r
    spans = [(slice(k * GROUP + TILE, (k + 1) * GROUP), slice(k * 2 * TILE, (k + 1) * 2 * TILE)) for k in range(PAIRS)]
    tall = jnp.concatenate([grads[2016:2048, theirs] for theirs, _ in spans], axis=1).astype(f32)
    nothing = jnp.zeros((8, 2 * D), f32)
    back_s[0] = tall[0:16].astype(bf16)
    back_s[1] = jnp.concatenate([tall[16:24], nothing], axis=0).astype(bf16)
    back_s[2] = jnp.concatenate([tall[24:32], nothing], axis=0).astype(bf16)
    back_out = [
        remote(back_s.at[0], back_r.at[0], r.far_sem.at[3], r.far_sem.at[2], (p.dp, other)),
        remote(back_s.at[1], back_r.at[1 + side], r.far_sem.at[3], r.far_sem.at[2], (p.dp, pairs_at)),
        remote(back_s.at[2], back_r.at[1 + side], r.far_sem.at[3], r.far_sem.at[2], (p.dp, pairs_at + 1)),
    ]
    for copy in back_out:
        copy.start()

    def total_a(part):
        return Total(da, lanes_at(part * GROUP, GROUP), part, p, r.sa[0], r.sa[1:])

    def far_grads():
        arrived(back_r, r.far_sem.at[2], p.by_core)
        gone(back_r, r.far_sem.at[3], p.by_core)
        two = (back_r[1].astype(f32) + back_r[2].astype(f32)).astype(bf16)
        for theirs, mine in spans:
            grads[2016:2032, theirs] = back_r[0, :, mine]
            grads[2032:2048, theirs] = two[:, mine]

    def send_rows():
        onward(total_o, (3, 3))
        for k, z in enumerate(p.zs):
            remote(do.at[z, p.y, p.x, p.c], r.so[6].at[k], r.so[7].at[1], r.so[7].at[0], p.by_z[k]).start()

    def finish_feed():
        for part in range(5):
            total_i(part).finish(r.keep_i)
        arrived(r.so[6], r.so[7].at[0], p.by_core)
        total = do[p.z, p.y, p.x, p.c].astype(f32)
        r.keep_o[...] = functools.reduce(jnp.add, [r.so[6][k].astype(f32) for k in range(3)], total)
        gone(r.so[6], r.so[7].at[1], p.by_core)
        for part in range(4):
            total_o(part).settle()
        for copy in kept[:2]:
            copy.start()

    if fast:
        kept = [
            pltpu.make_async_copy(src, dst, r.keep_sem.at[k])
            for k, (src, dst) in enumerate(
                ((r.keep_i, r.o_i), (r.keep_o, r.o_o), (r.keep_a, r.o_a), (r.keep_v, r.o_v))
            )
        ]

        early = TotalVectors(r.vec_b, p, r.v_sem.at[0], r.got_b, r.mid_b, r.far_b)
        late = TotalVectors(r.vec_s, p, r.v_sem.at[1], r.got_a, r.mid_a, r.far_a)
    vec_b[4:8, :] = jnp.concatenate([r.lanes_in[0:1, k * 512 : (k + 1) * 512] for k in range(4)], axis=0)

    def early_done():
        r.done_b[...] = early.finish()
        long = jnp.concatenate([r.done_b[4 + k : 5 + k] for k in range(4)], axis=1)
        long = pltpu.roll(jnp.concatenate([long] * 8, axis=0), 2048 - HEAD * whose, axis=1)[:, 0:SMALL]
        r.keep_v[8:16] = long

    def pair_backward(pair, carry):
        def near_back(group, carry):
            for one in range(TOGETHER):
                tile = group * TOGETHER + one
                tile_backward(tile, pair, tile_scale(tile))
            return carry

        lax.fori_loop(0, 15 // TOGETHER, near_back, 0)
        pl.when(pair == 0)(far_grads)
        if fast:
            pl.when(pair == 0)(lambda: onward(total_i, (3, 3), (4, 2)))
            pl.when(pair == 0)(send_rows)
            pl.when(pair == 1)(lambda: onward(total_i, (4, 3)))
            pl.when(pair == 0)(early.begin)
            pl.when(pair == 1)(early.second)
            pl.when(pair == 3)(finish_feed)
            pl.when(pair == 3)(early_done)
        onward(total_a, (pair - 3, 3), (pair - 2, 2), (pair - 1, 1))

        lanes = lanes_at(pair * GROUP, GROUP)

        def level_sums(step, carry):
            chunk = pl.ds(pl.multiple_of(step * CHUNK, CHUNK), CHUNK)
            top = grads[FIRST[4] : STACK, lanes]
            coarse = [grads[rows, lanes] for rows in chunk_rows(step)] + [top[0:32], top]
            made = nn(spread[chunk, :], jnp.concatenate(coarse, axis=0))
            stack[chunk, lanes] = (made + grads[chunk, lanes].astype(f32)).astype(bf16)
            return carry

        lax.fori_loop(0, SHORT // CHUNK, level_sums, 0)
        da[:, :, :, :, :, lanes] = tn(n_one[...], stack[0:SHORT, lanes]).astype(bf16).reshape(4, 2, 2, 2, 16, GROUP)
        onward(total_a, (pair, 0))
        return carry

    lax.fori_loop(0, PAIRS, pair_backward, 0)

    acc_two[...] = nt(stack[0:SHORT, :], wa[:, :, :, :, :, SMALL : SMALL + WIDTH].reshape(D, WIDTH))
    onward(total_a, (3, 1), (1, 3), (2, 2))

    def first_back(step, carry):
        pl.when(step == 2)(lambda: onward(total_a, (3, 2), (2, 3)))
        chunk = pl.ds(pl.multiple_of(step * CHUNK, CHUNK), CHUNK)
        g_one = acc_two[chunk, :]
        normed, inverse = normalize(tok[chunk, :].astype(f32))
        vec_a[0:1, :] += jnp.sum(g_one * normed, axis=0, keepdims=True)
        vec_a[1:2, :] += jnp.sum(g_one, axis=0, keepdims=True)
        g_att[chunk, :] = (resid[chunk, :] + normalize_back(g_one * gain_one, normed, inverse)).astype(bf16)
        return carry

    lax.fori_loop(0, SHORT // CHUNK, first_back, 0)
    tok_copy = pltpu.make_async_copy(g_att, r.g_tok, r.out_sem.at[1])
    tok_copy.start()
    if fast:
        for row in range(2):
            for part in range(4):
                at = row * 4 + part
                r.vec_s[at : at + 1, :] = vec_a[row : row + 1, part * TILE : (part + 1) * TILE]
        late.begin()
        onward(total_a, (3, 3))
        late.second()
        for part in range(3):
            total_a(part).finish(r.keep_a)
        last = late.finish()
        rows = [jnp.concatenate([last[at + part : at + part + 1] for part in range(4)], axis=1) for at in (0, 4)]
        short = jnp.concatenate(rows + [r.done_b[0:4], jnp.zeros((2, D), f32)], axis=0)
        short = pltpu.roll(short, 512 - 16 * whose, axis=1)[:, 0:SMALL]
        r.keep_v[0:8] = short
        kept[3].start()
        total_a(3).finish(r.keep_a)
        kept[2].start()
        for copy in kept:
            copy.wait()
    else:
        r.o_v[0:8] = vec_a[...]
        r.o_v[8:16] = vec_b[...]
    out_copy.wait()
    tok_copy.wait()


def final_kernel(*refs):
    big, small, outs, (kept, vmem_a, vmem_i, vmem_o, vmem_v, sem) = refs[:2], refs[2:6], refs[6:21], refs[21:]
    parts = [pl.ds(k * CHUNK, CHUNK) for k in range(SHORT // CHUNK)]
    count = iter(range(24))
    copy = lambda src, dst: pltpu.make_async_copy(src, dst, sem.at[next(count)])
    into = [copy(ref.at[at], kept.at[slot, at]) for slot, ref in enumerate(big) for at in parts]
    onto = [copy(kept.at[slot, at], outs[slot].at[at]) for slot in range(2) for at in parts]
    rest = [copy(src, dst) for src, dst in zip(small, (vmem_a, vmem_i, vmem_o, vmem_v))]
    for one in into + rest:
        one.start()
    for one, then in zip(into, onto):
        one.wait()
        then.start()
    for one in rest:
        one.wait()
    for slot, at in ((2, 0), (3, 1), (8, 2), (9, 3), (10, 4), (14, 5)):
        outs[slot][...] = vmem_v[at : at + 1, 0:16].reshape(16)
    outs[12][...] = vmem_v[8:9, 0:HEAD].reshape(HEAD)
    for k in range(3):
        for pair in range(PAIRS):
            at = pair * GROUP + k * TILE
            outs[4 + k][:, pair * TILE : (pair + 1) * TILE] = vmem_a[:, at : at + TILE]
    outs[7][...] = vmem_i[:, 4 * D :]
    outs[11][...] = vmem_i[:, : 4 * D]
    outs[13][...] = vmem_o[...]
    for one in onto:
        one.wait()


def scratch_list(fast):
    V, S = pltpu.VMEM, pltpu.SemaphoreType.DMA
    made = dict(
        tok=V((SHORT, D), bf16),
        cot=V((SHORT, D), bf16),
        member=V((D, SHORT), bf16),
        spread=V((SHORT, GROUP), bf16),
        head_m=V((2 * TILE, TILE), bf16),
        group_m=V((TILE, 2 * TILE), bf16),
        bias=V((3, 32, 2 * TILE), f32),
        in_sem=S((17,)),
        out_sem=S((2,)),
        stack=V((STACK, WIDTH), bf16),
        probs=V((16, 32, HEADS * TILE), bf16),
        out_t=V((D, STACK), bf16),
        mix_t=V((D, SHORT), bf16),
        lse_s=V((PAIRS, 2, STACK), f32),
        share=V((LEVELS, HEADS, SHORT), f32),
        inner_s=V((HEADS, SHORT), f32),
        total_h=V((PAIRS, 2, STACK), f32),
        resid=V((SHORT, D), f32),
        n_one=V((SHORT, D), bf16),
        n_two=V((SHORT, D), bf16),
        acc_out=V((SHORT, D), f32),
        acc_two=V((SHORT, D), f32),
        grads=V((STACK, WIDTH), bf16),
        g_att=V((SHORT, D), bf16),
        weight=V((PAIRS, 2, STACK), f32),
        g_num=V((STACK, D), bf16),
        vec_a=V((8, D), f32),
        vec_b=V((8, D), f32),
        param=V((16, D), f32),
        bias_in=V((1, 4 * D), f32),
        lanes_in=V((8, 4 * D), f32),
        far_s=V((2, 16, 2 * D), bf16),
        far_r=V((3, 16, 2 * D), bf16),
        far_sem=S((4,)),
        back_s=V((3, 16, 2 * D), bf16),
        back_r=V((3, 16, 2 * D), bf16),
    )
    if fast:

        def sums(parts, wide):
            shape = lambda *dims: V((parts,) + dims + (16, wide), bf16)
            return [S((parts, 7)), shape(4, 2, 2), shape(2, 2), shape(2, 2), shape(2), shape(2), shape(3)]

        rows = lambda *dims: V((4,) + dims + (D,), bf16)
        made.update(
            wa=V(SLOTS + (16, WIDTH + SMALL), bf16),
            wi=V(SLOTS + (16, 5 * D), bf16),
            wo=V(SLOTS + (64, D), bf16),
            da=V(SLOTS + (16, WIDTH), bf16),
            di=V(SLOTS + (16, 5 * D), bf16),
            do=V(SLOTS + (64, D), bf16),
            g_sem=S((5, 7)),
            si=sums(5, D),
            so=[S((4, 5)), rows(2, 2, 64), rows(2, 32), rows(2, 32), rows(32), rows(32), V((3, 64, D), bf16), S((2,))],
            sa=sums(4, GROUP),
            v_sem=S((2, 4)),
            vec_s=V((8, TILE), f32),
            got_a=V((7, 8, TILE), f32),
            mid_a=V((8, TILE), f32),
            far_a=V((3, 8, TILE), f32),
            got_b=V((7, 8, D), f32),
            mid_b=V((8, D), f32),
            far_b=V((3, 8, D), f32),
            done_b=V((8, D), f32),
            vec_in=[V((16,), bf16)] * 6 + [V((HEAD,), bf16)],
            keep_a=V((16, WIDTH), f32),
            keep_i=V((16, 5 * D), f32),
            keep_o=V((HEAD, D), f32),
            keep_v=V((16, SMALL), f32),
            keep_sem=S((4,)),
        )
    return made


def constants():
    member = member_matrix()
    as_low = lambda values: jnp.asarray(values.astype(np.float32), bf16)
    return dict(
        member_h=as_low(member),
        spread_h=as_low(np.ascontiguousarray(spread_matrix())),
        head_h=as_low(head_mask()),
        group_h=as_low(group_mask()),
        bias_h=jnp.asarray(block_bias()),
    )


def run_layer(fast, hbm, vmem):
    sd = jax.ShapeDtypeStruct
    const = constants()
    hbm = dict(hbm, **const)
    here, there = pl.BlockSpec(memory_space=pltpu.VMEM), pl.BlockSpec(memory_space=pl.ANY)
    slots = () if fast else SLOTS
    kind = f32 if fast else bf16
    outs = dict(
        out=sd((SHORT, D), bf16),
        g_tok=sd((SHORT, D), bf16),
        o_a=sd(slots + (16, WIDTH), kind),
        o_i=sd(slots + (16, 5 * D), kind),
        o_o=sd(slots + (64, D), kind),
        o_v=sd((16, SMALL if fast else D), f32),
    )
    row_length = hbm.pop("row_length")
    operands = dict(hbm, row_length=row_length, **vmem)
    flat = lambda parts: [one for part in parts.values() for one in (part if isinstance(part, list) else [part])]
    specs = [there] * len(flat(hbm)) + [pl.BlockSpec(memory_space=pltpu.SMEM)] + [here] * len(vmem)
    hbm_outs = len(outs) if fast else 2
    return pl.pallas_call(
        functools.partial(layer_kernel, fast, dict(operands, **outs)),
        out_shape=list(outs.values()),
        in_specs=specs,
        out_specs=[there] * hbm_outs + [here] * (len(outs) - hbm_outs),
        scratch_shapes=flat(scratch_list(fast)),
        compiler_params=pltpu.CompilerParams(
            collective_id=0, has_side_effects=True, vmem_limit_bytes=63 * 2**20
        ),
    )(*flat(operands))


def finish_outputs(*parts):
    sd = jax.ShapeDtypeStruct
    vmem, hbm = pl.BlockSpec(memory_space=pltpu.VMEM), pl.BlockSpec(memory_space=pl.ANY)
    own, square = sd((16,), f32), sd((16, D), f32)
    tokens = sd((SHORT, D), bf16)
    outs = [tokens, tokens, own, own, square, square, square, square, own, own, own]
    outs += [sd((16, 4 * D), f32), sd((HEAD,), f32), sd((HEAD, D), f32), own]
    return pl.pallas_call(
        final_kernel,
        out_shape=outs,
        in_specs=[hbm] * 6,
        out_specs=[hbm] * 2 + [vmem] * 13,
        scratch_shapes=[
            pltpu.VMEM((2, SHORT, D), bf16),
            pltpu.VMEM((16, WIDTH), f32),
            pltpu.VMEM((16, 5 * D), f32),
            pltpu.VMEM((HEAD, D), f32),
            pltpu.VMEM((16, SMALL), f32),
            pltpu.SemaphoreType.DMA((20,)),
        ],
    )(*parts)


def on_device(
    tokens, cotangent, row_length, first_gain, first_shift, query_weight, key_weight, value_weight,
    mixer_weight, mixer_bias, second_gain, second_shift, inner_weight, inner_bias, outer_weight, outer_bias,
):
    n_dp, n_fsdp = lax.axis_size("dp"), lax.axis_size("fsdp")
    fast = (n_dp, n_fsdp) == (8, 4) and query_weight.shape[0] == 16
    vectors = (first_gain, first_shift, mixer_bias, second_gain, second_shift, outer_bias)
    first = dict(tok_h=tokens, cot_h=cotangent, row_length=row_length)
    if fast:
        first.update(
            wq_s=query_weight, wk_s=key_weight, wv_s=value_weight, wm_s=mixer_weight, wi_s=inner_weight, wo_s=outer_weight,
            vectors=list(vectors) + [inner_bias],
        )
        return finish_outputs(*run_layer(True, first, dict()))
    whole = lambda part: lax.all_gather(part, AXES, axis=0, tiled=True)
    three = jnp.stack([part.reshape(-1, PAIRS, TILE) for part in (query_weight, key_weight, value_weight)], axis=2)
    wide = whole(three.reshape(-1, WIDTH))
    eights = [whole(vector).reshape(4, 8, 16) for vector in vectors]
    small = jnp.zeros((4, 8, 16, SMALL), bf16)
    for row, vector in enumerate(eights):
        for at in range(8):
            small = small.at[:, at, row, 16 * at : 16 * at + 16].set(vector[:, at])
    pairs = whole(inner_bias).reshape(4, 4, 2, 64)
    pairs_at = small.reshape(4, 4, 2, 16, SMALL)
    for at in range(2):
        pairs_at = pairs_at.at[:, :, at, 6, 64 * at : 64 * at + 64].set(pairs[:, :, at])
    wide = jnp.concatenate((pairs_at.reshape(4, 8, 16, SMALL), wide.reshape(4, 8, 16, WIDTH)), axis=-1)
    weights = dict(
        wa=wide.reshape(SLOTS + (16, WIDTH + SMALL)),
        wi=whole(jnp.concatenate((inner_weight, mixer_weight), axis=1)).reshape(SLOTS + (16, 5 * D)),
        wo=whole(outer_weight).reshape(SLOTS + (64, D)),
    )
    out, g_tok, d_a, d_i, d_o, o_v = run_layer(False, first, weights)
    owned = lambda part: lax.psum_scatter(part, AXES, scatter_dimension=0, tiled=True)
    g_a = owned(d_a.astype(f32).reshape(D, WIDTH))
    g_q, g_k, g_v = (g_a.reshape(-1, PAIRS, 3, TILE)[:, :, k].reshape(-1, D) for k in range(3))
    g_i = owned(d_i.astype(f32).reshape(D, 5 * D))
    g_i, g_m = g_i[:, : 4 * D], g_i[:, 4 * D :]
    g_o = owned(d_o.astype(f32).reshape(4 * D, D))
    six = [owned(o_v[k]) for k in (0, 1, 8, 9, 10, 11)]
    g_bias_in = owned(o_v[12:16].reshape(-1))
    return (
        out, g_tok, six[0], six[1], g_q, g_k, g_v, g_m, six[2], six[3], six[4], g_i, g_bias_in, g_o, six[5],
    )


def solution(mesh):
    rows, flat, both = P(AXES, None), P(AXES), P("dp")
    in_specs = (rows, rows, both, flat, flat, rows, rows, rows, rows, flat, flat, flat, rows, flat, rows, flat)
    out_specs = (rows, rows, flat, flat, rows, rows, rows, rows, flat, flat, flat, rows, flat, rows, flat)
    return jax.shard_map(on_device, mesh=mesh, in_specs=in_specs, out_specs=out_specs, check_vma=False)
```

```python
import functools
import math
import types

import jax
import jax.numpy as jnp
import numpy as np
from jax import lax
from jax.experimental import pallas as pl
from jax.experimental.pallas import tpu as pltpu
from jax.sharding import PartitionSpec as P

D = 512
HEADS = 8
HEAD = 64
BLOCK = 16
SHORT = 1024
LEVELS = 8
TILE = 128
TOGETHER = 5
CHUNK = 256
STACK = 2 * SHORT
WIDTH = 3 * D
SMALL = 128
GROUP = 3 * TILE
PAIRS = HEADS // 2
FEED_STEPS = 2
AXES = ("dp", "fsdp")
MESH = pl.DeviceIdType.MESH
SLOTS = (4, 2, 2, 2)

norm_eps = 1e-05
far_off = -1e30
f32 = jnp.float32
bf16 = jnp.bfloat16

FIRST = [STACK - (STACK >> level) for level in range(LEVELS + 1)]
LOW_TOP = 4


def member_matrix():
    token = np.arange(SHORT)
    rows = []
    for level, span in ((1, 256), (2, 512), (3, 1024)):
        rows.append((token[None] % span) >> level == np.arange(TILE)[:, None])
    for level in range(LOW_TOP, LEVELS):
        rows.append(token[None] >> level == np.arange(SHORT >> level)[:, None])
    rows.append(np.zeros((8, SHORT), bool))
    return np.concatenate(rows).astype(np.float32)


def spread_matrix():
    member = member_matrix()
    near = np.concatenate([member[0:128, :CHUNK], member[128:192, :CHUNK], member[256:288, :CHUNK], np.zeros((32, CHUNK))])
    return np.concatenate([np.tile(near, (1, SHORT // CHUNK)), member[384:]]).T.astype(np.float32)


def block_bias():
    key = np.arange(32)[:, None]
    query = np.arange(2 * TILE)[None]
    across = (key < BLOCK) != (query % 32 < BLOCK)
    last = np.where(query % TILE >= 96, ~across, across)
    kinds = [np.ones_like(across), across, last]
    return np.stack([np.where(kind, 0.0, far_off) for kind in kinds]).astype(np.float32)


def head_mask():
    lane = np.arange(TILE)[None]
    side = np.arange(2 * TILE)[:, None] // TILE
    return (lane // HEAD == side).astype(np.float32)


def group_mask():
    key = np.arange(TILE)[:, None]
    query = np.arange(2 * TILE)[None]
    return (key // 32 == query % TILE // 32).astype(np.float32)


def top_level_of():
    index = np.arange(TILE)
    return np.minimum(LOW_TOP + (index >= 64) * 1 + (index >= 96) * 1 + (index >= 112) * 1, 7)


def nn(a, b):
    return lax.dot_general(a, b, (((1,), (0,)), ((), ())), preferred_element_type=f32)


def nt(a, b):
    return lax.dot_general(a, b, (((1,), (1,)), ((), ())), preferred_element_type=f32)


def tn(a, b):
    return lax.dot_general(a, b, (((0,), (0,)), ((), ())), preferred_element_type=f32)


def normalize(values):
    center = values - jnp.mean(values, axis=-1, keepdims=True)
    inverse = lax.rsqrt(jnp.mean(center * center, axis=-1, keepdims=True) + norm_eps)
    return center * inverse, inverse


def normalize_back(grad_normed, normed, inverse):
    return inverse * (
        grad_normed
        - jnp.mean(grad_normed, axis=-1, keepdims=True)
        - normed * jnp.mean(grad_normed * normed, axis=-1, keepdims=True)
    )


def gelu_both(v):
    mag = jnp.abs(v) * (0.5**0.5)
    t = 1.0 / (1.0 + 0.3275911 * mag)
    gauss = jnp.exp(-0.5 * v * v)
    poly = t * (
        0.254829592
        + t * (-0.284496736 + t * (1.421413741 + t * (-1.453152027 + t * 1.061405429)))
    )
    tail = 0.5 * poly * gauss
    cdf = jnp.where(v < 0, tail, 1.0 - tail)
    return v * cdf, cdf + v * gauss * ((2 * math.pi) ** -0.5)


def split3(values):
    one = values.astype(bf16)
    rest = values - one.astype(f32)
    two = rest.astype(bf16)
    return one, two, (rest - two.astype(f32)).astype(bf16)


def split2(values):
    one = values.astype(bf16)
    return one, (values - one.astype(f32)).astype(bf16)


class Place:
    def __init__(self):
        self.dp = lax.axis_index("dp")
        self.fs = lax.axis_index("fsdp")
        self.z, self.y = self.dp // 2, self.dp % 2
        self.x, self.c = self.fs // 2, self.fs % 2
        self.oy, self.ox, self.oc = 1 - self.y, 1 - self.x, 1 - self.c
        self.zs = [lax.rem(self.z + step, 4) for step in (1, 2, 3)]
        self.by_core = (self.dp, self.x * 2 + self.oc)
        self.by_x = (self.dp, self.ox * 2 + self.c)
        self.by_y = (self.z * 2 + self.oy, self.fs)
        self.by_z = [(z * 2 + self.y, self.fs) for z in self.zs]
        ys, xs, cs = (self.y, self.oy), (self.x, self.ox), (self.c, self.oc)
        self.plane = [(self.z * 2 + ys[k // 4], xs[k // 2 % 2] * 2 + cs[k % 2]) for k in range(1, 8)]


def remote(src, dst, send, recv, device):
    return pltpu.make_async_remote_copy(
        src_ref=src, dst_ref=dst, send_sem=send, recv_sem=recv, device_id=device, device_id_type=MESH
    )


def arrived(ref, sem, device):
    remote(ref, ref, sem, sem, device).wait_recv()


def gone(ref, sem, device):
    remote(ref, ref, sem, sem, device).wait_send()


class Gather:
    def __init__(self, ref, lanes, p, sems):
        self.at = lambda z, y, x: ref.at[z, y, x, p.c, :, lanes]
        self.p, self.sems = p, sems

    def advance(self, step):
        p, at, sems = self.p, self.at, self.sems
        low, high, both, full = pl.ds(0, 2), pl.ds(2, 2), pl.ds(0, 2), pl.ds(0, 4)
        if step:
            ref = (at(pl.ds(0, 3), p.y, p.x), at(full, p.y, p.x), at(full, both, p.x), at(full, both, both))[step - 1]
            arrived(ref, sems.at[step - 1], p.by_core)
        if step == 4:
            gone(at(pl.ds(0, 3), p.y, p.x), sems.at[4], p.by_core)
            gone(at(pl.ds(0, 3), both, both), sems.at[5], p.by_core)
            gone(at(full, both, both), sems.at[6], p.by_core)
            return
        if step == 0:
            parts = [(at(p.z, p.y, p.x), device) for device in p.by_z]
        elif step == 1:
            parts = [(at(low, p.y, p.x), p.by_x), (at(high, p.y, p.x), p.by_y)]
        elif step == 2:
            parts = [(at(low, p.y, both), p.by_y), (at(high, both, p.x), p.by_x)]
        else:
            parts = [(at(full, both, both), p.by_core)]
        for part, device in parts:
            remote(part, part, sems.at[(4, 5, 5, 6)[step]], sems.at[step], device).start()


class Total:
    def __init__(self, ref, lanes, part, p, sems, bufs):
        self.ref, self.lanes, self.part, self.p, self.bufs = ref, lanes, part, p, bufs
        self.sems, self.sent = sems[0].at[part], sems[1]

    def add(self, index, buf):
        at = index + (self.p.c, slice(None), self.lanes)
        self.ref[at] = self.ref[at] + buf

    def advance(self, step):
        p, part, sems = self.p, self.part, self.sems
        from_core, one_a, one_b, two_a, two_b, far = self.bufs
        at = lambda z, y, x, c: self.ref.at[z, y, x, c, :, self.lanes]
        low, high, both, full, every = pl.ds(0, 2), pl.ds(2, 2), pl.ds(0, 2), pl.ds(0, 4), slice(None)
        if step:
            ref = (from_core.at[part], from_core.at[part, both], from_core.at[part, 0])[step - 1]
            arrived(ref, sems.at[step - 1], p.by_core)
        if step == 0:
            sends = [(at(full, both, both, p.oc), from_core, p.by_core)]
        elif step == 1:
            for z in range(4):
                self.add((z, every, every), from_core[part, z])
            sends = [(at(low, p.oy, both, p.c), one_a, p.by_y), (at(high, both, p.ox, p.c), one_b, p.by_x)]
        elif step == 2:
            for z in range(2):
                self.add((z, p.y, every), one_a[part, z])
                self.add((2 + z, every, p.x), one_b[part, z])
            sends = [(at(low, p.y, p.ox, p.c), two_a, p.by_x), (at(high, p.oy, p.x, p.c), two_b, p.by_y)]
        else:
            for z in range(2):
                self.add((z, p.y, p.x), two_a[part, z])
                self.add((2 + z, p.y, p.x), two_b[part, z])
            for k, z in enumerate(p.zs):
                remote(at(z, p.y, p.x, p.c), far.at[part, k], self.sent.at[2], sems.at[3], p.by_z[k]).start()
            return
        for src, buf, device in sends:
            remote(src, buf.at[part], self.sent.at[(0, 1, 1)[step]], sems.at[step], device).start()

    def finish(self, out):
        p, sems, far, part = self.p, self.sems, self.bufs[5], self.part
        arrived(far.at[part], sems.at[3], p.by_core)
        total = self.ref[p.z, p.y, p.x, p.c, :, self.lanes].astype(f32)
        out[:, self.lanes] = functools.reduce(jnp.add, [far[part, k].astype(f32) for k in range(3)], total)

    def settle(self):
        everything, far = self.bufs[0], self.bufs[5]
        gone(everything, self.sent.at[0], self.p.by_core)
        gone(everything.at[:, pl.ds(0, 3)], self.sent.at[1], self.p.by_core)
        gone(far, self.sent.at[2], self.p.by_core)


class TotalRows:
    def __init__(self, ref, part, p, sems, bufs):
        self.ref, self.part, self.p, self.bufs = ref, part, p, bufs
        self.sems, self.sent = sems[0].at[part], sems[1]

    def add(self, index, buf):
        at = (self.part,) + index
        self.ref[at] = self.ref[at] + buf

    def advance(self, step):
        p, part, sems = self.p, self.part, self.sems
        from_core, one_a, one_b, two_a, two_b, _ = self.bufs
        both, every, low, high = pl.ds(0, 2), slice(None), pl.ds(0, 32), pl.ds(32, 32)
        at = lambda y, x, c, *rows: self.ref.at[(part, y, x, c) + rows]
        if step:
            ref = (from_core.at[part], from_core.at[part, 0], from_core.at[part, 0, 0])[step - 1]
            arrived(ref, sems.at[step - 1], p.by_core)
        if step == 0:
            sends = [(at(both, both, p.oc), from_core, p.by_core)]
        elif step == 1:
            self.add((every, every, p.c), from_core[part])
            sends = [(at(p.oy, both, p.c, low), one_a, p.by_y), (at(both, p.ox, p.c, high), one_b, p.by_x)]
        elif step == 2:
            self.add((p.y, every, p.c, low), one_a[part])
            self.add((every, p.x, p.c, high), one_b[part])
            sends = [(at(p.y, p.ox, p.c, low), two_a, p.by_x), (at(p.oy, p.x, p.c, high), two_b, p.by_y)]
        else:
            self.add((p.y, p.x, p.c, low), two_a[part])
            self.add((p.y, p.x, p.c, high), two_b[part])
            return
        for src, buf, device in sends:
            remote(src, buf.at[part], self.sent.at[(0, 1, 1)[step]], sems.at[step], device).start()

    def settle(self):
        gone(self.bufs[0], self.sent.at[0], self.p.by_core)
        gone(self.bufs[0].at[pl.ds(0, 3)], self.sent.at[1], self.p.by_core)


class TotalVectors:
    def __init__(self, ref, p, sems, got, mid, far):
        self.ref, self.p, self.sems, self.got, self.mid, self.far = ref, p, sems, got, mid, far

    def begin(self):
        for k, device in enumerate(self.p.plane):
            remote(self.ref, self.got.at[k], self.sems.at[1], self.sems.at[0], device).start()

    def second(self):
        arrived(self.got, self.sems.at[0], self.p.by_core)
        self.mid[...] = functools.reduce(jnp.add, [self.got[k] for k in range(7)], self.ref[...])
        for k, device in enumerate(self.p.by_z):
            remote(self.mid, self.far.at[k], self.sems.at[3], self.sems.at[2], device).start()

    def finish(self):
        arrived(self.far, self.sems.at[2], self.p.by_core)
        gone(self.got, self.sems.at[1], self.p.by_core)
        gone(self.far, self.sems.at[3], self.p.by_core)
        return functools.reduce(jnp.add, [self.far[k] for k in range(3)], self.mid[...])


def layer_kernel(fast, kinds, *refs):
    shapes = dict(kinds, **scratch_list(fast))
    r, left = types.SimpleNamespace(), list(refs)
    for name, kind in shapes.items():
        amount = len(kind) if isinstance(kind, list) else 1
        taken, left = left[:amount], left[amount:]
        setattr(r, name, taken if isinstance(kind, list) else taken[0])
    assert not left
    p = Place()
    tok, cot = r.tok, r.cot
    member, spread = r.member, r.spread
    stack, probs, out_t, mix_t = r.stack, r.probs, r.out_t, r.mix_t
    lse_s, share, inner_s, total_h = r.lse_s, r.share, r.inner_s, r.total_h
    resid, n_one, n_two = r.resid, r.n_one, r.n_two
    acc_out, acc_two = r.acc_out, r.acc_two
    g_att, g_num = r.g_att, r.g_num
    g_mix, weight = g_num.at[0:SHORT], r.weight
    grads = r.grads
    vec_a, vec_b = r.vec_a, r.vec_b
    wa, wi, wo = r.wa, r.wi, r.wo
    da, di, do = (r.da, r.di, r.do) if fast else (r.o_a, r.o_i, r.o_o)

    def fetch(src, dst, slot):
        copy = pltpu.make_async_copy(src, dst, r.in_sem.at[slot])
        copy.start()
        return copy

    def taken(ref, slot):
        pltpu.make_async_copy(ref, ref, r.in_sem.at[slot]).wait()

    if fast:
        small_in = [fetch(ref, kept, k) for k, (ref, kept) in enumerate(zip(r.vectors, r.vec_in))]
        own_a, own_i, own_o = (ref.at[p.z, p.y, p.x, p.c] for ref in (wa, wi, wo))
        for pair in range(PAIRS):
            for slot, ref in enumerate((r.wq_s, r.wk_s, r.wv_s)):
                there = pl.ds(SMALL + pair * GROUP + slot * TILE, TILE)
                fetch(ref.at[:, pl.ds(pair * TILE, TILE)], own_a.at[:, there], 7)
        fetch(r.wi_s, own_i.at[:, pl.ds(0, 4 * D)], 8)
        fetch(r.wm_s, own_i.at[:, pl.ds(4 * D, D)], 8)
        fetch(r.wo_s, own_o, 9)
    tok_in = fetch(r.tok_h, tok, 10)
    rest_in = [
        fetch(src, dst, 11 + k)
        for k, (src, dst) in enumerate(
            ((r.member_h, member), (r.head_h, r.head_m), (r.group_h, r.group_m), (r.bias_h, r.bias), (r.cot_h, cot), (r.spread_h, spread))
        )
    ]

    other = p.fs // 2 * 2 + 1 - p.fs % 2
    pairs_at = (1 - p.fs // 2) * 2
    side = p.fs % 2
    barrier = pltpu.get_barrier_semaphore()
    reach = [(p.dp, other), (p.dp, pairs_at), (p.dp, pairs_at + 1)]
    if fast:
        reach += p.plane[3:] + p.by_z
    for device in reach:
        pl.semaphore_signal(barrier, inc=1, device_id=device, device_id_type=MESH)
    if fast:
        whose = p.dp * 4 + p.fs
        for copy in small_in:
            copy.wait()
        at = lax.broadcasted_iota(jnp.int32, (HEAD, SMALL), 0)
        lane = lax.broadcasted_iota(jnp.int32, (HEAD, SMALL), 1)
        rows = [ref[...].astype(f32).reshape(1, 16) for ref in r.vec_in[:6]]
        rows = jnp.concatenate(rows + [jnp.zeros((10, 16), f32)], axis=0).astype(bf16)
        spot = (lane[0:16] == at[0:16] + 16 * (whose % 8)).astype(f32).astype(bf16)
        own = nn(rows, spot)
        bias = jnp.concatenate([r.vec_in[6][...].astype(f32).reshape(1, HEAD), jnp.zeros((15, HEAD), f32)], axis=0)
        spot = (lane == at + HEAD * (whose % 2)).astype(f32).astype(bf16)
        own_bias = nn(bias.astype(bf16), spot)
        own = jnp.concatenate([own[0:6], own_bias[0:1], jnp.zeros((9, SMALL), f32)], axis=0)
        own_a[:, 0:SMALL] = own.astype(bf16)
    if fast:
        taken(own_a.at[:, pl.ds(SMALL, WIDTH)], 7)
    pl.semaphore_wait(barrier, len(reach))


    def first_norm(step, carry):
        at = pl.ds(pl.multiple_of(step * CHUNK, CHUNK), CHUNK)
        acc_two[at, :] = normalize(tok[at, :].astype(f32))[0]
        return carry

    if fast:
        spans = [(wa, 0, SMALL + GROUP), (wa, SMALL + GROUP, 3 * GROUP), (wi, 0, 1280), (wi, 1280, 1280), (wo, 0, D)]
        gathers = [
            Gather(ref, pl.ds(lo, wide), p, r.g_sem.at[k]) for k, (ref, lo, wide) in enumerate(spans)
        ]

    def pump(*events):
        if fast:
            for k, step in events:
                gathers[k].advance(step)

    pump((0, 0), (1, 0))
    if fast:
        taken(own_i, 8)
        taken(own_o, 9)
    tok_in.wait()
    lax.fori_loop(0, SHORT // CHUNK, first_norm, 0)
    pump((0, 1), (0, 2), (1, 1), (2, 0), (0, 3), (1, 2), (3, 0), (0, 4), (2, 1))
    for copy in rest_in:
        copy.wait()

    def rows_of(ref, lo, width):
        return ref[:, :, :, :, :, lo : lo + width].reshape(512, width)

    small = wa[:, :, :, :, :, 0:SMALL].astype(f32)
    by_z = jnp.sum(small, axis=(1, 2, 3))
    param = jnp.concatenate([by_z[z] for z in range(4)], axis=1)
    r.param[...] = param
    by_pair = jnp.sum(small, axis=3)
    r.bias_in[...] = jnp.concatenate(
        [by_pair[z, y, x, 6:7, :] for z in range(4) for y in range(2) for x in range(2)], axis=1
    )
    vec_a[...] = jnp.zeros_like(vec_a)
    vec_b[...] = jnp.zeros_like(vec_b)
    r.lanes_in[...] = jnp.zeros_like(r.lanes_in)

    gain_one, shift_one = r.param[0:1, :], r.param[1:2, :]

    def scale_shift(step, carry):
        at = pl.ds(pl.multiple_of(step * CHUNK, CHUNK), CHUNK)
        n_one[at, :] = (acc_two[at, :] * gain_one + shift_one).astype(bf16)
        return carry

    lax.fori_loop(0, SHORT // CHUNK, scale_shift, 0)

    index = lax.broadcasted_iota(jnp.int32, (TILE, 1), 0)
    steps_down = jnp.where(
        index < 64, 1 / 16, jnp.where(index < 96, 1 / 32, jnp.where(index < 112, 1 / 64, 1 / 128))
    ).astype(f32)

    def chunk_rows(step):
        one = pl.ds(pl.multiple_of(FIRST[1] + step * 128, 128), 128)
        two = pl.ds(pl.multiple_of(FIRST[2] + step * 64, 64), 64)
        return one, two, pl.ds(pl.multiple_of(FIRST[3] + step * 32, 32), 32)

    def chunk_members(chunk):
        near = [member[lo:hi, 0:CHUNK] for lo, hi in ((0, 128), (128, 192), (256, 288))]
        return near + [member[lo:hi, chunk] for lo, hi in ((384, 448), (448, 480), (480, 496), (496, 512))]

    lane_group = lax.broadcasted_iota(jnp.int32, (32, TILE), 1) // 32

    def squeeze(tall):
        parts = [tall[32 * part : 32 * part + 32, :] for part in range(4)]
        return jnp.where(
            lane_group < 2,
            jnp.where(lane_group == 0, parts[0], parts[1]),
            jnp.where(lane_group == 2, parts[2], parts[3]),
        )

    def widen(low):
        return jnp.concatenate([low, low, low, low], axis=0) * r.group_m[:, 0 : low.shape[1]]

    def by_head(both):
        half = both.shape[0] // 2
        lane = lax.broadcasted_iota(jnp.int32, (half, TILE), 1)
        return jnp.where(lane < HEAD, both[:half], both[half:])

    def two_heads(low):
        return jnp.concatenate([low, low], axis=0) * r.head_m[...]

    top_lane = lax.broadcasted_iota(jnp.int32, (HEADS, TILE), 1)
    top_scale_t = jnp.where(
        top_lane < 64, 1 / 16, jnp.where(top_lane < 96, 1 / 32, jnp.where(top_lane < 112, 1 / 64, 1 / 128))
    ).astype(f32)

    def tile_scale(tile):
        return jnp.where(
            tile < 8, 1.0, jnp.where(tile < 12, 0.5, jnp.where(tile < 14, 0.25, 0.125))
        ).astype(f32)

    def lanes_at(start, wide):
        return pl.ds(pl.multiple_of(start, TILE), wide)

    def tile_forward(tile, pair, kind, scale_t):
        rows = lanes_at(tile * TILE, TILE)
        at = lambda slot: (rows, lanes_at(pair * GROUP + slot * TILE, TILE))
        score = nt(two_heads(stack[at(1)]), stack[at(0)])
        score = jnp.concatenate([squeeze(score[:TILE]), squeeze(score[TILE:])], axis=1) + r.bias[kind]
        peak = jnp.max(score, axis=0, keepdims=True)
        prob = jnp.exp(score - peak)
        total = jnp.sum(prob, axis=0, keepdims=True)
        low = (prob * (1.0 / total)).astype(bf16)
        probs[tile, :, lanes_at(pair * 2 * TILE, 2 * TILE)] = low
        log_total = peak + jnp.log(total)
        lse_s[pair, 0:1, rows] = log_total[:, :TILE]
        lse_s[pair, 1:2, rows] = log_total[:, TILE:]
        made = nn(stack[at(2)].T, widen(low))
        head = pl.multiple_of(pair * TILE, TILE)
        out_t[pl.ds(head, HEAD), rows] = (made[:HEAD, :TILE] * scale_t).astype(bf16)
        out_t[pl.ds(head + HEAD, HEAD), rows] = (made[HEAD:, TILE:] * scale_t).astype(bf16)

    far_s, far_r = r.far_s, r.far_r
    far_out = [
        remote(far_s.at[0], far_r.at[0], r.far_sem.at[1], r.far_sem.at[0], (p.dp, other)),
        remote(far_s.at[1], far_r.at[1 + side], r.far_sem.at[1], r.far_sem.at[0], (p.dp, pairs_at)),
        remote(far_s.at[1], far_r.at[1 + side], r.far_sem.at[1], r.far_sem.at[0], (p.dp, pairs_at + 1)),
    ]
    tops_acc = acc_out

    def pair_forward(pair, carry):
        def pump_here(*plan):
            for number, events in enumerate(plan):
                if events:
                    pl.when(pair == number)(functools.partial(pump, *events))

        pump_here([], [(1, 4)])
        lanes = lanes_at(pair * GROUP, GROUP)
        made = nn(n_one[...], wa[:, :, :, :, :, lanes_at(SMALL + pair * GROUP, GROUP)].reshape(D, GROUP))
        first = lax.broadcasted_iota(jnp.int32, (1, GROUP), 1)
        stack[0:SHORT, lanes] = (made * jnp.where(first < TILE, 0.125, 1.0)).astype(bf16)
        key_like = first < 2 * TILE
        pump_here([(4, 0)])
        tops_acc[0:TILE, 0:GROUP] = jnp.zeros((TILE, GROUP), f32)

        def pool(step, carry):
            chunk = pl.ds(pl.multiple_of(step * CHUNK, CHUNK), CHUNK)
            made = nn(jnp.concatenate(chunk_members(chunk), axis=0), stack[chunk, lanes])
            to = chunk_rows(step)
            for level, (lo, hi) in enumerate(((0, 128), (128, 192), (192, 224))):
                scale = jnp.where(key_like, 0.5 ** (level + 1), 1.0)
                stack[to[level], lanes] = (made[lo:hi] * scale).astype(bf16)
            tops_acc[0:TILE, 0:GROUP] += made[224:352]
            return carry

        lax.fori_loop(0, SHORT // CHUNK, pool, 0)
        stack[FIRST[4] : STACK, lanes] = (
            tops_acc[0:TILE, 0:GROUP] * jnp.where(key_like, steps_down, 1.0)
        ).astype(bf16)
        theirs = lanes_at(pair * GROUP + TILE, 2 * TILE)
        mine = lanes_at(pair * 2 * TILE, 2 * TILE)
        far_s[0, :, mine] = stack[2016:2032, theirs]
        far_s[1, :, mine] = stack[2032:2048, theirs]

        @pl.when(pair == PAIRS - 1)
        def _():
            for copy in far_out:
                copy.start()

        def near_tiles(group, carry):
            for one in range(TOGETHER):
                tile = group * TOGETHER + one
                tile_forward(tile, pair, jnp.where(tile < 8, 0, 1), tile_scale(tile))
            for when, what, events in (
                (0, 1, [(1, 3), (2, 2)]),
                (0, 2, [(3, 1)]),
                (1, 2, [(2, 3), (3, 2), (4, 1)]),
                (2, 2, [(2, 4)]),
                (3, 0, [(3, 3), (4, 2)]),
            ):
                pl.when((pair == when) & (group == what))(functools.partial(pump, *events))
            return carry

        lax.fori_loop(0, 15 // TOGETHER, near_tiles, 0)
        return carry

    lax.fori_loop(0, PAIRS, pair_forward, 0)
    arrived(far_r, r.far_sem.at[0], p.by_core)
    gone(far_r, r.far_sem.at[1], p.by_core)
    last_rows = jnp.concatenate([far_r[1].astype(f32)[:8], far_r[2].astype(f32)[:8]], axis=0).astype(bf16)
    for pair in range(PAIRS):
        theirs = slice(pair * GROUP + TILE, (pair + 1) * GROUP)
        mine = slice(pair * 2 * TILE, (pair + 1) * 2 * TILE)
        stack[2016:2032, theirs] = far_r[0, :, mine]
        stack[2032:2048, theirs] = last_rows[:, mine]
    for pair in range(PAIRS):
        tile_forward(15, pair, 2, top_scale_t[0:1, :])
    idle = jnp.where(r.row_length[0] > SHORT, 0.0, far_off)
    lse_s[:, :, 1920:2048] = lse_s[:, :, 1920:2048] + jnp.where(top_lane[0:2] >= 96, idle, 0.0)

    edges = (0, 64, 96, 112, 128)

    def windows(step):
        one = pl.ds(pl.multiple_of(FIRST[1] + step * TILE, TILE), TILE)
        two = pl.ds(pl.multiple_of(FIRST[2] + step // 2 * TILE, TILE), TILE)
        return one, two, pl.ds(FIRST[3], TILE), pl.ds(FIRST[4], TILE)

    def per_level(step, chunk):
        one = member[0:512, chunk]

        def for_head(head):
            rows = []
            spans = [(0, 128), (128, 256), (256, 384), (384, 448), (448, 480), (480, 496), (496, 512)]
            for level, (lo, hi) in enumerate(spans, 1):
                rows.append(one[lo:hi] * share[level, head : head + 1, chunk].astype(bf16))
            return jnp.concatenate(rows, axis=0)

        return for_head

    def lse_of(lanes):
        return jnp.concatenate([lse_s[pair, :, lanes] for pair in range(PAIRS)], axis=0)

    def combine(step, carry):
        chunk = pl.ds(pl.multiple_of(step * CHUNK, CHUNK), CHUNK)
        wins = windows(step)
        logs = [lse_of(chunk)]
        for slot in range(3):
            parts = jnp.concatenate(split3(lse_of(wins[slot])), axis=0)
            made = nn(parts, member[slot * TILE : (slot + 1) * TILE, chunk])
            logs.append(made[0:8] + made[8:16] + made[16:24] + (slot + 1) * math.log(2.0))
        top = lse_of(wins[3])
        parts = []
        for slot in range(4):
            inside = (top_lane >= edges[slot]) & (top_lane < edges[slot + 1])
            parts += list(split3(jnp.where(inside, top, 0.0)))
        made = nn(jnp.concatenate(parts, axis=0), member[384:512, chunk])
        for slot in range(4):
            b = slot * 24
            logs.append(made[b : b + 8] + made[b + 8 : b + 16] + made[b + 16 : b + 24] + (slot + 4) * math.log(2.0))
        peak = functools.reduce(jnp.maximum, logs)
        den = functools.reduce(jnp.add, [jnp.exp(one - peak) for one in logs])
        lse = peak + jnp.log(den)
        for level in range(LEVELS):
            share[level, :, chunk] = jnp.exp(logs[level] - lse)
        for_head = per_level(step, chunk)
        for head in range(HEADS):
            at = slice(head * HEAD, (head + 1) * HEAD)
            coarse = jnp.concatenate([out_t[at, win] for win in wins], axis=1)
            made = nn(coarse, for_head(head))
            made = made + share[0, head : head + 1, chunk] * out_t[at, chunk].astype(f32)
            mix_t[at, chunk] = made.astype(bf16)
        return carry

    lax.fori_loop(0, SHORT // CHUNK, combine, 0)
    pump((3, 4), (4, 3))

    bias_mix, gain_two = r.param[2:3, :], r.param[3:4, :]
    shift_two, bias_out = r.param[4:5, :], r.param[5:6, :]
    w_mix = rows_of(wi, 4 * D, D)
    halves = [slice(half * 512, (half + 1) * 512) for half in range(2)]
    for at in halves:
        mid = tok[at, :].astype(f32) + tn(mix_t[:, at], w_mix) + bias_mix
        resid[at, :] = mid
        acc_out[at, :] = mid + bias_out
        normed, _ = normalize(mid)
        n_two[at, :] = (normed * gain_two + shift_two).astype(bf16)
    pump((4, 4))

    hid, g_pre = grads.at[0:SHORT, 0:D], grads.at[0:SHORT, D : 2 * D]
    acc_two[...] = jnp.zeros_like(acc_two)

    def total_i(part):
        return Total(di, lanes_at(part * 512, 512), part, p, r.si[0:2], r.si[2:])

    def total_o(part):
        return TotalRows(do, part, p, r.so[0:2], r.so[2:8])

    def onward(total, *steps):
        if fast:
            for part, step in steps:
                if isinstance(part, int):
                    total(part).advance(step)
                else:
                    pl.when(part >= 0)(lambda: total(part).advance(step))

    def feed(part, carry):
        lanes = pl.ds(pl.multiple_of(part * 512, 512), 512)
        w_in = wi[:, :, :, :, :, lanes].reshape(512, 512)
        w_out = wo[part].reshape(512, 512)
        b_in = r.bias_in[:, lanes]
        sums = jnp.zeros((1, 512), f32)
        for step in range(FEED_STEPS):
            at = pl.ds(step * (SHORT // FEED_STEPS), SHORT // FEED_STEPS)
            act, slope = gelu_both(nn(n_two[at, :], w_in) + b_in)
            act = act.astype(bf16)
            hid[at, :] = act
            back = (nt(cot[at, :], w_out) * slope).astype(bf16)
            g_pre[at, :] = back
            acc_out[at, :] += nn(act, w_out)
            acc_two[at, :] += nt(back, w_in)
            sums = sums + jnp.sum(back.astype(f32), axis=0, keepdims=True)
            if step == 0:
                onward(total_i, (part - 3, 3), (part - 2, 2), (part - 1, 1))
                onward(total_o, (part - 3, 3), (part - 2, 2), (part - 1, 1))
        r.lanes_in[0:1, lanes] = sums
        di[:, :, :, :, :, lanes] = tn(n_two[...], g_pre[...]).astype(bf16).reshape(4, 2, 2, 2, 16, 512)
        do[part] = tn(hid[...], cot[...]).astype(bf16).reshape(2, 2, 2, 64, 512)
        if fast:
            onward(total_i, (part, 0))
            onward(total_o, (part, 0))
        return carry

    lax.fori_loop(0, 4, feed, 0)

    for at in halves:
        n_two[at, :] = acc_out[at, :].astype(bf16)
        normed, inverse = normalize(resid[at, :])
        g_two = acc_two[at, :]
        c = cot[at, :].astype(f32)
        g_mid = c + normalize_back(g_two * gain_two, normed, inverse)
        resid[at, :] = g_mid
        low = g_mid.astype(bf16)
        g_att[at, :] = low
        for row, values in enumerate((low.astype(f32), g_two * normed, g_two, c)):
            vec_b[row : row + 1, :] += jnp.sum(values, axis=0, keepdims=True)
        g_mix[at, :] = nt(low, w_mix).astype(bf16)
        turned = nt(w_mix, low).astype(bf16).astype(f32) * mix_t[:, at].astype(f32)
        inner_s[:, at] = jnp.concatenate(
            [jnp.sum(turned[h * HEAD : (h + 1) * HEAD], axis=0, keepdims=True) for h in range(HEADS)], axis=0
        )
    out_copy = pltpu.make_async_copy(n_two, r.out, r.out_sem.at[0])
    out_copy.start()
    onward(total_i, (1, 3), (2, 2), (3, 1))
    onward(total_o, (1, 3), (2, 2), (3, 1))
    made = nn(mix_t[...], g_att[...])
    di[:, :, :, :, :, 4 * D :] = made.astype(bf16).reshape(4, 2, 2, 2, 16, D)
    onward(total_i, (4, 0))


    def keep_h(lanes, values):
        for pair in range(PAIRS):
            total_h[pair, :, lanes] = values[2 * pair : 2 * pair + 2]

    def sums_of(level, source, members):
        both = jnp.concatenate(split2(share[level, :, source] * inner_s[:, source]), axis=0)
        made = nt(both, members)
        return made[0:8] + made[8:16]

    tops_acc[0:TILE, :] = jnp.zeros((TILE, D), f32)

    def lift(step, carry):
        chunk = pl.ds(pl.multiple_of(step * CHUNK, CHUNK), CHUNK)
        to = chunk_rows(step)
        members = chunk_members(chunk)
        made = []
        for pair in range(PAIRS):
            weighted = [
                one * share[1 + k, head : head + 1, chunk].astype(bf16)
                for head in (2 * pair, 2 * pair + 1)
                for k, one in enumerate(members)
            ]
            tokens = g_num[chunk, pair * TILE : (pair + 1) * TILE]
            made.append(by_head(nn(jnp.concatenate(weighted, axis=0), tokens)))
        made = jnp.concatenate(made, axis=1)
        for level, (low, high) in enumerate(((0, 128), (128, 192), (192, 224))):
            g_num[to[level], :] = (made[low:high] * 0.5 ** (level + 1)).astype(bf16)
        tops_acc[0:TILE, :] += made[224:352]
        keep_h(chunk, share[0, :, chunk] * inner_s[:, chunk])
        keep_h(to[0], sums_of(1, chunk, member[0:128, chunk]))
        return carry

    lax.fori_loop(0, SHORT // CHUNK, lift, 0)
    g_num[FIRST[4] : STACK, :] = (tops_acc[0:TILE, :] * steps_down).astype(bf16)

    def lift_two(step, carry):
        source = pl.ds(pl.multiple_of(step * 512, 512), 512)
        rows = pl.ds(pl.multiple_of(FIRST[2] + step * TILE, TILE), TILE)
        keep_h(rows, sums_of(2, source, member[128:256, source]))
        return carry

    lax.fori_loop(0, 2, lift_two, 0)
    onward(total_i, (2, 3))
    onward(total_o, (2, 3))
    every = pl.ds(0, SHORT)
    keep_h(pl.ds(FIRST[3], TILE), sums_of(3, every, member[256:384, :]))
    tops = [sums_of(4 + slot, every, member[384:512, :]) for slot in range(4)]
    keep_h(
        pl.ds(FIRST[4], TILE),
        jnp.where(top_lane < 64, tops[0], jnp.where(top_lane < 96, tops[1], jnp.where(top_lane < 112, tops[2], tops[3]))),
    )
    for pair in range(PAIRS):
        weight[pair, :, 0:SHORT] = share[0, 2 * pair : 2 * pair + 2]
    weight[:, :, SHORT:STACK] = jnp.ones((PAIRS, 2, SHORT), f32)

    def tile_backward(tile, pair, scale):
        rows = lanes_at(tile * TILE, TILE)
        at = lambda slot: (rows, lanes_at(pair * GROUP + slot * TILE, TILE))
        num = g_num[rows, lanes_at(pair * TILE, TILE)]
        got = nt(two_heads(stack[at(2)]), num)
        got = jnp.concatenate([squeeze(got[:TILE]), squeeze(got[TILE:])], axis=1)
        both = lambda ref: jnp.concatenate([ref[pair, 0:1, rows], ref[pair, 1:2, rows]], axis=1)
        low = probs[tile, :, lanes_at(pair * 2 * TILE, 2 * TILE)].astype(f32)
        times = both(weight)
        wide_s = widen((low * (got * times - both(total_h))).astype(bf16))
        wide_p = widen((low * times).astype(bf16))
        tall = lambda wide: jnp.concatenate([wide[:, :TILE], wide[:, TILE:]], axis=0)
        grads[at(1)] = (by_head(nn(tall(wide_s), stack[at(0)])) * scale).astype(bf16)
        grads[at(2)] = by_head(nn(tall(wide_p), num)).astype(bf16)
        made = nn(stack[at(1)].T, wide_s)
        made = jnp.concatenate([made[:HEAD, :TILE], made[HEAD:, TILE:]], axis=0).astype(bf16).T
        grads[at(0)] = (made.astype(f32) * (scale * 0.125)).astype(bf16)

    for pair in range(PAIRS):
        tile_backward(15, pair, steps_down)
    back_s, back_r = r.back_s, r.back_r
    spans = [(slice(k * GROUP + TILE, (k + 1) * GROUP), slice(k * 2 * TILE, (k + 1) * 2 * TILE)) for k in range(PAIRS)]
    tall = jnp.concatenate([grads[2016:2048, theirs] for theirs, _ in spans], axis=1).astype(f32)
    nothing = jnp.zeros((8, 2 * D), f32)
    back_s[0] = tall[0:16].astype(bf16)
    back_s[1] = jnp.concatenate([tall[16:24], nothing], axis=0).astype(bf16)
    back_s[2] = jnp.concatenate([tall[24:32], nothing], axis=0).astype(bf16)
    back_out = [
        remote(back_s.at[0], back_r.at[0], r.far_sem.at[3], r.far_sem.at[2], (p.dp, other)),
        remote(back_s.at[1], back_r.at[1 + side], r.far_sem.at[3], r.far_sem.at[2], (p.dp, pairs_at)),
        remote(back_s.at[2], back_r.at[1 + side], r.far_sem.at[3], r.far_sem.at[2], (p.dp, pairs_at + 1)),
    ]
    for copy in back_out:
        copy.start()
    onward(total_i, (3, 2), (4, 1))
    onward(total_o, (3, 2))

    def total_a(part):
        return Total(da, lanes_at(part * GROUP, GROUP), part, p, r.sa[0:2], r.sa[2:])

    def far_grads():
        arrived(back_r, r.far_sem.at[2], p.by_core)
        gone(back_r, r.far_sem.at[3], p.by_core)
        two = (back_r[1].astype(f32) + back_r[2].astype(f32)).astype(bf16)
        for theirs, mine in spans:
            grads[2016:2032, theirs] = back_r[0, :, mine]
            grads[2032:2048, theirs] = two[:, mine]

    def send_rows():
        onward(total_o, (3, 3))
        for k, z in enumerate(p.zs):
            remote(do.at[z, p.y, p.x, p.c], r.so[7].at[k], r.so[8].at[1], r.so[8].at[0], p.by_z[k]).start()

    def finish_feed():
        for part in range(5):
            total_i(part).finish(r.keep_i)
        arrived(r.so[7], r.so[8].at[0], p.by_core)
        total = do[p.z, p.y, p.x, p.c].astype(f32)
        r.keep_o[...] = functools.reduce(jnp.add, [r.so[7][k].astype(f32) for k in range(3)], total)
        gone(r.so[7], r.so[8].at[1], p.by_core)
        total_o(0).settle()
        total_i(0).settle()
        for copy in kept[:2]:
            copy.start()

    if fast:
        kept = [
            pltpu.make_async_copy(src, dst, r.keep_sem.at[k])
            for k, (src, dst) in enumerate(
                ((r.keep_i, r.o_i), (r.keep_o, r.o_o), (r.keep_a, r.o_a), (r.keep_v, r.o_v))
            )
        ]

        early = TotalVectors(r.vec_b, p, r.v_sem.at[0], r.got_b, r.mid_b, r.far_b)
        late = TotalVectors(r.vec_s, p, r.v_sem.at[1], r.got_a, r.mid_a, r.far_a)
    vec_b[4:8, :] = jnp.concatenate([r.lanes_in[0:1, k * 512 : (k + 1) * 512] for k in range(4)], axis=0)

    def early_done():
        r.done_b[...] = early.finish()
        long = jnp.concatenate([r.done_b[4 + k : 5 + k] for k in range(4)], axis=1)
        long = pltpu.roll(jnp.concatenate([long] * 8, axis=0), 2048 - HEAD * whose, axis=1)[:, 0:SMALL]
        r.keep_v[8:16] = long

    def pair_backward(pair, carry):
        def near_back(group, carry):
            for one in range(TOGETHER):
                tile = group * TOGETHER + one
                tile_backward(tile, pair, tile_scale(tile))
            return carry

        lax.fori_loop(0, 15 // TOGETHER, near_back, 0)
        pl.when(pair == 0)(far_grads)
        if fast:
            pl.when(pair == 0)(lambda: onward(total_i, (3, 3), (4, 2)))
            pl.when(pair == 0)(send_rows)
            pl.when(pair == 1)(lambda: onward(total_i, (4, 3)))
            pl.when(pair == 0)(early.begin)
            pl.when(pair == 1)(early.second)
            pl.when(pair == 3)(finish_feed)
            pl.when(pair == 3)(early_done)
        onward(total_a, (pair - 3, 3), (pair - 2, 2), (pair - 1, 1))

        lanes = lanes_at(pair * GROUP, GROUP)

        def level_sums(step, carry):
            chunk = pl.ds(pl.multiple_of(step * CHUNK, CHUNK), CHUNK)
            top = grads[FIRST[4] : STACK, lanes]
            coarse = [grads[rows, lanes] for rows in chunk_rows(step)] + [top[0:32], top]
            made = nn(spread[chunk, :], jnp.concatenate(coarse, axis=0))
            stack[chunk, lanes] = (made + grads[chunk, lanes].astype(f32)).astype(bf16)
            return carry

        lax.fori_loop(0, SHORT // CHUNK, level_sums, 0)
        da[:, :, :, :, :, lanes] = tn(n_one[...], stack[0:SHORT, lanes]).astype(bf16).reshape(4, 2, 2, 2, 16, GROUP)
        onward(total_a, (pair, 0))
        return carry

    lax.fori_loop(0, PAIRS, pair_backward, 0)

    w_qkv = lambda: wa[:, :, :, :, :, SMALL : SMALL + WIDTH].reshape(D, WIDTH)

    def first_back(at, g_one):
        normed, inverse = normalize(tok[at, :].astype(f32))
        vec_a[0:1, :] += jnp.sum(g_one * normed, axis=0, keepdims=True)
        vec_a[1:2, :] += jnp.sum(g_one, axis=0, keepdims=True)
        g_att[at, :] = (resid[at, :] + normalize_back(g_one * gain_one, normed, inverse)).astype(bf16)

    acc_two[halves[0], :] = nt(stack[halves[0], :], w_qkv())
    acc_two[halves[1], :] = nt(stack[halves[1], :], w_qkv())
    first_back(halves[0], acc_two[halves[0], :])
    onward(total_a, (3, 1), (2, 2))
    first_back(halves[1], acc_two[halves[1], :])
    tok_copy = pltpu.make_async_copy(g_att, r.g_tok, r.out_sem.at[1])
    tok_copy.start()
    if fast:
        for row in range(2):
            for part in range(4):
                at = row * 4 + part
                r.vec_s[at : at + 1, :] = vec_a[row : row + 1, part * TILE : (part + 1) * TILE]
        late.begin()
        onward(total_a, (1, 3), (3, 2), (2, 3))
        late.second()
        onward(total_a, (3, 3))
        for part in range(3):
            total_a(part).finish(r.keep_a)
        last = late.finish()
        rows = [jnp.concatenate([last[at + part : at + part + 1] for part in range(4)], axis=1) for at in (0, 4)]
        short = jnp.concatenate(rows + [r.done_b[0:4], jnp.zeros((2, D), f32)], axis=0)
        short = pltpu.roll(short, 512 - 16 * whose, axis=1)[:, 0:SMALL]
        r.keep_v[0:8] = short
        kept[3].start()
        total_a(3).finish(r.keep_a)
        total_a(0).settle()
        kept[2].start()
        for copy in kept:
            copy.wait()
    else:
        r.o_v[0:8] = vec_a[...]
        r.o_v[8:16] = vec_b[...]
    out_copy.wait()
    tok_copy.wait()


def final_kernel(*refs):
    big, small, outs, (kept, vmem_a, vmem_i, vmem_o, vmem_v, sem) = refs[:2], refs[2:6], refs[6:21], refs[21:]
    parts = [pl.ds(k * CHUNK, CHUNK) for k in range(SHORT // CHUNK)]
    count = iter(range(24))
    copy = lambda src, dst: pltpu.make_async_copy(src, dst, sem.at[next(count)])
    into = [copy(ref.at[at], kept.at[slot, at]) for slot, ref in enumerate(big) for at in parts]
    onto = [copy(kept.at[slot, at], outs[slot].at[at]) for slot in range(2) for at in parts]
    rest = [copy(src, dst) for src, dst in zip(small, (vmem_a, vmem_i, vmem_o, vmem_v))]
    for one in into + rest:
        one.start()
    for one, then in zip(into, onto):
        one.wait()
        then.start()
    for one in rest:
        one.wait()
    for slot, at in ((2, 0), (3, 1), (8, 2), (9, 3), (10, 4), (14, 5)):
        outs[slot][...] = vmem_v[at : at + 1, 0:16].reshape(16)
    outs[12][...] = vmem_v[8:9, 0:HEAD].reshape(HEAD)
    for k in range(3):
        for pair in range(PAIRS):
            at = pair * GROUP + k * TILE
            outs[4 + k][:, pair * TILE : (pair + 1) * TILE] = vmem_a[:, at : at + TILE]
    outs[7][...] = vmem_i[:, 4 * D :]
    outs[11][...] = vmem_i[:, : 4 * D]
    outs[13][...] = vmem_o[...]
    for one in onto:
        one.wait()


def scratch_list(fast):
    V, S = pltpu.VMEM, pltpu.SemaphoreType.DMA
    made = dict(
        tok=V((SHORT, D), bf16),
        cot=V((SHORT, D), bf16),
        member=V((D, SHORT), bf16),
        spread=V((SHORT, GROUP), bf16),
        head_m=V((2 * TILE, TILE), bf16),
        group_m=V((TILE, 2 * TILE), bf16),
        bias=V((3, 32, 2 * TILE), f32),
        in_sem=S((17,)),
        out_sem=S((2,)),
        stack=V((STACK, WIDTH), bf16),
        probs=V((16, 32, HEADS * TILE), bf16),
        out_t=V((D, STACK), bf16),
        mix_t=V((D, SHORT), bf16),
        lse_s=V((PAIRS, 2, STACK), f32),
        share=V((LEVELS, HEADS, SHORT), f32),
        inner_s=V((HEADS, SHORT), f32),
        total_h=V((PAIRS, 2, STACK), f32),
        resid=V((SHORT, D), f32),
        n_one=V((SHORT, D), bf16),
        n_two=V((SHORT, D), bf16),
        acc_out=V((SHORT, D), f32),
        acc_two=V((SHORT, D), f32),
        grads=V((STACK, WIDTH), bf16),
        g_att=V((SHORT, D), bf16),
        weight=V((PAIRS, 2, STACK), f32),
        g_num=V((STACK, D), bf16),
        vec_a=V((8, D), f32),
        vec_b=V((8, D), f32),
        param=V((16, D), f32),
        bias_in=V((1, 4 * D), f32),
        lanes_in=V((8, 4 * D), f32),
        far_s=V((2, 16, 2 * D), bf16),
        far_r=V((3, 16, 2 * D), bf16),
        far_sem=S((4,)),
        back_s=V((3, 16, 2 * D), bf16),
        back_r=V((3, 16, 2 * D), bf16),
    )
    if fast:

        def sums(parts, wide):
            shape = lambda *dims: V((parts,) + dims + (16, wide), bf16)
            return [S((parts, 4)), S((3,)), shape(4, 2, 2), shape(2, 2), shape(2, 2), shape(2), shape(2), shape(3)]

        rows = lambda *dims: V((4,) + dims + (D,), bf16)
        made.update(
            wa=V(SLOTS + (16, WIDTH + SMALL), bf16),
            wi=V(SLOTS + (16, 5 * D), bf16),
            wo=V(SLOTS + (64, D), bf16),
            da=V(SLOTS + (16, WIDTH), bf16),
            di=V(SLOTS + (16, 5 * D), bf16),
            do=V(SLOTS + (64, D), bf16),
            g_sem=S((5, 7)),
            si=sums(5, D),
            so=[S((4, 3)), S((2,)), rows(2, 2, 64), rows(2, 32), rows(2, 32), rows(32), rows(32), V((3, 64, D), bf16), S((2,))],
            sa=sums(4, GROUP),
            v_sem=S((2, 4)),
            vec_s=V((8, TILE), f32),
            got_a=V((7, 8, TILE), f32),
            mid_a=V((8, TILE), f32),
            far_a=V((3, 8, TILE), f32),
            got_b=V((7, 8, D), f32),
            mid_b=V((8, D), f32),
            far_b=V((3, 8, D), f32),
            done_b=V((8, D), f32),
            vec_in=[V((16,), bf16)] * 6 + [V((HEAD,), bf16)],
            keep_a=V((16, WIDTH), f32),
            keep_i=V((16, 5 * D), f32),
            keep_o=V((HEAD, D), f32),
            keep_v=V((16, SMALL), f32),
            keep_sem=S((4,)),
        )
    return made


def constants():
    member = member_matrix()
    as_low = lambda values: jnp.asarray(values.astype(np.float32), bf16)
    return dict(
        member_h=as_low(member),
        spread_h=as_low(np.ascontiguousarray(spread_matrix())),
        head_h=as_low(head_mask()),
        group_h=as_low(group_mask()),
        bias_h=jnp.asarray(block_bias()),
    )


def run_layer(fast, hbm, vmem):
    sd = jax.ShapeDtypeStruct
    const = constants()
    hbm = dict(hbm, **const)
    here, there = pl.BlockSpec(memory_space=pltpu.VMEM), pl.BlockSpec(memory_space=pl.ANY)
    slots = () if fast else SLOTS
    kind = f32 if fast else bf16
    outs = dict(
        out=sd((SHORT, D), bf16),
        g_tok=sd((SHORT, D), bf16),
        o_a=sd(slots + (16, WIDTH), kind),
        o_i=sd(slots + (16, 5 * D), kind),
        o_o=sd(slots + (64, D), kind),
        o_v=sd((16, SMALL if fast else D), f32),
    )
    row_length = hbm.pop("row_length")
    operands = dict(hbm, row_length=row_length, **vmem)
    flat = lambda parts: [one for part in parts.values() for one in (part if isinstance(part, list) else [part])]
    specs = [there] * len(flat(hbm)) + [pl.BlockSpec(memory_space=pltpu.SMEM)] + [here] * len(vmem)
    hbm_outs = len(outs) if fast else 2
    return pl.pallas_call(
        functools.partial(layer_kernel, fast, dict(operands, **outs)),
        out_shape=list(outs.values()),
        in_specs=specs,
        out_specs=[there] * hbm_outs + [here] * (len(outs) - hbm_outs),
        scratch_shapes=flat(scratch_list(fast)),
        compiler_params=pltpu.CompilerParams(
            collective_id=0, has_side_effects=True, vmem_limit_bytes=63 * 2**20
        ),
    )(*flat(operands))


def finish_outputs(*parts):
    sd = jax.ShapeDtypeStruct
    vmem, hbm = pl.BlockSpec(memory_space=pltpu.VMEM), pl.BlockSpec(memory_space=pl.ANY)
    own, square = sd((16,), f32), sd((16, D), f32)
    tokens = sd((SHORT, D), bf16)
    outs = [tokens, tokens, own, own, square, square, square, square, own, own, own]
    outs += [sd((16, 4 * D), f32), sd((HEAD,), f32), sd((HEAD, D), f32), own]
    return pl.pallas_call(
        final_kernel,
        out_shape=outs,
        in_specs=[hbm] * 6,
        out_specs=[hbm] * 2 + [vmem] * 13,
        scratch_shapes=[
            pltpu.VMEM((2, SHORT, D), bf16),
            pltpu.VMEM((16, WIDTH), f32),
            pltpu.VMEM((16, 5 * D), f32),
            pltpu.VMEM((HEAD, D), f32),
            pltpu.VMEM((16, SMALL), f32),
            pltpu.SemaphoreType.DMA((20,)),
        ],
    )(*parts)


def on_device(
    tokens, cotangent, row_length, first_gain, first_shift, query_weight, key_weight, value_weight,
    mixer_weight, mixer_bias, second_gain, second_shift, inner_weight, inner_bias, outer_weight, outer_bias,
):
    n_dp, n_fsdp = lax.axis_size("dp"), lax.axis_size("fsdp")
    fast = (n_dp, n_fsdp) == (8, 4) and query_weight.shape[0] == 16
    vectors = (first_gain, first_shift, mixer_bias, second_gain, second_shift, outer_bias)
    first = dict(tok_h=tokens, cot_h=cotangent, row_length=row_length)
    if fast:
        first.update(
            wq_s=query_weight, wk_s=key_weight, wv_s=value_weight, wm_s=mixer_weight, wi_s=inner_weight, wo_s=outer_weight,
            vectors=list(vectors) + [inner_bias],
        )
        return finish_outputs(*run_layer(True, first, dict()))
    whole = lambda part: lax.all_gather(part, AXES, axis=0, tiled=True)
    three = jnp.stack([part.reshape(-1, PAIRS, TILE) for part in (query_weight, key_weight, value_weight)], axis=2)
    wide = whole(three.reshape(-1, WIDTH))
    eights = [whole(vector).reshape(4, 8, 16) for vector in vectors]
    small = jnp.zeros((4, 8, 16, SMALL), bf16)
    for row, vector in enumerate(eights):
        for at in range(8):
            small = small.at[:, at, row, 16 * at : 16 * at + 16].set(vector[:, at])
    pairs = whole(inner_bias).reshape(4, 4, 2, 64)
    pairs_at = small.reshape(4, 4, 2, 16, SMALL)
    for at in range(2):
        pairs_at = pairs_at.at[:, :, at, 6, 64 * at : 64 * at + 64].set(pairs[:, :, at])
    wide = jnp.concatenate((pairs_at.reshape(4, 8, 16, SMALL), wide.reshape(4, 8, 16, WIDTH)), axis=-1)
    weights = dict(
        wa=wide.reshape(SLOTS + (16, WIDTH + SMALL)),
        wi=whole(jnp.concatenate((inner_weight, mixer_weight), axis=1)).reshape(SLOTS + (16, 5 * D)),
        wo=whole(outer_weight).reshape(SLOTS + (64, D)),
    )
    out, g_tok, d_a, d_i, d_o, o_v = run_layer(False, first, weights)
    owned = lambda part: lax.psum_scatter(part, AXES, scatter_dimension=0, tiled=True)
    g_a = owned(d_a.astype(f32).reshape(D, WIDTH))
    g_q, g_k, g_v = (g_a.reshape(-1, PAIRS, 3, TILE)[:, :, k].reshape(-1, D) for k in range(3))
    g_i = owned(d_i.astype(f32).reshape(D, 5 * D))
    g_i, g_m = g_i[:, : 4 * D], g_i[:, 4 * D :]
    g_o = owned(d_o.astype(f32).reshape(4 * D, D))
    six = [owned(o_v[k]) for k in (0, 1, 8, 9, 10, 11)]
    g_bias_in = owned(o_v[12:16].reshape(-1))
    return (
        out, g_tok, six[0], six[1], g_q, g_k, g_v, g_m, six[2], six[3], six[4], g_i, g_bias_in, g_o, six[5],
    )


def solution(mesh):
    rows, flat, both = P(AXES, None), P(AXES), P("dp")
    in_specs = (rows, rows, both, flat, flat, rows, rows, rows, rows, flat, flat, flat, rows, flat, rows, flat)
    out_specs = (rows, rows, flat, flat, rows, rows, rows, rows, flat, flat, flat, rows, flat, rows, flat)
    return jax.shard_map(on_device, mesh=mesh, in_specs=in_specs, out_specs=out_specs, check_vma=False)
```

```python
import functools
import math
import types

import jax
import jax.numpy as jnp
import numpy as np
from jax import lax
from jax.experimental import pallas as pl
from jax.experimental.pallas import tpu as pltpu
from jax.sharding import PartitionSpec as P

D = 512
HEADS = 8
HEAD = 64
BLOCK = 16
SHORT = 1024
LEVELS = 8
TILE = 128
TOGETHER = 5
CHUNK = 256
STACK = 2 * SHORT
WIDTH = 3 * D
SMALL = 128
GROUP = 3 * TILE
PAIRS = HEADS // 2
AXES = ("dp", "fsdp")
MESH = pl.DeviceIdType.MESH
SLOTS = (4, 2, 2, 2)

norm_eps = 1e-05
far_off = -1e30
f32 = jnp.float32
bf16 = jnp.bfloat16

FIRST = [STACK - (STACK >> level) for level in range(LEVELS + 1)]
LOW_TOP = 4


def member_matrix():
    token = np.arange(SHORT)
    rows = []
    for level, span in ((1, 256), (2, 512), (3, 1024)):
        rows.append((token[None] % span) >> level == np.arange(TILE)[:, None])
    for level in range(LOW_TOP, LEVELS):
        rows.append(token[None] >> level == np.arange(SHORT >> level)[:, None])
    rows.append(np.zeros((8, SHORT), bool))
    return np.concatenate(rows).astype(np.float32)


def spread_matrix():
    member = member_matrix()
    near = np.concatenate([member[0:128, :CHUNK], member[128:192, :CHUNK], member[256:288, :CHUNK], np.zeros((32, CHUNK))])
    return np.concatenate([np.tile(near, (1, SHORT // CHUNK)), member[384:]]).T.astype(np.float32)


def block_bias():
    key = np.arange(32)[:, None]
    query = np.arange(2 * TILE)[None]
    across = (key < BLOCK) != (query % 32 < BLOCK)
    last = np.where(query % TILE >= 96, ~across, across)
    kinds = [np.ones_like(across), across, last]
    return np.stack([np.where(kind, 0.0, far_off) for kind in kinds]).astype(np.float32)


def head_mask():
    lane = np.arange(TILE)[None]
    side = np.arange(2 * TILE)[:, None] // TILE
    return (lane // HEAD == side).astype(np.float32)


def group_mask():
    key = np.arange(TILE)[:, None]
    query = np.arange(2 * TILE)[None]
    return (key // 32 == query % TILE // 32).astype(np.float32)


def top_level_of():
    index = np.arange(TILE)
    return np.minimum(LOW_TOP + (index >= 64) * 1 + (index >= 96) * 1 + (index >= 112) * 1, 7)


def nn(a, b):
    return lax.dot_general(a, b, (((1,), (0,)), ((), ())), preferred_element_type=f32)


def nt(a, b):
    return lax.dot_general(a, b, (((1,), (1,)), ((), ())), preferred_element_type=f32)


def tn(a, b):
    return lax.dot_general(a, b, (((0,), (0,)), ((), ())), preferred_element_type=f32)


def normalize(values):
    center = values - jnp.mean(values, axis=-1, keepdims=True)
    inverse = lax.rsqrt(jnp.mean(center * center, axis=-1, keepdims=True) + norm_eps)
    return center * inverse, inverse


def normalize_back(grad_normed, normed, inverse):
    return inverse * (
        grad_normed
        - jnp.mean(grad_normed, axis=-1, keepdims=True)
        - normed * jnp.mean(grad_normed * normed, axis=-1, keepdims=True)
    )


def gelu_both(v):
    mag = jnp.abs(v) * (0.5**0.5)
    t = 1.0 / (1.0 + 0.3275911 * mag)
    gauss = jnp.exp(-0.5 * v * v)
    poly = t * (
        0.254829592
        + t * (-0.284496736 + t * (1.421413741 + t * (-1.453152027 + t * 1.061405429)))
    )
    tail = 0.5 * poly * gauss
    cdf = jnp.where(v < 0, tail, 1.0 - tail)
    return v * cdf, cdf + v * gauss * ((2 * math.pi) ** -0.5)


def split3(values):
    one = values.astype(bf16)
    rest = values - one.astype(f32)
    two = rest.astype(bf16)
    return one, two, (rest - two.astype(f32)).astype(bf16)


def split2(values):
    one = values.astype(bf16)
    return one, (values - one.astype(f32)).astype(bf16)


class Place:
    def __init__(self):
        self.dp = lax.axis_index("dp")
        self.fs = lax.axis_index("fsdp")
        self.z, self.y = self.dp // 2, self.dp % 2
        self.x, self.c = self.fs // 2, self.fs % 2
        self.oy, self.ox, self.oc = 1 - self.y, 1 - self.x, 1 - self.c
        self.zs = [lax.rem(self.z + step, 4) for step in (1, 2, 3)]
        self.by_core = (self.dp, self.x * 2 + self.oc)
        self.by_x = (self.dp, self.ox * 2 + self.c)
        self.by_y = (self.z * 2 + self.oy, self.fs)
        self.by_z = [(z * 2 + self.y, self.fs) for z in self.zs]
        ys, xs, cs = (self.y, self.oy), (self.x, self.ox), (self.c, self.oc)
        self.plane = [(self.z * 2 + ys[k // 4], xs[k // 2 % 2] * 2 + cs[k % 2]) for k in range(1, 8)]


def remote(src, dst, send, recv, device):
    return pltpu.make_async_remote_copy(
        src_ref=src, dst_ref=dst, send_sem=send, recv_sem=recv, device_id=device, device_id_type=MESH
    )


def arrived(ref, sem, device):
    remote(ref, ref, sem, sem, device).wait_recv()


def gone(ref, sem, device):
    remote(ref, ref, sem, sem, device).wait_send()


class Gather:
    def __init__(self, ref, lanes, p, sems):
        self.at = lambda z, y, x: ref.at[z, y, x, p.c, :, lanes]
        self.p, self.sems = p, sems

    def advance(self, step):
        p, at, sems = self.p, self.at, self.sems
        low, high, both, full = pl.ds(0, 2), pl.ds(2, 2), pl.ds(0, 2), pl.ds(0, 4)
        if step:
            ref = (at(pl.ds(0, 3), p.y, p.x), at(full, p.y, p.x), at(full, both, p.x), at(full, both, both))[step - 1]
            arrived(ref, sems.at[step - 1], p.by_core)
        if step == 4:
            gone(at(pl.ds(0, 3), p.y, p.x), sems.at[4], p.by_core)
            gone(at(pl.ds(0, 3), both, both), sems.at[5], p.by_core)
            gone(at(full, both, both), sems.at[6], p.by_core)
            return
        if step == 0:
            parts = [(at(p.z, p.y, p.x), device) for device in p.by_z]
        elif step == 1:
            parts = [(at(low, p.y, p.x), p.by_x), (at(high, p.y, p.x), p.by_y)]
        elif step == 2:
            parts = [(at(low, p.y, both), p.by_y), (at(high, both, p.x), p.by_x)]
        else:
            parts = [(at(full, both, both), p.by_core)]
        for part, device in parts:
            remote(part, part, sems.at[(4, 5, 5, 6)[step]], sems.at[step], device).start()


class Total:
    def __init__(self, ref, lanes, part, p, sems, bufs):
        self.ref, self.lanes, self.part, self.p, self.bufs = ref, lanes, part, p, bufs
        self.sems, self.sent = sems[0].at[part], sems[1]

    def add(self, index, buf):
        at = index + (self.p.c, slice(None), self.lanes)
        self.ref[at] = self.ref[at] + buf

    def advance(self, step):
        p, part, sems = self.p, self.part, self.sems
        from_core, one_a, one_b, two_a, two_b, far = self.bufs
        at = lambda z, y, x, c: self.ref.at[z, y, x, c, :, self.lanes]
        low, high, both, full, every = pl.ds(0, 2), pl.ds(2, 2), pl.ds(0, 2), pl.ds(0, 4), slice(None)
        if step:
            ref = (from_core.at[part], from_core.at[part, both], from_core.at[part, 0])[step - 1]
            arrived(ref, sems.at[step - 1], p.by_core)
        if step == 0:
            sends = [(at(full, both, both, p.oc), from_core, p.by_core)]
        elif step == 1:
            for z in range(4):
                self.add((z, every, every), from_core[part, z])
            sends = [(at(low, p.oy, both, p.c), one_a, p.by_y), (at(high, both, p.ox, p.c), one_b, p.by_x)]
        elif step == 2:
            for z in range(2):
                self.add((z, p.y, every), one_a[part, z])
                self.add((2 + z, every, p.x), one_b[part, z])
            sends = [(at(low, p.y, p.ox, p.c), two_a, p.by_x), (at(high, p.oy, p.x, p.c), two_b, p.by_y)]
        else:
            for z in range(2):
                self.add((z, p.y, p.x), two_a[part, z])
                self.add((2 + z, p.y, p.x), two_b[part, z])
            for k, z in enumerate(p.zs):
                remote(at(z, p.y, p.x, p.c), far.at[part, k], self.sent.at[2], sems.at[3], p.by_z[k]).start()
            return
        for src, buf, device in sends:
            remote(src, buf.at[part], self.sent.at[(0, 1, 1)[step]], sems.at[step], device).start()

    def finish(self, out):
        p, sems, far, part = self.p, self.sems, self.bufs[5], self.part
        arrived(far.at[part], sems.at[3], p.by_core)
        total = self.ref[p.z, p.y, p.x, p.c, :, self.lanes].astype(f32)
        out[:, self.lanes] = functools.reduce(jnp.add, [far[part, k].astype(f32) for k in range(3)], total)

    def settle(self):
        everything, far = self.bufs[0], self.bufs[5]
        gone(everything, self.sent.at[0], self.p.by_core)
        gone(everything.at[:, pl.ds(0, 3)], self.sent.at[1], self.p.by_core)
        gone(far, self.sent.at[2], self.p.by_core)


class TotalRows:
    def __init__(self, ref, part, p, sems, bufs):
        self.ref, self.part, self.p, self.bufs = ref, part, p, bufs
        self.sems, self.sent = sems[0].at[part], sems[1]

    def add(self, index, buf):
        at = (self.part,) + index
        self.ref[at] = self.ref[at] + buf

    def advance(self, step):
        p, part, sems = self.p, self.part, self.sems
        from_core, one_a, one_b, two_a, two_b, _ = self.bufs
        both, every, low, high = pl.ds(0, 2), slice(None), pl.ds(0, 32), pl.ds(32, 32)
        at = lambda y, x, c, *rows: self.ref.at[(part, y, x, c) + rows]
        if step:
            ref = (from_core.at[part], from_core.at[part, 0], from_core.at[part, 0, 0])[step - 1]
            arrived(ref, sems.at[step - 1], p.by_core)
        if step == 0:
            sends = [(at(both, both, p.oc), from_core, p.by_core)]
        elif step == 1:
            self.add((every, every, p.c), from_core[part])
            sends = [(at(p.oy, both, p.c, low), one_a, p.by_y), (at(both, p.ox, p.c, high), one_b, p.by_x)]
        elif step == 2:
            self.add((p.y, every, p.c, low), one_a[part])
            self.add((every, p.x, p.c, high), one_b[part])
            sends = [(at(p.y, p.ox, p.c, low), two_a, p.by_x), (at(p.oy, p.x, p.c, high), two_b, p.by_y)]
        else:
            self.add((p.y, p.x, p.c, low), two_a[part])
            self.add((p.y, p.x, p.c, high), two_b[part])
            return
        for src, buf, device in sends:
            remote(src, buf.at[part], self.sent.at[(0, 1, 1)[step]], sems.at[step], device).start()

    def settle(self):
        gone(self.bufs[0], self.sent.at[0], self.p.by_core)
        gone(self.bufs[0].at[pl.ds(0, 3)], self.sent.at[1], self.p.by_core)


class TotalVectors:
    def __init__(self, ref, p, sems, got, mid, far):
        self.ref, self.p, self.sems, self.got, self.mid, self.far = ref, p, sems, got, mid, far

    def begin(self):
        for k, device in enumerate(self.p.plane):
            remote(self.ref, self.got.at[k], self.sems.at[1], self.sems.at[0], device).start()

    def second(self):
        arrived(self.got, self.sems.at[0], self.p.by_core)
        self.mid[...] = functools.reduce(jnp.add, [self.got[k] for k in range(7)], self.ref[...])
        for k, device in enumerate(self.p.by_z):
            remote(self.mid, self.far.at[k], self.sems.at[3], self.sems.at[2], device).start()

    def finish(self):
        arrived(self.far, self.sems.at[2], self.p.by_core)
        gone(self.got, self.sems.at[1], self.p.by_core)
        gone(self.far, self.sems.at[3], self.p.by_core)
        return functools.reduce(jnp.add, [self.far[k] for k in range(3)], self.mid[...])


def layer_kernel(fast, kinds, *refs):
    shapes = dict(kinds, **scratch_list(fast))
    r, left = types.SimpleNamespace(), list(refs)
    for name, kind in shapes.items():
        amount = len(kind) if isinstance(kind, list) else 1
        taken, left = left[:amount], left[amount:]
        setattr(r, name, taken if isinstance(kind, list) else taken[0])
    assert not left
    p = Place()
    tok, cot = r.tok, r.cot
    member, spread = r.member, r.spread
    stack, probs, out_t, mix_t = r.stack, r.probs, r.out_t, r.mix_t
    lse_s, share, inner_s, total_h = r.lse_s, r.share, r.inner_s, r.total_h
    resid, n_one, n_two = r.resid, r.n_one, r.n_two
    acc_out, acc_two = r.acc_out, r.acc_two
    g_att, g_num = r.g_att, r.g_num
    g_mix, weight = g_num.at[0:SHORT], r.weight
    grads = r.grads
    vec_a, vec_b = r.vec_a, r.vec_b
    wa, wi, wo = r.wa, r.wi, r.wo
    da, di, do = (r.da, r.di, r.do) if fast else (r.o_a, r.o_i, r.o_o)

    def fetch(src, dst, slot):
        copy = pltpu.make_async_copy(src, dst, r.in_sem.at[slot])
        copy.start()
        return copy

    def taken(ref, slot):
        pltpu.make_async_copy(ref, ref, r.in_sem.at[slot]).wait()

    if fast:
        small_in = [fetch(ref, kept, k) for k, (ref, kept) in enumerate(zip(r.vectors, r.vec_in))]
        own_a, own_i, own_o = (ref.at[p.z, p.y, p.x, p.c] for ref in (wa, wi, wo))
        for pair in range(PAIRS):
            for slot, ref in enumerate((r.wq_s, r.wk_s, r.wv_s)):
                there = pl.ds(SMALL + pair * GROUP + slot * TILE, TILE)
                fetch(ref.at[:, pl.ds(pair * TILE, TILE)], own_a.at[:, there], 7)
        fetch(r.wi_s, own_i.at[:, pl.ds(0, 4 * D)], 8)
        fetch(r.wm_s, own_i.at[:, pl.ds(4 * D, D)], 8)
        fetch(r.wo_s, own_o, 9)
    tok_in = fetch(r.tok_h, tok, 10)
    rest_in = [
        fetch(src, dst, 11 + k)
        for k, (src, dst) in enumerate(
            ((r.member_h, member), (r.head_h, r.head_m), (r.group_h, r.group_m), (r.bias_h, r.bias), (r.cot_h, cot), (r.spread_h, spread))
        )
    ]

    other = p.fs // 2 * 2 + 1 - p.fs % 2
    pairs_at = (1 - p.fs // 2) * 2
    side = p.fs % 2
    barrier = pltpu.get_barrier_semaphore()
    reach = [(p.dp, other), (p.dp, pairs_at), (p.dp, pairs_at + 1)]
    if fast:
        reach += p.plane[3:] + p.by_z
    for device in reach:
        pl.semaphore_signal(barrier, inc=1, device_id=device, device_id_type=MESH)
    if fast:
        whose = p.dp * 4 + p.fs
        for copy in small_in:
            copy.wait()
        at = lax.broadcasted_iota(jnp.int32, (HEAD, SMALL), 0)
        lane = lax.broadcasted_iota(jnp.int32, (HEAD, SMALL), 1)
        rows = [ref[...].astype(f32).reshape(1, 16) for ref in r.vec_in[:6]]
        rows = jnp.concatenate(rows + [jnp.zeros((10, 16), f32)], axis=0).astype(bf16)
        spot = (lane[0:16] == at[0:16] + 16 * (whose % 8)).astype(f32).astype(bf16)
        own = nn(rows, spot)
        bias = jnp.concatenate([r.vec_in[6][...].astype(f32).reshape(1, HEAD), jnp.zeros((15, HEAD), f32)], axis=0)
        spot = (lane == at + HEAD * (whose % 2)).astype(f32).astype(bf16)
        own_bias = nn(bias.astype(bf16), spot)
        own = jnp.concatenate([own[0:6], own_bias[0:1], jnp.zeros((9, SMALL), f32)], axis=0)
        own_a[:, 0:SMALL] = own.astype(bf16)
    if fast:
        taken(own_a.at[:, pl.ds(SMALL, WIDTH)], 7)
    pl.semaphore_wait(barrier, len(reach))


    def first_norm(step, carry):
        at = pl.ds(pl.multiple_of(step * CHUNK, CHUNK), CHUNK)
        acc_two[at, :] = normalize(tok[at, :].astype(f32))[0]
        return carry

    if fast:
        spans = [(wa, 0, SMALL + GROUP), (wa, SMALL + GROUP, 3 * GROUP), (wi, 0, 1280), (wi, 1280, 1280), (wo, 0, D)]
        gathers = [
            Gather(ref, pl.ds(lo, wide), p, r.g_sem.at[k]) for k, (ref, lo, wide) in enumerate(spans)
        ]

    def pump(*events):
        if fast:
            for k, step in events:
                gathers[k].advance(step)

    pump((0, 0), (1, 0))
    if fast:
        taken(own_i, 8)
        taken(own_o, 9)
    tok_in.wait()
    lax.fori_loop(0, SHORT // CHUNK, first_norm, 0)
    pump((0, 1), (0, 2), (1, 1), (2, 0), (0, 3), (1, 2), (3, 0), (0, 4), (2, 1))
    for copy in rest_in:
        copy.wait()

    def rows_of(ref, lo, width):
        return ref[:, :, :, :, :, lo : lo + width].reshape(512, width)

    small = wa[:, :, :, :, :, 0:SMALL].astype(f32)
    by_z = jnp.sum(small, axis=(1, 2, 3))
    param = jnp.concatenate([by_z[z] for z in range(4)], axis=1)
    r.param[...] = param
    by_pair = jnp.sum(small, axis=3)
    r.bias_in[...] = jnp.concatenate(
        [by_pair[z, y, x, 6:7, :] for z in range(4) for y in range(2) for x in range(2)], axis=1
    )
    vec_a[...] = jnp.zeros_like(vec_a)
    vec_b[...] = jnp.zeros_like(vec_b)
    r.lanes_in[...] = jnp.zeros_like(r.lanes_in)

    gain_one, shift_one = r.param[0:1, :], r.param[1:2, :]

    def scale_shift(step, carry):
        at = pl.ds(pl.multiple_of(step * CHUNK, CHUNK), CHUNK)
        n_one[at, :] = (acc_two[at, :] * gain_one + shift_one).astype(bf16)
        return carry

    lax.fori_loop(0, SHORT // CHUNK, scale_shift, 0)

    index = lax.broadcasted_iota(jnp.int32, (TILE, 1), 0)
    steps_down = jnp.where(
        index < 64, 1 / 16, jnp.where(index < 96, 1 / 32, jnp.where(index < 112, 1 / 64, 1 / 128))
    ).astype(f32)

    def chunk_rows(step):
        one = pl.ds(pl.multiple_of(FIRST[1] + step * 128, 128), 128)
        two = pl.ds(pl.multiple_of(FIRST[2] + step * 64, 64), 64)
        return one, two, pl.ds(pl.multiple_of(FIRST[3] + step * 32, 32), 32)

    def chunk_members(chunk):
        near = [member[lo:hi, 0:CHUNK] for lo, hi in ((0, 128), (128, 192), (256, 288))]
        return near + [member[lo:hi, chunk] for lo, hi in ((384, 448), (448, 480), (480, 496), (496, 512))]

    lane_group = lax.broadcasted_iota(jnp.int32, (32, TILE), 1) // 32

    def squeeze(tall):
        parts = [tall[32 * part : 32 * part + 32, :] for part in range(4)]
        return jnp.where(
            lane_group < 2,
            jnp.where(lane_group == 0, parts[0], parts[1]),
            jnp.where(lane_group == 2, parts[2], parts[3]),
        )

    def widen(low):
        return jnp.concatenate([low, low, low, low], axis=0) * r.group_m[:, 0 : low.shape[1]]

    def by_head(both):
        half = both.shape[0] // 2
        lane = lax.broadcasted_iota(jnp.int32, (half, TILE), 1)
        return jnp.where(lane < HEAD, both[:half], both[half:])

    def two_heads(low):
        return jnp.concatenate([low, low], axis=0) * r.head_m[...]

    top_lane = lax.broadcasted_iota(jnp.int32, (HEADS, TILE), 1)
    top_scale_t = jnp.where(
        top_lane < 64, 1 / 16, jnp.where(top_lane < 96, 1 / 32, jnp.where(top_lane < 112, 1 / 64, 1 / 128))
    ).astype(f32)

    def tile_scale(tile):
        return jnp.where(
            tile < 8, 1.0, jnp.where(tile < 12, 0.5, jnp.where(tile < 14, 0.25, 0.125))
        ).astype(f32)

    def lanes_at(start, wide):
        return pl.ds(pl.multiple_of(start, TILE), wide)

    def tile_forward(tile, pair, kind, scale_t):
        rows = lanes_at(tile * TILE, TILE)
        at = lambda slot: (rows, lanes_at(pair * GROUP + slot * TILE, TILE))
        score = nt(two_heads(stack[at(1)]), stack[at(0)])
        score = jnp.concatenate([squeeze(score[:TILE]), squeeze(score[TILE:])], axis=1) + r.bias[kind]
        peak = jnp.max(score, axis=0, keepdims=True)
        prob = jnp.exp(score - peak)
        total = jnp.sum(prob, axis=0, keepdims=True)
        low = (prob * (1.0 / total)).astype(bf16)
        probs[tile, :, lanes_at(pair * 2 * TILE, 2 * TILE)] = low
        log_total = peak + jnp.log(total)
        lse_s[pair, 0:1, rows] = log_total[:, :TILE]
        lse_s[pair, 1:2, rows] = log_total[:, TILE:]
        made = nn(stack[at(2)].T, widen(low))
        head = pl.multiple_of(pair * TILE, TILE)
        out_t[pl.ds(head, HEAD), rows] = (made[:HEAD, :TILE] * scale_t).astype(bf16)
        out_t[pl.ds(head + HEAD, HEAD), rows] = (made[HEAD:, TILE:] * scale_t).astype(bf16)

    far_s, far_r = r.far_s, r.far_r
    far_out = [
        remote(far_s.at[0], far_r.at[0], r.far_sem.at[1], r.far_sem.at[0], (p.dp, other)),
        remote(far_s.at[1], far_r.at[1 + side], r.far_sem.at[1], r.far_sem.at[0], (p.dp, pairs_at)),
        remote(far_s.at[1], far_r.at[1 + side], r.far_sem.at[1], r.far_sem.at[0], (p.dp, pairs_at + 1)),
    ]
    tops_acc = acc_out

    def pair_forward(pair, carry):
        def pump_here(*plan):
            for number, events in enumerate(plan):
                if events:
                    pl.when(pair == number)(functools.partial(pump, *events))

        pump_here([], [(1, 4)])
        lanes = lanes_at(pair * GROUP, GROUP)
        made = nn(n_one[...], wa[:, :, :, :, :, lanes_at(SMALL + pair * GROUP, GROUP)].reshape(D, GROUP))
        first = lax.broadcasted_iota(jnp.int32, (1, GROUP), 1)
        stack[0:SHORT, lanes] = (made * jnp.where(first < TILE, 0.125, 1.0)).astype(bf16)
        key_like = first < 2 * TILE
        pump_here([(4, 0)])
        tops_acc[0:TILE, 0:GROUP] = jnp.zeros((TILE, GROUP), f32)

        def pool(step, carry):
            chunk = pl.ds(pl.multiple_of(step * CHUNK, CHUNK), CHUNK)
            made = nn(jnp.concatenate(chunk_members(chunk), axis=0), stack[chunk, lanes])
            to = chunk_rows(step)
            for level, (lo, hi) in enumerate(((0, 128), (128, 192), (192, 224))):
                scale = jnp.where(key_like, 0.5 ** (level + 1), 1.0)
                stack[to[level], lanes] = (made[lo:hi] * scale).astype(bf16)
            tops_acc[0:TILE, 0:GROUP] += made[224:352]
            return carry

        lax.fori_loop(0, SHORT // CHUNK, pool, 0)
        stack[FIRST[4] : STACK, lanes] = (
            tops_acc[0:TILE, 0:GROUP] * jnp.where(key_like, steps_down, 1.0)
        ).astype(bf16)
        theirs = lanes_at(pair * GROUP + TILE, 2 * TILE)
        mine = lanes_at(pair * 2 * TILE, 2 * TILE)
        far_s[0, :, mine] = stack[2016:2032, theirs]
        far_s[1, :, mine] = stack[2032:2048, theirs]

        @pl.when(pair == PAIRS - 1)
        def _():
            for copy in far_out:
                copy.start()

        def near_tiles(group, carry):
            for one in range(TOGETHER):
                tile = group * TOGETHER + one
                tile_forward(tile, pair, jnp.where(tile < 8, 0, 1), tile_scale(tile))
            for when, what, events in (
                (0, 1, [(1, 3), (2, 2)]),
                (0, 2, [(3, 1)]),
                (1, 2, [(2, 3), (3, 2), (4, 1)]),
                (2, 2, [(2, 4)]),
                (3, 0, [(3, 3), (4, 2)]),
            ):
                pl.when((pair == when) & (group == what))(functools.partial(pump, *events))
            return carry

        lax.fori_loop(0, 15 // TOGETHER, near_tiles, 0)
        return carry

    lax.fori_loop(0, PAIRS, pair_forward, 0)
    arrived(far_r, r.far_sem.at[0], p.by_core)
    gone(far_r, r.far_sem.at[1], p.by_core)
    last_rows = jnp.concatenate([far_r[1].astype(f32)[:8], far_r[2].astype(f32)[:8]], axis=0).astype(bf16)
    for pair in range(PAIRS):
        theirs = slice(pair * GROUP + TILE, (pair + 1) * GROUP)
        mine = slice(pair * 2 * TILE, (pair + 1) * 2 * TILE)
        stack[2016:2032, theirs] = far_r[0, :, mine]
        stack[2032:2048, theirs] = last_rows[:, mine]
    for pair in range(PAIRS):
        tile_forward(15, pair, 2, top_scale_t[0:1, :])
    idle = jnp.where(r.row_length[0] > SHORT, 0.0, far_off)
    lse_s[:, :, 1920:2048] = lse_s[:, :, 1920:2048] + jnp.where(top_lane[0:2] >= 96, idle, 0.0)

    edges = (0, 64, 96, 112, 128)

    def windows(step):
        one = pl.ds(pl.multiple_of(FIRST[1] + step * TILE, TILE), TILE)
        two = pl.ds(pl.multiple_of(FIRST[2] + step // 2 * TILE, TILE), TILE)
        return one, two, pl.ds(FIRST[3], TILE), pl.ds(FIRST[4], TILE)

    def per_level(step, chunk):
        one = member[0:512, chunk]

        def for_head(head):
            rows = []
            spans = [(0, 128), (128, 256), (256, 384), (384, 448), (448, 480), (480, 496), (496, 512)]
            for level, (lo, hi) in enumerate(spans, 1):
                rows.append(one[lo:hi] * share[level, head : head + 1, chunk].astype(bf16))
            return jnp.concatenate(rows, axis=0)

        return for_head

    def lse_of(lanes):
        return jnp.concatenate([lse_s[pair, :, lanes] for pair in range(PAIRS)], axis=0)

    def combine(step, carry):
        chunk = pl.ds(pl.multiple_of(step * CHUNK, CHUNK), CHUNK)
        wins = windows(step)
        logs = [lse_of(chunk)]
        for slot in range(3):
            parts = jnp.concatenate(split3(lse_of(wins[slot])), axis=0)
            made = nn(parts, member[slot * TILE : (slot + 1) * TILE, chunk])
            logs.append(made[0:8] + made[8:16] + made[16:24] + (slot + 1) * math.log(2.0))
        top = lse_of(wins[3])
        parts = []
        for slot in range(4):
            inside = (top_lane >= edges[slot]) & (top_lane < edges[slot + 1])
            parts += list(split3(jnp.where(inside, top, 0.0)))
        made = nn(jnp.concatenate(parts, axis=0), member[384:512, chunk])
        for slot in range(4):
            b = slot * 24
            logs.append(made[b : b + 8] + made[b + 8 : b + 16] + made[b + 16 : b + 24] + (slot + 4) * math.log(2.0))
        peak = functools.reduce(jnp.maximum, logs)
        den = functools.reduce(jnp.add, [jnp.exp(one - peak) for one in logs])
        lse = peak + jnp.log(den)
        for level in range(LEVELS):
            share[level, :, chunk] = jnp.exp(logs[level] - lse)
        for_head = per_level(step, chunk)
        for head in range(HEADS):
            at = slice(head * HEAD, (head + 1) * HEAD)
            coarse = jnp.concatenate([out_t[at, win] for win in wins], axis=1)
            made = nn(coarse, for_head(head))
            made = made + share[0, head : head + 1, chunk] * out_t[at, chunk].astype(f32)
            mix_t[at, chunk] = made.astype(bf16)
        return carry

    lax.fori_loop(0, SHORT // CHUNK, combine, 0)
    pump((3, 4), (4, 3))

    bias_mix, gain_two = r.param[2:3, :], r.param[3:4, :]
    shift_two, bias_out = r.param[4:5, :], r.param[5:6, :]
    w_mix = rows_of(wi, 4 * D, D)
    halves = [slice(half * 512, (half + 1) * 512) for half in range(2)]
    for at in halves:
        mid = tok[at, :].astype(f32) + tn(mix_t[:, at], w_mix) + bias_mix
        resid[at, :] = mid
        acc_out[at, :] = mid + bias_out
        normed, _ = normalize(mid)
        n_two[at, :] = (normed * gain_two + shift_two).astype(bf16)
    pump((4, 4))

    rows = (pl.ds(0, SHORT), pl.ds(SHORT, SHORT))
    hid, g_pre = ([grads.at[at, pl.ds(lane, D)] for at in rows] for lane in (0, D))
    acc_two[...] = jnp.zeros_like(acc_two)

    def total_i(part):
        return Total(di, lanes_at(part * 512, 512), part, p, r.si[0:2], r.si[2:])

    def total_o(part):
        return TotalRows(do, part, p, r.so[0:2], r.so[2:8])

    def onward(total, *steps):
        if fast:
            for part, step in steps:
                if isinstance(part, int):
                    total(part).advance(step)
                else:
                    pl.when(part >= 0)(lambda: total(part).advance(step))

    def feed_grads(part):
        lanes = pl.ds(part * 512, 512)
        di[:, :, :, :, :, lanes] = tn(n_two[...], g_pre[part % 2][...]).astype(bf16).reshape(4, 2, 2, 2, 16, 512)
        do[part] = tn(hid[part % 2][...], cot[...]).astype(bf16).reshape(2, 2, 2, 64, 512)
        onward(total_i, (part, 0))
        onward(total_o, (part, 0))

    for part in range(4):
        lanes = pl.ds(part * 512, 512)
        w_in = wi[:, :, :, :, :, lanes].reshape(512, 512)
        w_out = wo[part].reshape(512, 512)
        pre = nn(n_two[...], w_in) + r.bias_in[:, lanes]
        back = nt(cot[...], w_out)
        if part:
            feed_grads(part - 1)
        act, slope = gelu_both(pre)
        act = act.astype(bf16)
        back = (back * slope).astype(bf16)
        hid[part % 2][...] = act
        g_pre[part % 2][...] = back
        r.lanes_in[0:1, lanes] = jnp.sum(back.astype(f32), axis=0, keepdims=True)
        acc_out[...] += nn(act, w_out)
        acc_two[...] += nt(back, w_in)
        for total in (total_i, total_o):
            onward(total, *[(part - k, k) for k in (3, 2, 1) if part >= k])
    feed_grads(3)

    for at in halves:
        n_two[at, :] = acc_out[at, :].astype(bf16)
        normed, inverse = normalize(resid[at, :])
        g_two = acc_two[at, :]
        c = cot[at, :].astype(f32)
        g_mid = c + normalize_back(g_two * gain_two, normed, inverse)
        resid[at, :] = g_mid
        low = g_mid.astype(bf16)
        g_att[at, :] = low
        for row, values in enumerate((low.astype(f32), g_two * normed, g_two, c)):
            vec_b[row : row + 1, :] += jnp.sum(values, axis=0, keepdims=True)
        g_mix[at, :] = nt(low, w_mix).astype(bf16)
        turned = nt(w_mix, low).astype(bf16).astype(f32) * mix_t[:, at].astype(f32)
        inner_s[:, at] = jnp.concatenate(
            [jnp.sum(turned[h * HEAD : (h + 1) * HEAD], axis=0, keepdims=True) for h in range(HEADS)], axis=0
        )
    out_copy = pltpu.make_async_copy(n_two, r.out, r.out_sem.at[0])
    out_copy.start()
    onward(total_i, (1, 3), (2, 2), (3, 1))
    made = nn(mix_t[...], g_att[...])
    di[:, :, :, :, :, 4 * D :] = made.astype(bf16).reshape(4, 2, 2, 2, 16, D)
    onward(total_i, (4, 0))
    onward(total_o, (1, 3), (2, 2), (3, 1))


    def keep_h(lanes, values):
        for pair in range(PAIRS):
            total_h[pair, :, lanes] = values[2 * pair : 2 * pair + 2]

    def sums_of(level, source, members):
        both = jnp.concatenate(split2(share[level, :, source] * inner_s[:, source]), axis=0)
        made = nt(both, members)
        return made[0:8] + made[8:16]

    tops_acc[0:TILE, :] = jnp.zeros((TILE, D), f32)

    def lift(step, carry):
        chunk = pl.ds(pl.multiple_of(step * CHUNK, CHUNK), CHUNK)
        to = chunk_rows(step)
        members = chunk_members(chunk)
        made = []
        for pair in range(PAIRS):
            weighted = [
                one * share[1 + k, head : head + 1, chunk].astype(bf16)
                for head in (2 * pair, 2 * pair + 1)
                for k, one in enumerate(members)
            ]
            tokens = g_num[chunk, pair * TILE : (pair + 1) * TILE]
            made.append(by_head(nn(jnp.concatenate(weighted, axis=0), tokens)))
        made = jnp.concatenate(made, axis=1)
        for level, (low, high) in enumerate(((0, 128), (128, 192), (192, 224))):
            g_num[to[level], :] = (made[low:high] * 0.5 ** (level + 1)).astype(bf16)
        tops_acc[0:TILE, :] += made[224:352]
        keep_h(chunk, share[0, :, chunk] * inner_s[:, chunk])
        keep_h(to[0], sums_of(1, chunk, member[0:128, chunk]))
        return carry

    lax.fori_loop(0, SHORT // CHUNK, lift, 0)
    g_num[FIRST[4] : STACK, :] = (tops_acc[0:TILE, :] * steps_down).astype(bf16)

    def lift_two(step, carry):
        source = pl.ds(pl.multiple_of(step * 512, 512), 512)
        rows = pl.ds(pl.multiple_of(FIRST[2] + step * TILE, TILE), TILE)
        keep_h(rows, sums_of(2, source, member[128:256, source]))
        return carry

    lax.fori_loop(0, 2, lift_two, 0)
    onward(total_i, (2, 3))
    onward(total_o, (2, 3))
    every = pl.ds(0, SHORT)
    keep_h(pl.ds(FIRST[3], TILE), sums_of(3, every, member[256:384, :]))
    tops = [sums_of(4 + slot, every, member[384:512, :]) for slot in range(4)]
    keep_h(
        pl.ds(FIRST[4], TILE),
        jnp.where(top_lane < 64, tops[0], jnp.where(top_lane < 96, tops[1], jnp.where(top_lane < 112, tops[2], tops[3]))),
    )
    for pair in range(PAIRS):
        weight[pair, :, 0:SHORT] = share[0, 2 * pair : 2 * pair + 2]
    weight[:, :, SHORT:STACK] = jnp.ones((PAIRS, 2, SHORT), f32)

    def tile_backward(tile, pair, scale):
        rows = lanes_at(tile * TILE, TILE)
        at = lambda slot: (rows, lanes_at(pair * GROUP + slot * TILE, TILE))
        num = g_num[rows, lanes_at(pair * TILE, TILE)]
        got = nt(two_heads(stack[at(2)]), num)
        got = jnp.concatenate([squeeze(got[:TILE]), squeeze(got[TILE:])], axis=1)
        both = lambda ref: jnp.concatenate([ref[pair, 0:1, rows], ref[pair, 1:2, rows]], axis=1)
        low = probs[tile, :, lanes_at(pair * 2 * TILE, 2 * TILE)].astype(f32)
        times = both(weight)
        wide_s = widen((low * (got * times - both(total_h))).astype(bf16))
        wide_p = widen((low * times).astype(bf16))
        tall = lambda wide: jnp.concatenate([wide[:, :TILE], wide[:, TILE:]], axis=0)
        grads[at(1)] = (by_head(nn(tall(wide_s), stack[at(0)])) * scale).astype(bf16)
        grads[at(2)] = by_head(nn(tall(wide_p), num)).astype(bf16)
        made = nn(stack[at(1)].T, wide_s)
        made = jnp.concatenate([made[:HEAD, :TILE], made[HEAD:, TILE:]], axis=0).astype(bf16).T
        grads[at(0)] = (made.astype(f32) * (scale * 0.125)).astype(bf16)

    for pair in range(PAIRS):
        tile_backward(15, pair, steps_down)
    back_s, back_r = r.back_s, r.back_r
    spans = [(slice(k * GROUP + TILE, (k + 1) * GROUP), slice(k * 2 * TILE, (k + 1) * 2 * TILE)) for k in range(PAIRS)]
    tall = jnp.concatenate([grads[2016:2048, theirs] for theirs, _ in spans], axis=1).astype(f32)
    nothing = jnp.zeros((8, 2 * D), f32)
    back_s[0] = tall[0:16].astype(bf16)
    back_s[1] = jnp.concatenate([tall[16:24], nothing], axis=0).astype(bf16)
    back_s[2] = jnp.concatenate([tall[24:32], nothing], axis=0).astype(bf16)
    back_out = [
        remote(back_s.at[0], back_r.at[0], r.far_sem.at[3], r.far_sem.at[2], (p.dp, other)),
        remote(back_s.at[1], back_r.at[1 + side], r.far_sem.at[3], r.far_sem.at[2], (p.dp, pairs_at)),
        remote(back_s.at[2], back_r.at[1 + side], r.far_sem.at[3], r.far_sem.at[2], (p.dp, pairs_at + 1)),
    ]
    for copy in back_out:
        copy.start()
    onward(total_i, (3, 2), (4, 1))
    onward(total_o, (3, 2))

    def total_a(part):
        return Total(da, lanes_at(part * GROUP, GROUP), part, p, r.sa[0:2], r.sa[2:])

    def far_grads():
        arrived(back_r, r.far_sem.at[2], p.by_core)
        gone(back_r, r.far_sem.at[3], p.by_core)
        two = (back_r[1].astype(f32) + back_r[2].astype(f32)).astype(bf16)
        for theirs, mine in spans:
            grads[2016:2032, theirs] = back_r[0, :, mine]
            grads[2032:2048, theirs] = two[:, mine]

    def send_rows():
        onward(total_o, (3, 3))
        for k, z in enumerate(p.zs):
            remote(do.at[z, p.y, p.x, p.c], r.so[7].at[k], r.so[8].at[1], r.so[8].at[0], p.by_z[k]).start()

    def finish_feed():
        for part in range(5):
            total_i(part).finish(r.keep_i)
        arrived(r.so[7], r.so[8].at[0], p.by_core)
        total = do[p.z, p.y, p.x, p.c].astype(f32)
        r.keep_o[...] = functools.reduce(jnp.add, [r.so[7][k].astype(f32) for k in range(3)], total)
        gone(r.so[7], r.so[8].at[1], p.by_core)
        total_o(0).settle()
        total_i(0).settle()
        for copy in kept[:2]:
            copy.start()

    if fast:
        kept = [
            pltpu.make_async_copy(src, dst, r.keep_sem.at[k])
            for k, (src, dst) in enumerate(
                ((r.keep_i, r.o_i), (r.keep_o, r.o_o), (r.keep_a, r.o_a), (r.keep_v, r.o_v))
            )
        ]

        early = TotalVectors(r.vec_b, p, r.v_sem.at[0], r.got_b, r.mid_b, r.far_b)
        late = TotalVectors(r.vec_s, p, r.v_sem.at[1], r.got_a, r.mid_a, r.far_a)
    vec_b[4:8, :] = jnp.concatenate([r.lanes_in[0:1, k * 512 : (k + 1) * 512] for k in range(4)], axis=0)

    def early_done():
        r.done_b[...] = early.finish()
        long = jnp.concatenate([r.done_b[4 + k : 5 + k] for k in range(4)], axis=1)
        long = pltpu.roll(jnp.concatenate([long] * 8, axis=0), 2048 - HEAD * whose, axis=1)[:, 0:SMALL]
        r.keep_v[8:16] = long

    def pair_backward(pair, carry):
        def near_back(group, carry):
            for one in range(TOGETHER):
                tile = group * TOGETHER + one
                tile_backward(tile, pair, tile_scale(tile))
            return carry

        lax.fori_loop(0, 15 // TOGETHER, near_back, 0)
        pl.when(pair == 0)(far_grads)
        if fast:
            pl.when(pair == 0)(lambda: onward(total_i, (3, 3), (4, 2)))
            pl.when(pair == 0)(send_rows)
            pl.when(pair == 1)(lambda: onward(total_i, (4, 3)))
            pl.when(pair == 0)(early.begin)
            pl.when(pair == 1)(early.second)
            pl.when(pair == 3)(finish_feed)
            pl.when(pair == 3)(early_done)
        onward(total_a, (pair - 3, 3), (pair - 2, 2), (pair - 1, 1))

        lanes = lanes_at(pair * GROUP, GROUP)

        def level_sums(step, carry):
            chunk = pl.ds(pl.multiple_of(step * CHUNK, CHUNK), CHUNK)
            top = grads[FIRST[4] : STACK, lanes]
            coarse = [grads[rows, lanes] for rows in chunk_rows(step)] + [top[0:32], top]
            made = nn(spread[chunk, :], jnp.concatenate(coarse, axis=0))
            stack[chunk, lanes] = (made + grads[chunk, lanes].astype(f32)).astype(bf16)
            return carry

        lax.fori_loop(0, SHORT // CHUNK, level_sums, 0)
        da[:, :, :, :, :, lanes] = tn(n_one[...], stack[0:SHORT, lanes]).astype(bf16).reshape(4, 2, 2, 2, 16, GROUP)
        onward(total_a, (pair, 0))
        return carry

    lax.fori_loop(0, PAIRS, pair_backward, 0)

    w_qkv = lambda: wa[:, :, :, :, :, SMALL : SMALL + WIDTH].reshape(D, WIDTH)

    def first_back(at, g_one):
        normed, inverse = normalize(tok[at, :].astype(f32))
        vec_a[0:1, :] += jnp.sum(g_one * normed, axis=0, keepdims=True)
        vec_a[1:2, :] += jnp.sum(g_one, axis=0, keepdims=True)
        g_att[at, :] = (resid[at, :] + normalize_back(g_one * gain_one, normed, inverse)).astype(bf16)

    acc_two[halves[0], :] = nt(stack[halves[0], :], w_qkv())
    acc_two[halves[1], :] = nt(stack[halves[1], :], w_qkv())
    first_back(halves[0], acc_two[halves[0], :])
    onward(total_a, (3, 1), (2, 2))
    first_back(halves[1], acc_two[halves[1], :])
    tok_copy = pltpu.make_async_copy(g_att, r.g_tok, r.out_sem.at[1])
    tok_copy.start()
    if fast:
        for row in range(2):
            for part in range(4):
                at = row * 4 + part
                r.vec_s[at : at + 1, :] = vec_a[row : row + 1, part * TILE : (part + 1) * TILE]
        late.begin()
        onward(total_a, (1, 3), (3, 2), (2, 3))
        late.second()
        onward(total_a, (3, 3))
        for part in range(3):
            total_a(part).finish(r.keep_a)
        last = late.finish()
        rows = [jnp.concatenate([last[at + part : at + part + 1] for part in range(4)], axis=1) for at in (0, 4)]
        short = jnp.concatenate(rows + [r.done_b[0:4], jnp.zeros((2, D), f32)], axis=0)
        short = pltpu.roll(short, 512 - 16 * whose, axis=1)[:, 0:SMALL]
        r.keep_v[0:8] = short
        kept[3].start()
        total_a(3).finish(r.keep_a)
        total_a(0).settle()
        kept[2].start()
        for copy in kept:
            copy.wait()
    else:
        r.o_v[0:8] = vec_a[...]
        r.o_v[8:16] = vec_b[...]
    out_copy.wait()
    tok_copy.wait()


def final_kernel(*refs):
    big, small, outs, (kept, vmem_a, vmem_i, vmem_o, vmem_v, sem) = refs[:2], refs[2:6], refs[6:21], refs[21:]
    parts = [pl.ds(k * CHUNK, CHUNK) for k in range(SHORT // CHUNK)]
    count = iter(range(24))
    copy = lambda src, dst: pltpu.make_async_copy(src, dst, sem.at[next(count)])
    into = [copy(ref.at[at], kept.at[slot, at]) for slot, ref in enumerate(big) for at in parts]
    onto = [copy(kept.at[slot, at], outs[slot].at[at]) for slot in range(2) for at in parts]
    rest = [copy(src, dst) for src, dst in zip(small, (vmem_a, vmem_i, vmem_o, vmem_v))]
    for one in into + rest:
        one.start()
    for one, then in zip(into, onto):
        one.wait()
        then.start()
    for one in rest:
        one.wait()
    for slot, at in ((2, 0), (3, 1), (8, 2), (9, 3), (10, 4), (14, 5)):
        outs[slot][...] = vmem_v[at : at + 1, 0:16].reshape(16)
    outs[12][...] = vmem_v[8:9, 0:HEAD].reshape(HEAD)
    for k in range(3):
        for pair in range(PAIRS):
            at = pair * GROUP + k * TILE
            outs[4 + k][:, pair * TILE : (pair + 1) * TILE] = vmem_a[:, at : at + TILE]
    outs[7][...] = vmem_i[:, 4 * D :]
    outs[11][...] = vmem_i[:, : 4 * D]
    outs[13][...] = vmem_o[...]
    for one in onto:
        one.wait()


def scratch_list(fast):
    V, S = pltpu.VMEM, pltpu.SemaphoreType.DMA
    made = dict(
        tok=V((SHORT, D), bf16),
        cot=V((SHORT, D), bf16),
        member=V((D, SHORT), bf16),
        spread=V((SHORT, GROUP), bf16),
        head_m=V((2 * TILE, TILE), bf16),
        group_m=V((TILE, 2 * TILE), bf16),
        bias=V((3, 32, 2 * TILE), f32),
        in_sem=S((17,)),
        out_sem=S((2,)),
        stack=V((STACK, WIDTH), bf16),
        probs=V((16, 32, HEADS * TILE), bf16),
        out_t=V((D, STACK), bf16),
        mix_t=V((D, SHORT), bf16),
        lse_s=V((PAIRS, 2, STACK), f32),
        share=V((LEVELS, HEADS, SHORT), f32),
        inner_s=V((HEADS, SHORT), f32),
        total_h=V((PAIRS, 2, STACK), f32),
        resid=V((SHORT, D), f32),
        n_one=V((SHORT, D), bf16),
        n_two=V((SHORT, D), bf16),
        acc_out=V((SHORT, D), f32),
        acc_two=V((SHORT, D), f32),
        grads=V((STACK, WIDTH), bf16),
        g_att=V((SHORT, D), bf16),
        weight=V((PAIRS, 2, STACK), f32),
        g_num=V((STACK, D), bf16),
        vec_a=V((8, D), f32),
        vec_b=V((8, D), f32),
        param=V((16, D), f32),
        bias_in=V((1, 4 * D), f32),
        lanes_in=V((8, 4 * D), f32),
        far_s=V((2, 16, 2 * D), bf16),
        far_r=V((3, 16, 2 * D), bf16),
        far_sem=S((4,)),
        back_s=V((3, 16, 2 * D), bf16),
        back_r=V((3, 16, 2 * D), bf16),
    )
    if fast:

        def sums(parts, wide):
            shape = lambda *dims: V((parts,) + dims + (16, wide), bf16)
            return [S((parts, 4)), S((3,)), shape(4, 2, 2), shape(2, 2), shape(2, 2), shape(2), shape(2), shape(3)]

        rows = lambda *dims: V((4,) + dims + (D,), bf16)
        made.update(
            wa=V(SLOTS + (16, WIDTH + SMALL), bf16),
            wi=V(SLOTS + (16, 5 * D), bf16),
            wo=V(SLOTS + (64, D), bf16),
            da=V(SLOTS + (16, WIDTH), bf16),
            di=V(SLOTS + (16, 5 * D), bf16),
            do=V(SLOTS + (64, D), bf16),
            g_sem=S((5, 7)),
            si=sums(5, D),
            so=[S((4, 3)), S((2,)), rows(2, 2, 64), rows(2, 32), rows(2, 32), rows(32), rows(32), V((3, 64, D), bf16), S((2,))],
            sa=sums(4, GROUP),
            v_sem=S((2, 4)),
            vec_s=V((8, TILE), f32),
            got_a=V((7, 8, TILE), f32),
            mid_a=V((8, TILE), f32),
            far_a=V((3, 8, TILE), f32),
            got_b=V((7, 8, D), f32),
            mid_b=V((8, D), f32),
            far_b=V((3, 8, D), f32),
            done_b=V((8, D), f32),
            vec_in=[V((16,), bf16)] * 6 + [V((HEAD,), bf16)],
            keep_a=V((16, WIDTH), f32),
            keep_i=V((16, 5 * D), f32),
            keep_o=V((HEAD, D), f32),
            keep_v=V((16, SMALL), f32),
            keep_sem=S((4,)),
        )
    return made


def constants():
    member = member_matrix()
    as_low = lambda values: jnp.asarray(values.astype(np.float32), bf16)
    return dict(
        member_h=as_low(member),
        spread_h=as_low(np.ascontiguousarray(spread_matrix())),
        head_h=as_low(head_mask()),
        group_h=as_low(group_mask()),
        bias_h=jnp.asarray(block_bias()),
    )


def run_layer(fast, hbm, vmem):
    sd = jax.ShapeDtypeStruct
    const = constants()
    hbm = dict(hbm, **const)
    here, there = pl.BlockSpec(memory_space=pltpu.VMEM), pl.BlockSpec(memory_space=pl.ANY)
    slots = () if fast else SLOTS
    kind = f32 if fast else bf16
    outs = dict(
        out=sd((SHORT, D), bf16),
        g_tok=sd((SHORT, D), bf16),
        o_a=sd(slots + (16, WIDTH), kind),
        o_i=sd(slots + (16, 5 * D), kind),
        o_o=sd(slots + (64, D), kind),
        o_v=sd((16, SMALL if fast else D), f32),
    )
    row_length = hbm.pop("row_length")
    operands = dict(hbm, row_length=row_length, **vmem)
    flat = lambda parts: [one for part in parts.values() for one in (part if isinstance(part, list) else [part])]
    specs = [there] * len(flat(hbm)) + [pl.BlockSpec(memory_space=pltpu.SMEM)] + [here] * len(vmem)
    hbm_outs = len(outs) if fast else 2
    return pl.pallas_call(
        functools.partial(layer_kernel, fast, dict(operands, **outs)),
        out_shape=list(outs.values()),
        in_specs=specs,
        out_specs=[there] * hbm_outs + [here] * (len(outs) - hbm_outs),
        scratch_shapes=flat(scratch_list(fast)),
        compiler_params=pltpu.CompilerParams(
            collective_id=0, has_side_effects=True, vmem_limit_bytes=63 * 2**20
        ),
    )(*flat(operands))


def finish_outputs(*parts):
    sd = jax.ShapeDtypeStruct
    vmem, hbm = pl.BlockSpec(memory_space=pltpu.VMEM), pl.BlockSpec(memory_space=pl.ANY)
    own, square = sd((16,), f32), sd((16, D), f32)
    tokens = sd((SHORT, D), bf16)
    outs = [tokens, tokens, own, own, square, square, square, square, own, own, own]
    outs += [sd((16, 4 * D), f32), sd((HEAD,), f32), sd((HEAD, D), f32), own]
    return pl.pallas_call(
        final_kernel,
        out_shape=outs,
        in_specs=[hbm] * 6,
        out_specs=[hbm] * 2 + [vmem] * 13,
        scratch_shapes=[
            pltpu.VMEM((2, SHORT, D), bf16),
            pltpu.VMEM((16, WIDTH), f32),
            pltpu.VMEM((16, 5 * D), f32),
            pltpu.VMEM((HEAD, D), f32),
            pltpu.VMEM((16, SMALL), f32),
            pltpu.SemaphoreType.DMA((20,)),
        ],
    )(*parts)


def on_device(
    tokens, cotangent, row_length, first_gain, first_shift, query_weight, key_weight, value_weight,
    mixer_weight, mixer_bias, second_gain, second_shift, inner_weight, inner_bias, outer_weight, outer_bias,
):
    n_dp, n_fsdp = lax.axis_size("dp"), lax.axis_size("fsdp")
    fast = (n_dp, n_fsdp) == (8, 4) and query_weight.shape[0] == 16
    vectors = (first_gain, first_shift, mixer_bias, second_gain, second_shift, outer_bias)
    first = dict(tok_h=tokens, cot_h=cotangent, row_length=row_length)
    if fast:
        first.update(
            wq_s=query_weight, wk_s=key_weight, wv_s=value_weight, wm_s=mixer_weight, wi_s=inner_weight, wo_s=outer_weight,
            vectors=list(vectors) + [inner_bias],
        )
        return finish_outputs(*run_layer(True, first, dict()))
    whole = lambda part: lax.all_gather(part, AXES, axis=0, tiled=True)
    three = jnp.stack([part.reshape(-1, PAIRS, TILE) for part in (query_weight, key_weight, value_weight)], axis=2)
    wide = whole(three.reshape(-1, WIDTH))
    eights = [whole(vector).reshape(4, 8, 16) for vector in vectors]
    small = jnp.zeros((4, 8, 16, SMALL), bf16)
    for row, vector in enumerate(eights):
        for at in range(8):
            small = small.at[:, at, row, 16 * at : 16 * at + 16].set(vector[:, at])
    pairs = whole(inner_bias).reshape(4, 4, 2, 64)
    pairs_at = small.reshape(4, 4, 2, 16, SMALL)
    for at in range(2):
        pairs_at = pairs_at.at[:, :, at, 6, 64 * at : 64 * at + 64].set(pairs[:, :, at])
    wide = jnp.concatenate((pairs_at.reshape(4, 8, 16, SMALL), wide.reshape(4, 8, 16, WIDTH)), axis=-1)
    weights = dict(
        wa=wide.reshape(SLOTS + (16, WIDTH + SMALL)),
        wi=whole(jnp.concatenate((inner_weight, mixer_weight), axis=1)).reshape(SLOTS + (16, 5 * D)),
        wo=whole(outer_weight).reshape(SLOTS + (64, D)),
    )
    out, g_tok, d_a, d_i, d_o, o_v = run_layer(False, first, weights)
    owned = lambda part: lax.psum_scatter(part, AXES, scatter_dimension=0, tiled=True)
    g_a = owned(d_a.astype(f32).reshape(D, WIDTH))
    g_q, g_k, g_v = (g_a.reshape(-1, PAIRS, 3, TILE)[:, :, k].reshape(-1, D) for k in range(3))
    g_i = owned(d_i.astype(f32).reshape(D, 5 * D))
    g_i, g_m = g_i[:, : 4 * D], g_i[:, 4 * D :]
    g_o = owned(d_o.astype(f32).reshape(4 * D, D))
    six = [owned(o_v[k]) for k in (0, 1, 8, 9, 10, 11)]
    g_bias_in = owned(o_v[12:16].reshape(-1))
    return (
        out, g_tok, six[0], six[1], g_q, g_k, g_v, g_m, six[2], six[3], six[4], g_i, g_bias_in, g_o, six[5],
    )


def solution(mesh):
    rows, flat, both = P(AXES, None), P(AXES), P("dp")
    in_specs = (rows, rows, both, flat, flat, rows, rows, rows, rows, flat, flat, flat, rows, flat, rows, flat)
    out_specs = (rows, rows, flat, flat, rows, rows, rows, rows, flat, flat, flat, rows, flat, rows, flat)
    return jax.shard_map(on_device, mesh=mesh, in_specs=in_specs, out_specs=out_specs, check_vma=False)
```

```python
import functools
import math
import types

import jax
import jax.numpy as jnp
import numpy as np
from jax import lax
from jax.experimental import pallas as pl
from jax.experimental.pallas import tpu as pltpu
from jax.sharding import PartitionSpec as P

D = 512
HEADS = 8
HEAD = 64
BLOCK = 16
SHORT = 1024
LEVELS = 8
TILE = 128
TOGETHER = 5
CHUNK = 256
STACK = 2 * SHORT
WIDTH = 3 * D
SMALL = 128
GROUP = 3 * TILE
PAIRS = HEADS // 2
AXES = ("dp", "fsdp")
MESH = pl.DeviceIdType.MESH
SLOTS = (4, 2, 2, 2)

norm_eps = 1e-05
far_off = -1e30
f32 = jnp.float32
bf16 = jnp.bfloat16

FIRST = [STACK - (STACK >> level) for level in range(LEVELS + 1)]
LOW_TOP = 4


def member_matrix():
    token = np.arange(SHORT)
    rows = []
    for level, span in ((1, 256), (2, 512), (3, 1024)):
        rows.append((token[None] % span) >> level == np.arange(TILE)[:, None])
    for level in range(LOW_TOP, LEVELS):
        rows.append(token[None] >> level == np.arange(SHORT >> level)[:, None])
    rows.append(np.zeros((8, SHORT), bool))
    return np.concatenate(rows).astype(np.float32)


def spread_matrix():
    member = member_matrix()
    near = np.concatenate([member[0:128, :CHUNK], member[128:192, :CHUNK], member[256:288, :CHUNK], np.zeros((32, CHUNK))])
    return np.concatenate([np.tile(near, (1, SHORT // CHUNK)), member[384:]]).T.astype(np.float32)


def block_bias():
    key = np.arange(32)[:, None]
    query = np.arange(2 * TILE)[None]
    across = (key < BLOCK) != (query % 32 < BLOCK)
    last = np.where(query % TILE >= 96, ~across, across)
    kinds = [np.ones_like(across), across, last]
    return np.stack([np.where(kind, 0.0, far_off) for kind in kinds]).astype(np.float32)


def head_mask():
    lane = np.arange(TILE)[None]
    side = np.arange(2 * TILE)[:, None] // TILE
    return (lane // HEAD == side).astype(np.float32)


def group_mask():
    key = np.arange(TILE)[:, None]
    query = np.arange(2 * TILE)[None]
    return (key // 32 == query % TILE // 32).astype(np.float32)


def top_level_of():
    index = np.arange(TILE)
    return np.minimum(LOW_TOP + (index >= 64) * 1 + (index >= 96) * 1 + (index >= 112) * 1, 7)


def nn(a, b):
    return lax.dot_general(a, b, (((1,), (0,)), ((), ())), preferred_element_type=f32)


def nt(a, b):
    return lax.dot_general(a, b, (((1,), (1,)), ((), ())), preferred_element_type=f32)


def tn(a, b):
    return lax.dot_general(a, b, (((0,), (0,)), ((), ())), preferred_element_type=f32)


def normalize(values):
    center = values - jnp.mean(values, axis=-1, keepdims=True)
    inverse = lax.rsqrt(jnp.mean(center * center, axis=-1, keepdims=True) + norm_eps)
    return center * inverse, inverse


def normalize_back(grad_normed, normed, inverse):
    return inverse * (
        grad_normed
        - jnp.mean(grad_normed, axis=-1, keepdims=True)
        - normed * jnp.mean(grad_normed * normed, axis=-1, keepdims=True)
    )


def gelu_both(v):
    mag = jnp.abs(v) * (0.5**0.5)
    t = 1.0 / (1.0 + 0.3275911 * mag)
    gauss = jnp.exp(-0.5 * v * v)
    poly = t * (
        0.254829592
        + t * (-0.284496736 + t * (1.421413741 + t * (-1.453152027 + t * 1.061405429)))
    )
    tail = 0.5 * poly * gauss
    cdf = jnp.where(v < 0, tail, 1.0 - tail)
    return v * cdf, cdf + v * gauss * ((2 * math.pi) ** -0.5)


def split3(values):
    one = values.astype(bf16)
    rest = values - one.astype(f32)
    two = rest.astype(bf16)
    return one, two, (rest - two.astype(f32)).astype(bf16)


def split2(values):
    one = values.astype(bf16)
    return one, (values - one.astype(f32)).astype(bf16)


class Place:
    def __init__(self):
        self.dp = lax.axis_index("dp")
        self.fs = lax.axis_index("fsdp")
        self.z, self.y = self.dp // 2, self.dp % 2
        self.x, self.c = self.fs // 2, self.fs % 2
        self.oy, self.ox, self.oc = 1 - self.y, 1 - self.x, 1 - self.c
        self.zs = [lax.rem(self.z + step, 4) for step in (1, 2, 3)]
        self.by_core = (self.dp, self.x * 2 + self.oc)
        self.by_x = (self.dp, self.ox * 2 + self.c)
        self.by_y = (self.z * 2 + self.oy, self.fs)
        self.by_z = [(z * 2 + self.y, self.fs) for z in self.zs]
        ys, xs, cs = (self.y, self.oy), (self.x, self.ox), (self.c, self.oc)
        self.plane = [(self.z * 2 + ys[k // 4], xs[k // 2 % 2] * 2 + cs[k % 2]) for k in range(1, 8)]


def remote(src, dst, send, recv, device):
    return pltpu.make_async_remote_copy(
        src_ref=src, dst_ref=dst, send_sem=send, recv_sem=recv, device_id=device, device_id_type=MESH
    )


def arrived(ref, sem, device):
    remote(ref, ref, sem, sem, device).wait_recv()


def gone(ref, sem, device):
    remote(ref, ref, sem, sem, device).wait_send()


class Gather:
    def __init__(self, ref, lanes, p, sems):
        self.at = lambda z, y, x: ref.at[z, y, x, p.c, :, lanes]
        self.p, self.sems = p, sems

    def advance(self, step):
        p, at, sems = self.p, self.at, self.sems
        low, high, both, full = pl.ds(0, 2), pl.ds(2, 2), pl.ds(0, 2), pl.ds(0, 4)
        if step:
            ref = (at(pl.ds(0, 3), p.y, p.x), at(full, p.y, p.x), at(full, both, p.x), at(full, both, both))[step - 1]
            arrived(ref, sems.at[step - 1], p.by_core)
        if step == 4:
            gone(at(pl.ds(0, 3), p.y, p.x), sems.at[4], p.by_core)
            gone(at(pl.ds(0, 3), both, both), sems.at[5], p.by_core)
            gone(at(full, both, both), sems.at[6], p.by_core)
            return
        if step == 0:
            parts = [(at(p.z, p.y, p.x), device) for device in p.by_z]
        elif step == 1:
            parts = [(at(low, p.y, p.x), p.by_x), (at(high, p.y, p.x), p.by_y)]
        elif step == 2:
            parts = [(at(low, p.y, both), p.by_y), (at(high, both, p.x), p.by_x)]
        else:
            parts = [(at(full, both, both), p.by_core)]
        for part, device in parts:
            remote(part, part, sems.at[(4, 5, 5, 6)[step]], sems.at[step], device).start()


class Total:
    def __init__(self, ref, lanes, part, p, sems, bufs):
        self.ref, self.lanes, self.part, self.p, self.bufs = ref, lanes, part, p, bufs
        self.sems, self.sent = sems[0].at[part], sems[1]

    def add(self, index, buf):
        at = index + (self.p.c, slice(None), self.lanes)
        self.ref[at] = self.ref[at] + buf

    def advance(self, step):
        p, part, sems = self.p, self.part, self.sems
        from_core, one_a, one_b, two_a, two_b, far = self.bufs
        at = lambda z, y, x, c: self.ref.at[z, y, x, c, :, self.lanes]
        low, high, both, full, every = pl.ds(0, 2), pl.ds(2, 2), pl.ds(0, 2), pl.ds(0, 4), slice(None)
        if step:
            ref = (from_core.at[part], from_core.at[part, both], from_core.at[part, 0])[step - 1]
            arrived(ref, sems.at[step - 1], p.by_core)
        if step == 0:
            sends = [(at(full, both, both, p.oc), from_core, p.by_core)]
        elif step == 1:
            for z in range(4):
                self.add((z, every, every), from_core[part, z])
            sends = [(at(low, p.oy, both, p.c), one_a, p.by_y), (at(high, both, p.ox, p.c), one_b, p.by_x)]
        elif step == 2:
            for z in range(2):
                self.add((z, p.y, every), one_a[part, z])
                self.add((2 + z, every, p.x), one_b[part, z])
            sends = [(at(low, p.y, p.ox, p.c), two_a, p.by_x), (at(high, p.oy, p.x, p.c), two_b, p.by_y)]
        else:
            for z in range(2):
                self.add((z, p.y, p.x), two_a[part, z])
                self.add((2 + z, p.y, p.x), two_b[part, z])
            for k, z in enumerate(p.zs):
                remote(at(z, p.y, p.x, p.c), far.at[part, k], self.sent.at[2], sems.at[3], p.by_z[k]).start()
            return
        for src, buf, device in sends:
            remote(src, buf.at[part], self.sent.at[(0, 1, 1)[step]], sems.at[step], device).start()

    def finish(self, out):
        p, sems, far, part = self.p, self.sems, self.bufs[5], self.part
        arrived(far.at[part], sems.at[3], p.by_core)
        total = self.ref[p.z, p.y, p.x, p.c, :, self.lanes].astype(f32)
        out[:, self.lanes] = functools.reduce(jnp.add, [far[part, k].astype(f32) for k in range(3)], total)

    def settle(self):
        everything, far = self.bufs[0], self.bufs[5]
        gone(everything, self.sent.at[0], self.p.by_core)
        gone(everything.at[:, pl.ds(0, 3)], self.sent.at[1], self.p.by_core)
        gone(far, self.sent.at[2], self.p.by_core)


class TotalRows:
    def __init__(self, ref, part, p, sems, bufs):
        self.ref, self.part, self.p, self.bufs = ref, part, p, bufs
        self.sems, self.sent = sems[0].at[part], sems[1]

    def add(self, index, buf):
        at = (self.part,) + index
        self.ref[at] = self.ref[at] + buf

    def advance(self, step):
        p, part, sems = self.p, self.part, self.sems
        from_core, one_a, one_b, two_a, two_b, _ = self.bufs
        both, every, low, high = pl.ds(0, 2), slice(None), pl.ds(0, 32), pl.ds(32, 32)
        at = lambda y, x, c, *rows: self.ref.at[(part, y, x, c) + rows]
        if step:
            ref = (from_core.at[part], from_core.at[part, 0], from_core.at[part, 0, 0])[step - 1]
            arrived(ref, sems.at[step - 1], p.by_core)
        if step == 0:
            sends = [(at(both, both, p.oc), from_core, p.by_core)]
        elif step == 1:
            self.add((every, every, p.c), from_core[part])
            sends = [(at(p.oy, both, p.c, low), one_a, p.by_y), (at(both, p.ox, p.c, high), one_b, p.by_x)]
        elif step == 2:
            self.add((p.y, every, p.c, low), one_a[part])
            self.add((every, p.x, p.c, high), one_b[part])
            sends = [(at(p.y, p.ox, p.c, low), two_a, p.by_x), (at(p.oy, p.x, p.c, high), two_b, p.by_y)]
        else:
            self.add((p.y, p.x, p.c, low), two_a[part])
            self.add((p.y, p.x, p.c, high), two_b[part])
            return
        for src, buf, device in sends:
            remote(src, buf.at[part], self.sent.at[(0, 1, 1)[step]], sems.at[step], device).start()

    def settle(self):
        gone(self.bufs[0], self.sent.at[0], self.p.by_core)
        gone(self.bufs[0].at[pl.ds(0, 3)], self.sent.at[1], self.p.by_core)


class TotalVectors:
    def __init__(self, ref, p, sems, got, mid, far):
        self.ref, self.p, self.sems, self.got, self.mid, self.far = ref, p, sems, got, mid, far

    def begin(self):
        for k, device in enumerate(self.p.plane):
            remote(self.ref, self.got.at[k], self.sems.at[1], self.sems.at[0], device).start()

    def second(self):
        arrived(self.got, self.sems.at[0], self.p.by_core)
        self.mid[...] = functools.reduce(jnp.add, [self.got[k] for k in range(7)], self.ref[...])
        for k, device in enumerate(self.p.by_z):
            remote(self.mid, self.far.at[k], self.sems.at[3], self.sems.at[2], device).start()

    def finish(self):
        arrived(self.far, self.sems.at[2], self.p.by_core)
        gone(self.got, self.sems.at[1], self.p.by_core)
        gone(self.far, self.sems.at[3], self.p.by_core)
        return functools.reduce(jnp.add, [self.far[k] for k in range(3)], self.mid[...])


def layer_kernel(fast, kinds, *refs):
    shapes = dict(kinds, **scratch_list(fast))
    r, left = types.SimpleNamespace(), list(refs)
    for name, kind in shapes.items():
        amount = len(kind) if isinstance(kind, list) else 1
        taken, left = left[:amount], left[amount:]
        setattr(r, name, taken if isinstance(kind, list) else taken[0])
    assert not left
    p = Place()
    tok, cot = r.tok, r.cot
    member, spread = r.member, r.spread
    stack, probs, out_t, mix_t = r.stack, r.probs, r.out_t, r.mix_t
    lse_s, share, inner_s, total_h = r.lse_s, r.share, r.inner_s, r.total_h
    resid, n_one, n_two = r.resid, r.n_one, r.n_two
    acc_out, acc_two = r.acc_out, r.acc_two
    g_att, g_num = r.g_att, r.g_num
    g_mix, weight = g_num.at[0:SHORT], r.weight
    grads = r.grads
    vec_a, vec_b = r.vec_a, r.vec_b
    wa, wi, wo = r.wa, r.wi, r.wo
    da, di, do = (r.da, r.di, r.do) if fast else (r.o_a, r.o_i, r.o_o)

    def fetch(src, dst, slot):
        copy = pltpu.make_async_copy(src, dst, r.in_sem.at[slot])
        copy.start()
        return copy

    def taken(ref, slot):
        pltpu.make_async_copy(ref, ref, r.in_sem.at[slot]).wait()

    if fast:
        small_in = [fetch(ref, kept, k) for k, (ref, kept) in enumerate(zip(r.vectors, r.vec_in))]
        own_a, own_i, own_o = (ref.at[p.z, p.y, p.x, p.c] for ref in (wa, wi, wo))
        for pair in range(PAIRS):
            for slot, ref in enumerate((r.wq_s, r.wk_s, r.wv_s)):
                there = pl.ds(SMALL + pair * GROUP + slot * TILE, TILE)
                fetch(ref.at[:, pl.ds(pair * TILE, TILE)], own_a.at[:, there], 7)
        fetch(r.wi_s, own_i.at[:, pl.ds(0, 4 * D)], 8)
        fetch(r.wm_s, own_i.at[:, pl.ds(4 * D, D)], 8)
        fetch(r.wo_s, own_o, 9)
    tok_in = fetch(r.tok_h, tok, 10)
    rest_in = [
        fetch(src, dst, 11 + k)
        for k, (src, dst) in enumerate(
            ((r.member_h, member), (r.head_h, r.head_m), (r.group_h, r.group_m), (r.bias_h, r.bias), (r.cot_h, cot), (r.spread_h, spread))
        )
    ]

    other = p.fs // 2 * 2 + 1 - p.fs % 2
    pairs_at = (1 - p.fs // 2) * 2
    side = p.fs % 2
    barrier = pltpu.get_barrier_semaphore()
    reach = [(p.dp, other), (p.dp, pairs_at), (p.dp, pairs_at + 1)]
    if fast:
        reach += p.plane[3:] + p.by_z
    for device in reach:
        pl.semaphore_signal(barrier, inc=1, device_id=device, device_id_type=MESH)
    if fast:
        whose = p.dp * 4 + p.fs
        for copy in small_in:
            copy.wait()
        at = lax.broadcasted_iota(jnp.int32, (HEAD, SMALL), 0)
        lane = lax.broadcasted_iota(jnp.int32, (HEAD, SMALL), 1)
        rows = [ref[...].astype(f32).reshape(1, 16) for ref in r.vec_in[:6]]
        rows = jnp.concatenate(rows + [jnp.zeros((10, 16), f32)], axis=0).astype(bf16)
        spot = (lane[0:16] == at[0:16] + 16 * (whose % 8)).astype(f32).astype(bf16)
        own = nn(rows, spot)
        bias = jnp.concatenate([r.vec_in[6][...].astype(f32).reshape(1, HEAD), jnp.zeros((15, HEAD), f32)], axis=0)
        spot = (lane == at + HEAD * (whose % 2)).astype(f32).astype(bf16)
        own_bias = nn(bias.astype(bf16), spot)
        own = jnp.concatenate([own[0:6], own_bias[0:1], jnp.zeros((9, SMALL), f32)], axis=0)
        own_a[:, 0:SMALL] = own.astype(bf16)
    if fast:
        taken(own_a.at[:, pl.ds(SMALL, WIDTH)], 7)
    pl.semaphore_wait(barrier, len(reach))


    def first_norm(step, carry):
        at = pl.ds(pl.multiple_of(step * CHUNK, CHUNK), CHUNK)
        acc_two[at, :] = normalize(tok[at, :].astype(f32))[0]
        return carry

    if fast:
        spans = [(wa, 0, SMALL + GROUP), (wa, SMALL + GROUP, 3 * GROUP), (wi, 0, 1280), (wi, 1280, 1280), (wo, 0, D)]
        gathers = [
            Gather(ref, pl.ds(lo, wide), p, r.g_sem.at[k]) for k, (ref, lo, wide) in enumerate(spans)
        ]

    def pump(*events):
        if fast:
            for k, step in events:
                gathers[k].advance(step)

    pump((0, 0), (1, 0))
    if fast:
        taken(own_i, 8)
        taken(own_o, 9)
    tok_in.wait()
    lax.fori_loop(0, SHORT // CHUNK, first_norm, 0)
    pump((0, 1), (0, 2), (1, 1), (2, 0), (0, 3), (1, 2), (3, 0), (0, 4), (2, 1))
    for copy in rest_in:
        copy.wait()

    def rows_of(ref, lo, width):
        return ref[:, :, :, :, :, lo : lo + width].reshape(512, width)

    small = wa[:, :, :, :, :, 0:SMALL].astype(f32)
    by_z = jnp.sum(small, axis=(1, 2, 3))
    param = jnp.concatenate([by_z[z] for z in range(4)], axis=1)
    r.param[...] = param
    by_pair = jnp.sum(small, axis=3)
    r.bias_in[...] = jnp.concatenate(
        [by_pair[z, y, x, 6:7, :] for z in range(4) for y in range(2) for x in range(2)], axis=1
    )
    vec_a[...] = jnp.zeros_like(vec_a)
    vec_b[...] = jnp.zeros_like(vec_b)
    r.lanes_in[...] = jnp.zeros_like(r.lanes_in)

    gain_one, shift_one = r.param[0:1, :], r.param[1:2, :]

    def scale_shift(step, carry):
        at = pl.ds(pl.multiple_of(step * CHUNK, CHUNK), CHUNK)
        n_one[at, :] = (acc_two[at, :] * gain_one + shift_one).astype(bf16)
        return carry

    lax.fori_loop(0, SHORT // CHUNK, scale_shift, 0)

    index = lax.broadcasted_iota(jnp.int32, (TILE, 1), 0)
    steps_down = jnp.where(
        index < 64, 1 / 16, jnp.where(index < 96, 1 / 32, jnp.where(index < 112, 1 / 64, 1 / 128))
    ).astype(f32)

    def chunk_rows(step):
        one = pl.ds(pl.multiple_of(FIRST[1] + step * 128, 128), 128)
        two = pl.ds(pl.multiple_of(FIRST[2] + step * 64, 64), 64)
        return one, two, pl.ds(pl.multiple_of(FIRST[3] + step * 32, 32), 32)

    def chunk_members(chunk):
        near = [member[lo:hi, 0:CHUNK] for lo, hi in ((0, 128), (128, 192), (256, 288))]
        return near + [member[lo:hi, chunk] for lo, hi in ((384, 448), (448, 480), (480, 496), (496, 512))]

    lane_group = lax.broadcasted_iota(jnp.int32, (32, TILE), 1) // 32

    def squeeze(tall):
        parts = [tall[32 * part : 32 * part + 32, :] for part in range(4)]
        return jnp.where(
            lane_group < 2,
            jnp.where(lane_group == 0, parts[0], parts[1]),
            jnp.where(lane_group == 2, parts[2], parts[3]),
        )

    def widen(low):
        return jnp.concatenate([low, low, low, low], axis=0) * r.group_m[:, 0 : low.shape[1]]

    def by_head(both):
        half = both.shape[0] // 2
        lane = lax.broadcasted_iota(jnp.int32, (half, TILE), 1)
        return jnp.where(lane < HEAD, both[:half], both[half:])

    def two_heads(low):
        return jnp.concatenate([low, low], axis=0) * r.head_m[...]

    top_lane = lax.broadcasted_iota(jnp.int32, (HEADS, TILE), 1)
    top_scale_t = jnp.where(
        top_lane < 64, 1 / 16, jnp.where(top_lane < 96, 1 / 32, jnp.where(top_lane < 112, 1 / 64, 1 / 128))
    ).astype(f32)

    def tile_scale(tile):
        return jnp.where(
            tile < 8, 1.0, jnp.where(tile < 12, 0.5, jnp.where(tile < 14, 0.25, 0.125))
        ).astype(f32)

    def lanes_at(start, wide):
        return pl.ds(pl.multiple_of(start, TILE), wide)

    def tile_forward(tile, pair, kind, scale_t):
        rows = lanes_at(tile * TILE, TILE)
        at = lambda slot: (rows, lanes_at(pair * GROUP + slot * TILE, TILE))
        score = nt(two_heads(stack[at(1)]), stack[at(0)])
        score = jnp.concatenate([squeeze(score[:TILE]), squeeze(score[TILE:])], axis=1) + r.bias[kind]
        peak = jnp.max(score, axis=0, keepdims=True)
        prob = jnp.exp(score - peak)
        total = jnp.sum(prob, axis=0, keepdims=True)
        low = (prob * (1.0 / total)).astype(bf16)
        probs[tile, :, lanes_at(pair * 2 * TILE, 2 * TILE)] = low
        log_total = peak + jnp.log(total)
        lse_s[pair, 0:1, rows] = log_total[:, :TILE]
        lse_s[pair, 1:2, rows] = log_total[:, TILE:]
        made = nn(stack[at(2)].T, widen(low))
        head = pl.multiple_of(pair * TILE, TILE)
        out_t[pl.ds(head, HEAD), rows] = (made[:HEAD, :TILE] * scale_t).astype(bf16)
        out_t[pl.ds(head + HEAD, HEAD), rows] = (made[HEAD:, TILE:] * scale_t).astype(bf16)

    far_s, far_r = r.far_s, r.far_r
    far_out = [
        remote(far_s.at[0], far_r.at[0], r.far_sem.at[1], r.far_sem.at[0], (p.dp, other)),
        remote(far_s.at[1], far_r.at[1 + side], r.far_sem.at[1], r.far_sem.at[0], (p.dp, pairs_at)),
        remote(far_s.at[1], far_r.at[1 + side], r.far_sem.at[1], r.far_sem.at[0], (p.dp, pairs_at + 1)),
    ]
    tops_acc = acc_out

    def pair_forward(pair, carry):
        def pump_here(*plan):
            for number, events in enumerate(plan):
                if events:
                    pl.when(pair == number)(functools.partial(pump, *events))

        pump_here([], [(1, 4)])
        lanes = lanes_at(pair * GROUP, GROUP)
        made = nn(n_one[...], wa[:, :, :, :, :, lanes_at(SMALL + pair * GROUP, GROUP)].reshape(D, GROUP))
        first = lax.broadcasted_iota(jnp.int32, (1, GROUP), 1)
        stack[0:SHORT, lanes] = (made * jnp.where(first < TILE, 0.125, 1.0)).astype(bf16)
        key_like = first < 2 * TILE
        pump_here([(4, 0)])
        tops_acc[0:TILE, 0:GROUP] = jnp.zeros((TILE, GROUP), f32)

        def pool(step, carry):
            chunk = pl.ds(pl.multiple_of(step * CHUNK, CHUNK), CHUNK)
            made = nn(jnp.concatenate(chunk_members(chunk), axis=0), stack[chunk, lanes])
            to = chunk_rows(step)
            for level, (lo, hi) in enumerate(((0, 128), (128, 192), (192, 224))):
                scale = jnp.where(key_like, 0.5 ** (level + 1), 1.0)
                stack[to[level], lanes] = (made[lo:hi] * scale).astype(bf16)
            tops_acc[0:TILE, 0:GROUP] += made[224:352]
            return carry

        lax.fori_loop(0, SHORT // CHUNK, pool, 0)
        stack[FIRST[4] : STACK, lanes] = (
            tops_acc[0:TILE, 0:GROUP] * jnp.where(key_like, steps_down, 1.0)
        ).astype(bf16)
        theirs = lanes_at(pair * GROUP + TILE, 2 * TILE)
        mine = lanes_at(pair * 2 * TILE, 2 * TILE)
        far_s[0, :, mine] = stack[2016:2032, theirs]
        far_s[1, :, mine] = stack[2032:2048, theirs]

        @pl.when(pair == PAIRS - 1)
        def _():
            for copy in far_out:
                copy.start()

        def near_tiles(group, carry):
            for one in range(TOGETHER):
                tile = group * TOGETHER + one
                tile_forward(tile, pair, jnp.where(tile < 8, 0, 1), tile_scale(tile))
            for when, what, events in (
                (0, 1, [(1, 3), (2, 2)]),
                (0, 2, [(3, 1)]),
                (1, 2, [(2, 3), (3, 2), (4, 1)]),
                (2, 2, [(2, 4)]),
                (3, 0, [(3, 3), (4, 2)]),
            ):
                pl.when((pair == when) & (group == what))(functools.partial(pump, *events))
            return carry

        lax.fori_loop(0, 15 // TOGETHER, near_tiles, 0)
        return carry

    lax.fori_loop(0, PAIRS, pair_forward, 0)
    arrived(far_r, r.far_sem.at[0], p.by_core)
    gone(far_r, r.far_sem.at[1], p.by_core)
    last_rows = jnp.concatenate([far_r[1].astype(f32)[:8], far_r[2].astype(f32)[:8]], axis=0).astype(bf16)
    for pair in range(PAIRS):
        theirs = slice(pair * GROUP + TILE, (pair + 1) * GROUP)
        mine = slice(pair * 2 * TILE, (pair + 1) * 2 * TILE)
        stack[2016:2032, theirs] = far_r[0, :, mine]
        stack[2032:2048, theirs] = last_rows[:, mine]
    for pair in range(PAIRS):
        tile_forward(15, pair, 2, top_scale_t[0:1, :])
    idle = jnp.where(r.row_length[0] > SHORT, 0.0, far_off)
    lse_s[:, :, 1920:2048] = lse_s[:, :, 1920:2048] + jnp.where(top_lane[0:2] >= 96, idle, 0.0)

    edges = (0, 64, 96, 112, 128)

    def windows(step):
        one = pl.ds(pl.multiple_of(FIRST[1] + step * TILE, TILE), TILE)
        two = pl.ds(pl.multiple_of(FIRST[2] + step // 2 * TILE, TILE), TILE)
        return one, two, pl.ds(FIRST[3], TILE), pl.ds(FIRST[4], TILE)

    def per_level(step, chunk):
        one = member[0:512, chunk]

        def for_head(head):
            rows = []
            spans = [(0, 128), (128, 256), (256, 384), (384, 448), (448, 480), (480, 496), (496, 512)]
            for level, (lo, hi) in enumerate(spans, 1):
                rows.append(one[lo:hi] * share[level, head : head + 1, chunk].astype(bf16))
            return jnp.concatenate(rows, axis=0)

        return for_head

    def lse_of(lanes):
        return jnp.concatenate([lse_s[pair, :, lanes] for pair in range(PAIRS)], axis=0)

    def combine(step, carry):
        chunk = pl.ds(pl.multiple_of(step * CHUNK, CHUNK), CHUNK)
        wins = windows(step)
        logs = [lse_of(chunk)]
        for slot in range(3):
            parts = jnp.concatenate(split3(lse_of(wins[slot])), axis=0)
            made = nn(parts, member[slot * TILE : (slot + 1) * TILE, chunk])
            logs.append(made[0:8] + made[8:16] + made[16:24] + (slot + 1) * math.log(2.0))
        top = lse_of(wins[3])
        parts = []
        for slot in range(4):
            inside = (top_lane >= edges[slot]) & (top_lane < edges[slot + 1])
            parts += list(split3(jnp.where(inside, top, 0.0)))
        made = nn(jnp.concatenate(parts, axis=0), member[384:512, chunk])
        for slot in range(4):
            b = slot * 24
            logs.append(made[b : b + 8] + made[b + 8 : b + 16] + made[b + 16 : b + 24] + (slot + 4) * math.log(2.0))
        peak = functools.reduce(jnp.maximum, logs)
        den = functools.reduce(jnp.add, [jnp.exp(one - peak) for one in logs])
        lse = peak + jnp.log(den)
        for level in range(LEVELS):
            share[level, :, chunk] = jnp.exp(logs[level] - lse)
        for_head = per_level(step, chunk)
        for head in range(HEADS):
            at = slice(head * HEAD, (head + 1) * HEAD)
            coarse = jnp.concatenate([out_t[at, win] for win in wins], axis=1)
            made = nn(coarse, for_head(head))
            made = made + share[0, head : head + 1, chunk] * out_t[at, chunk].astype(f32)
            mix_t[at, chunk] = made.astype(bf16)
        return carry

    lax.fori_loop(0, SHORT // CHUNK, combine, 0)
    pump((3, 4), (4, 3))

    bias_mix, gain_two = r.param[2:3, :], r.param[3:4, :]
    shift_two, bias_out = r.param[4:5, :], r.param[5:6, :]
    w_mix = rows_of(wi, 4 * D, D)
    halves = [slice(half * 512, (half + 1) * 512) for half in range(2)]
    for at in halves:
        mid = tok[at, :].astype(f32) + tn(mix_t[:, at], w_mix) + bias_mix
        resid[at, :] = mid
        acc_out[at, :] = mid + bias_out
        normed, _ = normalize(mid)
        n_two[at, :] = (normed * gain_two + shift_two).astype(bf16)
    pump((4, 4))

    rows = (pl.ds(0, SHORT), pl.ds(SHORT, SHORT))
    hid, g_pre = ([grads.at[at, pl.ds(lane, D)] for at in rows] for lane in (0, D))

    def total_i(part):
        return Total(di, lanes_at(part * 512, 512), part, p, r.si[0:2], r.si[2:])

    def total_o(part):
        return TotalRows(do, part, p, r.so[0:2], r.so[2:8])

    def onward(total, *steps):
        if fast:
            for part, step in steps:
                if isinstance(part, int):
                    total(part).advance(step)
                else:
                    pl.when(part >= 0)(lambda: total(part).advance(step))

    def feed_grads(part):
        lanes = pl.ds(part * 512, 512)
        di[:, :, :, :, :, lanes] = tn(n_two[...], g_pre[part % 2][...]).astype(bf16).reshape(4, 2, 2, 2, 16, 512)
        do[part] = tn(hid[part % 2][...], cot[...]).astype(bf16).reshape(2, 2, 2, 64, 512)
        onward(total_i, (part, 0))
        onward(total_o, (part, 0))

    for part in range(4):
        lanes = pl.ds(part * 512, 512)
        w_in = wi[:, :, :, :, :, lanes].reshape(512, 512)
        w_out = wo[part].reshape(512, 512)
        pre = nn(n_two[...], w_in) + r.bias_in[:, lanes]
        back = nt(cot[...], w_out)
        if part:
            feed_grads(part - 1)
        act, slope = gelu_both(pre)
        act = act.astype(bf16)
        back = (back * slope).astype(bf16)
        hid[part % 2][...] = act
        g_pre[part % 2][...] = back
        r.lanes_in[0:1, lanes] = jnp.sum(back.astype(f32), axis=0, keepdims=True)
        acc_out[...] += nn(act, w_out)
        shares = nt(back, w_in)
        acc_two[...] = acc_two[...] + shares if part else shares
        for total in (total_i, total_o):
            onward(total, *[(part - k, k) for k in (3, 2, 1) if part >= k])
    feed_grads(3)

    for at in halves:
        n_two[at, :] = acc_out[at, :].astype(bf16)
        normed, inverse = normalize(resid[at, :])
        g_two = acc_two[at, :]
        c = cot[at, :].astype(f32)
        g_mid = c + normalize_back(g_two * gain_two, normed, inverse)
        resid[at, :] = g_mid
        low = g_mid.astype(bf16)
        g_att[at, :] = low
        for row, values in enumerate((low.astype(f32), g_two * normed, g_two, c)):
            vec_b[row : row + 1, :] += jnp.sum(values, axis=0, keepdims=True)
        g_mix[at, :] = nt(low, w_mix).astype(bf16)
        turned = nt(w_mix, low).astype(bf16).astype(f32) * mix_t[:, at].astype(f32)
        inner_s[:, at] = jnp.concatenate(
            [jnp.sum(turned[h * HEAD : (h + 1) * HEAD], axis=0, keepdims=True) for h in range(HEADS)], axis=0
        )
    out_copy = pltpu.make_async_copy(n_two, r.out, r.out_sem.at[0])
    out_copy.start()
    onward(total_i, (1, 3), (2, 2), (3, 1))
    made = nn(mix_t[...], g_att[...])
    di[:, :, :, :, :, 4 * D :] = made.astype(bf16).reshape(4, 2, 2, 2, 16, D)
    onward(total_i, (4, 0))
    onward(total_o, (1, 3), (2, 2), (3, 1))


    def keep_h(lanes, values):
        for pair in range(PAIRS):
            total_h[pair, :, lanes] = values[2 * pair : 2 * pair + 2]

    def sums_of(level, source, members):
        both = jnp.concatenate(split2(share[level, :, source] * inner_s[:, source]), axis=0)
        made = nt(both, members)
        return made[0:8] + made[8:16]

    tops_acc[0:TILE, :] = jnp.zeros((TILE, D), f32)

    def lift(step, carry):
        chunk = pl.ds(pl.multiple_of(step * CHUNK, CHUNK), CHUNK)
        to = chunk_rows(step)
        members = chunk_members(chunk)
        made = []
        for pair in range(PAIRS):
            weighted = [
                one * share[1 + k, head : head + 1, chunk].astype(bf16)
                for head in (2 * pair, 2 * pair + 1)
                for k, one in enumerate(members)
            ]
            tokens = g_num[chunk, pair * TILE : (pair + 1) * TILE]
            made.append(by_head(nn(jnp.concatenate(weighted, axis=0), tokens)))
        made = jnp.concatenate(made, axis=1)
        for level, (low, high) in enumerate(((0, 128), (128, 192), (192, 224))):
            g_num[to[level], :] = (made[low:high] * 0.5 ** (level + 1)).astype(bf16)
        tops_acc[0:TILE, :] += made[224:352]
        keep_h(chunk, share[0, :, chunk] * inner_s[:, chunk])
        keep_h(to[0], sums_of(1, chunk, member[0:128, chunk]))
        return carry

    lax.fori_loop(0, SHORT // CHUNK, lift, 0)
    g_num[FIRST[4] : STACK, :] = (tops_acc[0:TILE, :] * steps_down).astype(bf16)

    def lift_two(step, carry):
        source = pl.ds(pl.multiple_of(step * 512, 512), 512)
        rows = pl.ds(pl.multiple_of(FIRST[2] + step * TILE, TILE), TILE)
        keep_h(rows, sums_of(2, source, member[128:256, source]))
        return carry

    lax.fori_loop(0, 2, lift_two, 0)
    onward(total_i, (2, 3))
    onward(total_o, (2, 3))
    every = pl.ds(0, SHORT)
    keep_h(pl.ds(FIRST[3], TILE), sums_of(3, every, member[256:384, :]))
    tops = [sums_of(4 + slot, every, member[384:512, :]) for slot in range(4)]
    keep_h(
        pl.ds(FIRST[4], TILE),
        jnp.where(top_lane < 64, tops[0], jnp.where(top_lane < 96, tops[1], jnp.where(top_lane < 112, tops[2], tops[3]))),
    )
    for pair in range(PAIRS):
        weight[pair, :, 0:SHORT] = share[0, 2 * pair : 2 * pair + 2]
    weight[:, :, SHORT:STACK] = jnp.ones((PAIRS, 2, SHORT), f32)

    def tile_backward(tile, pair, scale):
        rows = lanes_at(tile * TILE, TILE)
        at = lambda slot: (rows, lanes_at(pair * GROUP + slot * TILE, TILE))
        num = g_num[rows, lanes_at(pair * TILE, TILE)]
        got = nt(two_heads(stack[at(2)]), num)
        got = jnp.concatenate([squeeze(got[:TILE]), squeeze(got[TILE:])], axis=1)
        both = lambda ref: jnp.concatenate([ref[pair, 0:1, rows], ref[pair, 1:2, rows]], axis=1)
        low = probs[tile, :, lanes_at(pair * 2 * TILE, 2 * TILE)].astype(f32)
        times = both(weight)
        wide_s = widen((low * (got * times - both(total_h))).astype(bf16))
        wide_p = widen((low * times).astype(bf16))
        tall = lambda wide: jnp.concatenate([wide[:, :TILE], wide[:, TILE:]], axis=0)
        grads[at(1)] = (by_head(nn(tall(wide_s), stack[at(0)])) * scale).astype(bf16)
        grads[at(2)] = by_head(nn(tall(wide_p), num)).astype(bf16)
        made = nn(stack[at(1)].T, wide_s)
        made = jnp.concatenate([made[:HEAD, :TILE], made[HEAD:, TILE:]], axis=0).astype(bf16).T
        grads[at(0)] = (made.astype(f32) * (scale * 0.125)).astype(bf16)

    for pair in range(PAIRS):
        tile_backward(15, pair, steps_down)
    back_s, back_r = r.back_s, r.back_r
    spans = [(slice(k * GROUP + TILE, (k + 1) * GROUP), slice(k * 2 * TILE, (k + 1) * 2 * TILE)) for k in range(PAIRS)]
    tall = jnp.concatenate([grads[2016:2048, theirs] for theirs, _ in spans], axis=1).astype(f32)
    nothing = jnp.zeros((8, 2 * D), f32)
    back_s[0] = tall[0:16].astype(bf16)
    back_s[1] = jnp.concatenate([tall[16:24], nothing], axis=0).astype(bf16)
    back_s[2] = jnp.concatenate([tall[24:32], nothing], axis=0).astype(bf16)
    back_out = [
        remote(back_s.at[0], back_r.at[0], r.far_sem.at[3], r.far_sem.at[2], (p.dp, other)),
        remote(back_s.at[1], back_r.at[1 + side], r.far_sem.at[3], r.far_sem.at[2], (p.dp, pairs_at)),
        remote(back_s.at[2], back_r.at[1 + side], r.far_sem.at[3], r.far_sem.at[2], (p.dp, pairs_at + 1)),
    ]
    for copy in back_out:
        copy.start()
    onward(total_i, (3, 2), (4, 1))
    onward(total_o, (3, 2))

    def total_a(part):
        return Total(da, lanes_at(part * GROUP, GROUP), part, p, r.sa[0:2], r.sa[2:])

    def far_grads():
        arrived(back_r, r.far_sem.at[2], p.by_core)
        gone(back_r, r.far_sem.at[3], p.by_core)
        two = (back_r[1].astype(f32) + back_r[2].astype(f32)).astype(bf16)
        for theirs, mine in spans:
            grads[2016:2032, theirs] = back_r[0, :, mine]
            grads[2032:2048, theirs] = two[:, mine]

    def send_rows():
        onward(total_o, (3, 3))
        for k, z in enumerate(p.zs):
            remote(do.at[z, p.y, p.x, p.c], r.so[7].at[k], r.so[8].at[1], r.so[8].at[0], p.by_z[k]).start()

    def finish_feed():
        for part in range(5):
            total_i(part).finish(r.keep_i)
        arrived(r.so[7], r.so[8].at[0], p.by_core)
        total = do[p.z, p.y, p.x, p.c].astype(f32)
        r.keep_o[...] = functools.reduce(jnp.add, [r.so[7][k].astype(f32) for k in range(3)], total)
        gone(r.so[7], r.so[8].at[1], p.by_core)
        total_o(0).settle()
        total_i(0).settle()
        for copy in kept[:2]:
            copy.start()

    if fast:
        kept = [
            pltpu.make_async_copy(src, dst, r.keep_sem.at[k])
            for k, (src, dst) in enumerate(
                ((r.keep_i, r.o_i), (r.keep_o, r.o_o), (r.keep_a, r.o_a), (r.keep_v, r.o_v))
            )
        ]

        early = TotalVectors(r.vec_b, p, r.v_sem.at[0], r.got_b, r.mid_b, r.far_b)
        late = TotalVectors(r.vec_s, p, r.v_sem.at[1], r.got_a, r.mid_a, r.far_a)
    vec_b[4:8, :] = jnp.concatenate([r.lanes_in[0:1, k * 512 : (k + 1) * 512] for k in range(4)], axis=0)

    def early_done():
        r.done_b[...] = early.finish()
        long = jnp.concatenate([r.done_b[4 + k : 5 + k] for k in range(4)], axis=1)
        long = pltpu.roll(jnp.concatenate([long] * 8, axis=0), 2048 - HEAD * whose, axis=1)[:, 0:SMALL]
        r.keep_v[8:16] = long

    def pair_backward(pair, carry):
        def near_back(group, carry):
            for one in range(TOGETHER):
                tile = group * TOGETHER + one
                tile_backward(tile, pair, tile_scale(tile))
            return carry

        lax.fori_loop(0, 15 // TOGETHER, near_back, 0)
        pl.when(pair == 0)(far_grads)
        if fast:
            pl.when(pair == 0)(lambda: onward(total_i, (3, 3), (4, 2)))
            pl.when(pair == 0)(send_rows)
            pl.when(pair == 1)(lambda: onward(total_i, (4, 3)))
            pl.when(pair == 0)(early.begin)
            pl.when(pair == 1)(early.second)
            pl.when(pair == 3)(finish_feed)
            pl.when(pair == 3)(early_done)
        onward(total_a, (pair - 3, 3), (pair - 2, 2), (pair - 1, 1))

        lanes = lanes_at(pair * GROUP, GROUP)

        def level_sums(step, carry):
            chunk = pl.ds(pl.multiple_of(step * CHUNK, CHUNK), CHUNK)
            top = grads[FIRST[4] : STACK, lanes]
            coarse = [grads[rows, lanes] for rows in chunk_rows(step)] + [top[0:32], top]
            made = nn(spread[chunk, :], jnp.concatenate(coarse, axis=0))
            stack[chunk, lanes] = (made + grads[chunk, lanes].astype(f32)).astype(bf16)
            return carry

        lax.fori_loop(0, SHORT // CHUNK, level_sums, 0)
        da[:, :, :, :, :, lanes] = tn(n_one[...], stack[0:SHORT, lanes]).astype(bf16).reshape(4, 2, 2, 2, 16, GROUP)
        onward(total_a, (pair, 0))
        return carry

    lax.fori_loop(0, PAIRS, pair_backward, 0)

    w_qkv = lambda: wa[:, :, :, :, :, SMALL : SMALL + WIDTH].reshape(D, WIDTH)

    def first_back(at, g_one):
        normed, inverse = normalize(tok[at, :].astype(f32))
        vec_a[0:1, :] += jnp.sum(g_one * normed, axis=0, keepdims=True)
        vec_a[1:2, :] += jnp.sum(g_one, axis=0, keepdims=True)
        g_att[at, :] = (resid[at, :] + normalize_back(g_one * gain_one, normed, inverse)).astype(bf16)

    acc_two[halves[0], :] = nt(stack[halves[0], :], w_qkv())
    acc_two[halves[1], :] = nt(stack[halves[1], :], w_qkv())
    first_back(halves[0], acc_two[halves[0], :])
    onward(total_a, (3, 1), (2, 2))
    first_back(halves[1], acc_two[halves[1], :])
    tok_copy = pltpu.make_async_copy(g_att, r.g_tok, r.out_sem.at[1])
    tok_copy.start()
    if fast:
        for row in range(2):
            for part in range(4):
                at = row * 4 + part
                r.vec_s[at : at + 1, :] = vec_a[row : row + 1, part * TILE : (part + 1) * TILE]
        late.begin()
        onward(total_a, (1, 3), (3, 2), (2, 3))
        late.second()
        onward(total_a, (3, 3))
        for part in range(3):
            total_a(part).finish(r.keep_a)
        last = late.finish()
        rows = [jnp.concatenate([last[at + part : at + part + 1] for part in range(4)], axis=1) for at in (0, 4)]
        short = jnp.concatenate(rows + [r.done_b[0:4], jnp.zeros((2, D), f32)], axis=0)
        short = pltpu.roll(short, 512 - 16 * whose, axis=1)[:, 0:SMALL]
        r.keep_v[0:8] = short
        kept[3].start()
        total_a(3).finish(r.keep_a)
        total_a(0).settle()
        kept[2].start()
        for copy in kept:
            copy.wait()
    else:
        r.o_v[0:8] = vec_a[...]
        r.o_v[8:16] = vec_b[...]
    out_copy.wait()
    tok_copy.wait()


def final_kernel(*refs):
    big, small, outs, (kept, vmem_a, vmem_i, vmem_o, vmem_v, sem) = refs[:2], refs[2:6], refs[6:21], refs[21:]
    parts = [pl.ds(k * CHUNK, CHUNK) for k in range(SHORT // CHUNK)]
    count = iter(range(24))
    copy = lambda src, dst: pltpu.make_async_copy(src, dst, sem.at[next(count)])
    into = [copy(ref.at[at], kept.at[slot, at]) for slot, ref in enumerate(big) for at in parts]
    onto = [copy(kept.at[slot, at], outs[slot].at[at]) for slot in range(2) for at in parts]
    rest = [copy(src, dst) for src, dst in zip(small, (vmem_a, vmem_i, vmem_o, vmem_v))]
    for one in into + rest:
        one.start()
    for one, then in zip(into, onto):
        one.wait()
        then.start()
    for one in rest:
        one.wait()
    for slot, at in ((2, 0), (3, 1), (8, 2), (9, 3), (10, 4), (14, 5)):
        outs[slot][...] = vmem_v[at : at + 1, 0:16].reshape(16)
    outs[12][...] = vmem_v[8:9, 0:HEAD].reshape(HEAD)
    for k in range(3):
        for pair in range(PAIRS):
            at = pair * GROUP + k * TILE
            outs[4 + k][:, pair * TILE : (pair + 1) * TILE] = vmem_a[:, at : at + TILE]
    outs[7][...] = vmem_i[:, 4 * D :]
    outs[11][...] = vmem_i[:, : 4 * D]
    outs[13][...] = vmem_o[...]
    for one in onto:
        one.wait()


def scratch_list(fast):
    V, S = pltpu.VMEM, pltpu.SemaphoreType.DMA
    made = dict(
        tok=V((SHORT, D), bf16),
        cot=V((SHORT, D), bf16),
        member=V((D, SHORT), bf16),
        spread=V((SHORT, GROUP), bf16),
        head_m=V((2 * TILE, TILE), bf16),
        group_m=V((TILE, 2 * TILE), bf16),
        bias=V((3, 32, 2 * TILE), f32),
        in_sem=S((17,)),
        out_sem=S((2,)),
        stack=V((STACK, WIDTH), bf16),
        probs=V((16, 32, HEADS * TILE), bf16),
        out_t=V((D, STACK), bf16),
        mix_t=V((D, SHORT), bf16),
        lse_s=V((PAIRS, 2, STACK), f32),
        share=V((LEVELS, HEADS, SHORT), f32),
        inner_s=V((HEADS, SHORT), f32),
        total_h=V((PAIRS, 2, STACK), f32),
        resid=V((SHORT, D), f32),
        n_one=V((SHORT, D), bf16),
        n_two=V((SHORT, D), bf16),
        acc_out=V((SHORT, D), f32),
        acc_two=V((SHORT, D), f32),
        grads=V((STACK, WIDTH), bf16),
        g_att=V((SHORT, D), bf16),
        weight=V((PAIRS, 2, STACK), f32),
        g_num=V((STACK, D), bf16),
        vec_a=V((8, D), f32),
        vec_b=V((8, D), f32),
        param=V((16, D), f32),
        bias_in=V((1, 4 * D), f32),
        lanes_in=V((8, 4 * D), f32),
        far_s=V((2, 16, 2 * D), bf16),
        far_r=V((3, 16, 2 * D), bf16),
        far_sem=S((4,)),
        back_s=V((3, 16, 2 * D), bf16),
        back_r=V((3, 16, 2 * D), bf16),
    )
    if fast:

        def sums(parts, wide):
            shape = lambda *dims: V((parts,) + dims + (16, wide), bf16)
            return [S((parts, 4)), S((3,)), shape(4, 2, 2), shape(2, 2), shape(2, 2), shape(2), shape(2), shape(3)]

        rows = lambda *dims: V((4,) + dims + (D,), bf16)
        made.update(
            wa=V(SLOTS + (16, WIDTH + SMALL), bf16),
            wi=V(SLOTS + (16, 5 * D), bf16),
            wo=V(SLOTS + (64, D), bf16),
            da=V(SLOTS + (16, WIDTH), bf16),
            di=V(SLOTS + (16, 5 * D), bf16),
            do=V(SLOTS + (64, D), bf16),
            g_sem=S((5, 7)),
            si=sums(5, D),
            so=[S((4, 3)), S((2,)), rows(2, 2, 64), rows(2, 32), rows(2, 32), rows(32), rows(32), V((3, 64, D), bf16), S((2,))],
            sa=sums(4, GROUP),
            v_sem=S((2, 4)),
            vec_s=V((8, TILE), f32),
            got_a=V((7, 8, TILE), f32),
            mid_a=V((8, TILE), f32),
            far_a=V((3, 8, TILE), f32),
            got_b=V((7, 8, D), f32),
            mid_b=V((8, D), f32),
            far_b=V((3, 8, D), f32),
            done_b=V((8, D), f32),
            vec_in=[V((16,), bf16)] * 6 + [V((HEAD,), bf16)],
            keep_a=V((16, WIDTH), f32),
            keep_i=V((16, 5 * D), f32),
            keep_o=V((HEAD, D), f32),
            keep_v=V((16, SMALL), f32),
            keep_sem=S((4,)),
        )
    return made


def constants():
    member = member_matrix()
    as_low = lambda values: jnp.asarray(values.astype(np.float32), bf16)
    return dict(
        member_h=as_low(member),
        spread_h=as_low(np.ascontiguousarray(spread_matrix())),
        head_h=as_low(head_mask()),
        group_h=as_low(group_mask()),
        bias_h=jnp.asarray(block_bias()),
    )


def run_layer(fast, hbm, vmem):
    sd = jax.ShapeDtypeStruct
    const = constants()
    hbm = dict(hbm, **const)
    here, there = pl.BlockSpec(memory_space=pltpu.VMEM), pl.BlockSpec(memory_space=pl.ANY)
    slots = () if fast else SLOTS
    kind = f32 if fast else bf16
    outs = dict(
        out=sd((SHORT, D), bf16),
        g_tok=sd((SHORT, D), bf16),
        o_a=sd(slots + (16, WIDTH), kind),
        o_i=sd(slots + (16, 5 * D), kind),
        o_o=sd(slots + (64, D), kind),
        o_v=sd((16, SMALL if fast else D), f32),
    )
    row_length = hbm.pop("row_length")
    operands = dict(hbm, row_length=row_length, **vmem)
    flat = lambda parts: [one for part in parts.values() for one in (part if isinstance(part, list) else [part])]
    specs = [there] * len(flat(hbm)) + [pl.BlockSpec(memory_space=pltpu.SMEM)] + [here] * len(vmem)
    hbm_outs = len(outs) if fast else 2
    return pl.pallas_call(
        functools.partial(layer_kernel, fast, dict(operands, **outs)),
        out_shape=list(outs.values()),
        in_specs=specs,
        out_specs=[there] * hbm_outs + [here] * (len(outs) - hbm_outs),
        scratch_shapes=flat(scratch_list(fast)),
        compiler_params=pltpu.CompilerParams(
            collective_id=0, has_side_effects=True, vmem_limit_bytes=63 * 2**20
        ),
    )(*flat(operands))


def finish_outputs(*parts):
    sd = jax.ShapeDtypeStruct
    vmem, hbm = pl.BlockSpec(memory_space=pltpu.VMEM), pl.BlockSpec(memory_space=pl.ANY)
    own, square = sd((16,), f32), sd((16, D), f32)
    tokens = sd((SHORT, D), bf16)
    outs = [tokens, tokens, own, own, square, square, square, square, own, own, own]
    outs += [sd((16, 4 * D), f32), sd((HEAD,), f32), sd((HEAD, D), f32), own]
    return pl.pallas_call(
        final_kernel,
        out_shape=outs,
        in_specs=[hbm] * 6,
        out_specs=[hbm] * 2 + [vmem] * 13,
        scratch_shapes=[
            pltpu.VMEM((2, SHORT, D), bf16),
            pltpu.VMEM((16, WIDTH), f32),
            pltpu.VMEM((16, 5 * D), f32),
            pltpu.VMEM((HEAD, D), f32),
            pltpu.VMEM((16, SMALL), f32),
            pltpu.SemaphoreType.DMA((20,)),
        ],
    )(*parts)


def on_device(
    tokens, cotangent, row_length, first_gain, first_shift, query_weight, key_weight, value_weight,
    mixer_weight, mixer_bias, second_gain, second_shift, inner_weight, inner_bias, outer_weight, outer_bias,
):
    n_dp, n_fsdp = lax.axis_size("dp"), lax.axis_size("fsdp")
    fast = (n_dp, n_fsdp) == (8, 4) and query_weight.shape[0] == 16
    vectors = (first_gain, first_shift, mixer_bias, second_gain, second_shift, outer_bias)
    first = dict(tok_h=tokens, cot_h=cotangent, row_length=row_length)
    if fast:
        first.update(
            wq_s=query_weight, wk_s=key_weight, wv_s=value_weight, wm_s=mixer_weight, wi_s=inner_weight, wo_s=outer_weight,
            vectors=list(vectors) + [inner_bias],
        )
        return finish_outputs(*run_layer(True, first, dict()))
    whole = lambda part: lax.all_gather(part, AXES, axis=0, tiled=True)
    three = jnp.stack([part.reshape(-1, PAIRS, TILE) for part in (query_weight, key_weight, value_weight)], axis=2)
    wide = whole(three.reshape(-1, WIDTH))
    eights = [whole(vector).reshape(4, 8, 16) for vector in vectors]
    small = jnp.zeros((4, 8, 16, SMALL), bf16)
    for row, vector in enumerate(eights):
        for at in range(8):
            small = small.at[:, at, row, 16 * at : 16 * at + 16].set(vector[:, at])
    pairs = whole(inner_bias).reshape(4, 4, 2, 64)
    pairs_at = small.reshape(4, 4, 2, 16, SMALL)
    for at in range(2):
        pairs_at = pairs_at.at[:, :, at, 6, 64 * at : 64 * at + 64].set(pairs[:, :, at])
    wide = jnp.concatenate((pairs_at.reshape(4, 8, 16, SMALL), wide.reshape(4, 8, 16, WIDTH)), axis=-1)
    weights = dict(
        wa=wide.reshape(SLOTS + (16, WIDTH + SMALL)),
        wi=whole(jnp.concatenate((inner_weight, mixer_weight), axis=1)).reshape(SLOTS + (16, 5 * D)),
        wo=whole(outer_weight).reshape(SLOTS + (64, D)),
    )
    out, g_tok, d_a, d_i, d_o, o_v = run_layer(False, first, weights)
    owned = lambda part: lax.psum_scatter(part, AXES, scatter_dimension=0, tiled=True)
    g_a = owned(d_a.astype(f32).reshape(D, WIDTH))
    g_q, g_k, g_v = (g_a.reshape(-1, PAIRS, 3, TILE)[:, :, k].reshape(-1, D) for k in range(3))
    g_i = owned(d_i.astype(f32).reshape(D, 5 * D))
    g_i, g_m = g_i[:, : 4 * D], g_i[:, 4 * D :]
    g_o = owned(d_o.astype(f32).reshape(4 * D, D))
    six = [owned(o_v[k]) for k in (0, 1, 8, 9, 10, 11)]
    g_bias_in = owned(o_v[12:16].reshape(-1))
    return (
        out, g_tok, six[0], six[1], g_q, g_k, g_v, g_m, six[2], six[3], six[4], g_i, g_bias_in, g_o, six[5],
    )


def solution(mesh):
    rows, flat, both = P(AXES, None), P(AXES), P("dp")
    in_specs = (rows, rows, both, flat, flat, rows, rows, rows, rows, flat, flat, flat, rows, flat, rows, flat)
    out_specs = (rows, rows, flat, flat, rows, rows, rows, rows, flat, flat, flat, rows, flat, rows, flat)
    return jax.shard_map(on_device, mesh=mesh, in_specs=in_specs, out_specs=out_specs, check_vma=False)
```
